32 devices in a mesh: dp: 8 (over z, y), head: 4 (over x, core).
Axes of the slice: x: 2, y: 2, z: 4, core: 2. Of those that a mesh axis runs over, the one named last changes fastest.
Arguments:
- pixels: bfloat16 [4, 8, 512, 261], P(None, 'dp', 'head'), may hold values from -6 to 6
- masks: int32 [4, 8, 512], P(None, 'dp'), may hold values from 0 to 1, as said below
- valid: int32 [4, 8], P(None, 'dp'), may hold values 0 or 1
- labels: int32 [4, 8], P(None, 'dp'), may hold values from 0 to 999
- square: float32 [10, 1024, 1024], P(None, ('dp', 'head')), may hold values from -0.1875 to 0.1875
- kv_weight: float32 [261, 2048], P(None, ('dp', 'head')), may hold values from -0.375 to 0.375
- head_weight: float32 [1024, 1000], P(('dp', 'head')), may hold values from -0.375 to 0.375
- latents: float32 [512, 1024], P(None, ('dp', 'head')), may hold values from -6 to 6
- small: float32 [6381], replicated, may hold values from 0.25 to 1.75
- square_mom: float32 [10, 1024, 1024], P(None, ('dp', 'head')), may hold values from -0.005859375 to 0.005859375
- kv_mom: float32 [261, 2048], P(None, ('dp', 'head')), may hold values from -0.005859375 to 0.005859375
- head_mom: float32 [1024, 1000], P(('dp', 'head')), may hold values from -0.005859375 to 0.005859375
- latent_mom: float32 [512, 1024], P(None, ('dp', 'head')), may hold values from -6.1035156e-05 to 6.1035156e-05
- small_mom: float32 [6381], replicated, may hold values from -0.0625 to 0.0625
- square_avg: float32 [10, 1024, 1024], P(None, ('dp', 'head')), may hold values from -0.1875 to 0.1875
- kv_avg: float32 [261, 2048], P(None, ('dp', 'head')), may hold values from -0.375 to 0.375
- head_avg: float32 [1024, 1000], P(('dp', 'head')), may hold values from -0.1875 to 0.1875
- latent_avg: float32 [512, 1024], P(None, ('dp', 'head')), may hold values from -6 to 6
- small_avg: float32 [6381], replicated, may hold values from 0.25 to 1.75
Outputs:
- loss_sum: float32 [], replicated
- image_count: float32 [], replicated
- square_grad: float32 [10, 1024, 1024], P(None, ('dp', 'head'))
- square_mom_new: float32 [10, 1024, 1024], P(None, ('dp', 'head'))
- square_new: float32 [10, 1024, 1024], P(None, ('dp', 'head'))
- square_avg_new: float32 [10, 1024, 1024], P(None, ('dp', 'head'))
- kv_grad: float32 [261, 2048], P(None, ('dp', 'head'))
- kv_mom_new: float32 [261, 2048], P(None, ('dp', 'head'))
- kv_new: float32 [261, 2048], P(None, ('dp', 'head'))
- kv_avg_new: float32 [261, 2048], P(None, ('dp', 'head'))
- head_grad: float32 [1024, 1000], P(('dp', 'head'))
- head_mom_new: float32 [1024, 1000], P(('dp', 'head'))
- head_new: float32 [1024, 1000], P(('dp', 'head'))
- head_avg_new: float32 [1024, 1000], P(('dp', 'head'))
- latent_grad: float32 [512, 1024], P(None, ('dp', 'head'))
- latent_mom_new: float32 [512, 1024], P(None, ('dp', 'head'))
- latent_new: float32 [512, 1024], P(None, ('dp', 'head'))
- latent_avg_new: float32 [512, 1024], P(None, ('dp', 'head'))
- small_grad: float32 [6381], replicated
- small_mom_new: float32 [6381], replicated
- small_new: float32 [6381], replicated
- small_avg_new: float32 [6381], replicated
The draws below stay inside these ranges and needn't reach their ends.
Inputs may be any that keep to these rules, and one draw needn't show every extreme that they name: `masks`: each image's mask is 1 on a leading run of at least 64 slots and 0 after it; in every micro-batch some image fills all 512 slots.
All inputs are finite; a program needn't handle non-finite values. No bound on the sum of `valid` on one device may be relied on, other than what follows from the above.
Results may differ from the reference program's by a relative error of at most 0.015.
Values may be sent and summed in bfloat16 or wider, within the bound.
A program may use at most 384 MiB of HBM per device.

```python
import math
import jax
import jax.numpy as jnp
from jax import lax

D = 1024
CIN = 261
LATENTS = 512
HEADS = 8
HEAD_DIM = 128
CLASSES = 1000
MICRO = 4
PIX = 512
IMAGES = 8
SMALL = 6381


def draw_masks(key, part):
    key = jax.random.fold_in(key, 11)
    key_shift, key_extra, key_pick = jax.random.split(key, 3)
    shift = jax.random.randint(key_shift, (MICRO, IMAGES), 0, 4)
    divisor = jnp.array([1, 2, 4, 8], jnp.int32)[shift]
    extra = jax.random.randint(key_extra, (MICRO, IMAGES), 0, PIX // 8 + 1)
    length = jnp.minimum(PIX // divisor + extra, PIX)
    pick = jax.random.randint(key_pick, (MICRO, 1), 0, IMAGES)
    length = jnp.where(jnp.arange(IMAGES)[None, :] == pick, PIX, length)
    return (jnp.arange(PIX)[None, None, :] < length[:, :, None]).astype(jnp.int32)


def set_ends(drawn, own_key, smallest, largest):
    longest = drawn.shape.index(max(drawn.shape))
    spots = []
    for shift in (0, 1):
        where = [jax.random.randint(jax.random.fold_in(own_key, axis), (), 0, length) for axis, length in enumerate(drawn.shape)]
        where[longest] = (where[longest] + shift) % drawn.shape[longest]
        spots.append(tuple(where))
    return drawn.at[spots[0]].set(smallest).at[spots[1]].set(largest)


def block_scale(stream_key, shape, pieces, smallest, largest):
    factor_of, own = 1.0, jax.random.fold_in(stream_key, 6)
    for position, blocks in pieces:
        heights = jnp.exp(jax.random.uniform(jax.random.fold_in(own, position), (blocks,), jnp.float32, smallest / len(pieces), largest / len(pieces)))
        factor_of = factor_of * jnp.repeat(heights, shape[position] // blocks).reshape([-1 if axis == position else 1 for axis in range(len(shape))])
    return factor_of


def noise(key, dims, spread, limit, cuts=(), held_as=jnp.bfloat16):
    factor_of = block_scale(key, dims, cuts, -0.22, 0.18) if cuts else 1.0
    values = jax.random.normal(key, dims, jnp.float32) * spread * factor_of
    return jnp.minimum(jnp.maximum(values, -limit), limit).astype(held_as)


def setup_inputs(seed: int = 0) -> dict:
    streams_of = jax.random.split(jax.random.key(seed), 20)
    pixels = noise(streams_of[0], (MICRO, IMAGES, PIX, CIN), 1.0, 6.0, ((1, 8), (2, 4)))
    masks = draw_masks(jax.random.fold_in(streams_of[19], 71), 0)
    valid = set_ends((jax.random.randint(streams_of[2], (MICRO, IMAGES), 0, 8) < 7).astype(jnp.int32), jax.random.fold_in(streams_of[2], 1), 0, 1)
    labels = set_ends(jax.random.randint(streams_of[3], (MICRO, IMAGES), 0, CLASSES), jax.random.fold_in(streams_of[3], 1), 0, CLASSES - 1).astype(jnp.int32)
    square = noise(streams_of[4], (10, D, D), D ** -0.5, 0.1875, ((1, 32),), jnp.float32)
    kv_weight = noise(streams_of[5], (CIN, 2 * D), CIN ** -0.5, 0.375, ((1, 32),), jnp.float32)
    head_weight = noise(streams_of[6], (D, CLASSES), (D / 4) ** -0.5, 0.375, ((0, 32),), jnp.float32)
    latents = noise(streams_of[7], (LATENTS, D), 1.0, 6.0, ((1, 32),), jnp.float32)
    small = jnp.clip(1.0 + 0.15 * jax.random.normal(streams_of[8], (SMALL,), jnp.float32), 0.25, 1.75)
    square_mom = noise(streams_of[9], (10, D, D), 0.001, 0.005859375, ((1, 32),), jnp.float32)
    kv_mom = noise(streams_of[10], (CIN, 2 * D), 0.001, 0.005859375, ((1, 32),), jnp.float32)
    head_mom = noise(streams_of[11], (D, CLASSES), 0.001, 0.005859375, ((0, 32),), jnp.float32)
    latent_mom = noise(streams_of[12], (LATENTS, D), (1 / (LATENTS * (D * MICRO * IMAGES) ** 0.5)), 6.103515625e-05, ((1, 32),), jnp.float32)
    small_mom = noise(streams_of[13], (SMALL,), 0.01, 0.0625, (), jnp.float32)
    square_avg = noise(streams_of[14], (10, D, D), D ** -0.5, 0.1875, ((1, 32),), jnp.float32)
    kv_avg = noise(streams_of[15], (CIN, 2 * D), CIN ** -0.5, 0.375, ((1, 32),), jnp.float32)
    head_avg = noise(streams_of[16], (D, CLASSES), D ** -0.5, 0.1875, ((0, 32),), jnp.float32)
    latent_avg = noise(streams_of[17], (LATENTS, D), 1.0, 6.0, ((1, 32),), jnp.float32)
    small_avg = jnp.clip(1.0 + 0.15 * jax.random.normal(streams_of[18], (SMALL,), jnp.float32), 0.25, 1.75)
    return {"pixels": pixels, "masks": masks, "valid": valid, "labels": labels, "square": square, "kv_weight": kv_weight, "head_weight": head_weight, "latents": latents, "small": small, "square_mom": square_mom, "kv_mom": kv_mom, "head_mom": head_mom, "latent_mom": latent_mom, "small_mom": small_mom, "square_avg": square_avg, "kv_avg": kv_avg, "head_avg": head_avg, "latent_avg": latent_avg, "small_avg": small_avg}


EPS = 1e-05
NEG_BIG = -1e+30
SMOOTH = 0.1
LEARN_RATE = 20.0
MOMENTUM = 0.9
AVERAGE_DECAY = 0.6

@jax.custom_vjp
def low(v):
    return lax.optimization_barrier(v.astype(jnp.bfloat16)).astype(jnp.float32)

@jax.custom_vjp
def low_back(v):
    return v

def low_keep(v):
    return (low(v), None)

def low_pass(kept, grad):
    return (grad,)

def back_keep(v):
    return (v, None)

def back_low(kept, grad):
    return (low(grad),)
low.defvjp(low_keep, low_pass)
low_back.defvjp(back_keep, back_low)

def both(v):
    return low_back(low(v))

def matmul(a, b):
    return jnp.dot(a, b, precision=lax.Precision.HIGHEST)

def layer_norm(v, gain):
    mean = lax.optimization_barrier(jnp.mean(v, axis=-1, keepdims=True))
    cent = v - mean
    var = lax.optimization_barrier(jnp.mean(cent * cent, axis=-1, keepdims=True))
    return cent * lax.rsqrt(var + EPS) * gain

def attention(query, keys, values, valid_keys):
    scale = query.shape[-1] ** (-0.5)
    scores = jnp.einsum('qhd,khd->hqk', query, keys, precision=lax.Precision.HIGHEST)
    scores = low_back(scores * scale)
    if valid_keys is not None:
        scores = jnp.where(valid_keys[None, None, :] > 0, scores, NEG_BIG)
    probs = low(jax.nn.softmax(scores, axis=-1))
    return both(jnp.einsum('hqk,khd->qhd', probs, values, precision=lax.Precision.HIGHEST))

def feed_forward(hidden, gain, w_in, w_out):
    pre = low_back(matmul(low(layer_norm(hidden, gain)), w_in))
    return hidden + low_back(matmul(low(jax.nn.gelu(pre)), w_out))

def image_loss(params, pixels, mask, valid, label):
    square, kv_weight, head_weight, latents, small = params
    gains = small[:5 * D].reshape(5, D)
    pix_gain = small[5 * D:5 * D + CIN]
    bias = small[5 * D + CIN:]
    normed_pix = low(layer_norm(pixels, pix_gain))
    keyval = both(matmul(normed_pix, kv_weight))
    query = both(matmul(low(layer_norm(latents, gains[0])), square[0]))
    cross = attention(query.reshape(LATENTS, 1, D), keyval[:, :D].reshape(-1, 1, D), keyval[:, D:].reshape(-1, 1, D), mask).reshape(LATENTS, D)
    hidden1 = latents + low_back(matmul(cross, square[1]))
    hidden2 = feed_forward(hidden1, gains[1], square[2], square[3])
    w_qkv = jnp.concatenate([square[4], square[5], square[6]], axis=1)
    qkv = both(matmul(low(layer_norm(hidden2, gains[2])), w_qkv)).reshape(LATENTS, 3, HEADS, HEAD_DIM)
    self_out = attention(qkv[:, 0], qkv[:, 1], qkv[:, 2], None).reshape(LATENTS, D)
    hidden3 = hidden2 + low_back(matmul(self_out, square[7]))
    hidden4 = feed_forward(hidden3, gains[3], square[8], square[9])
    pooled = lax.optimization_barrier(jnp.mean(layer_norm(hidden4, gains[4]), axis=0))
    logits = matmul(low(pooled)[None, :], head_weight)[0] + bias
    logp = jax.nn.log_softmax(logits)
    target = jnp.sum(jnp.where(jnp.arange(CLASSES) == label, logp, 0.0))
    return -valid.astype(jnp.float32) * ((1.0 - SMOOTH) * target + SMOOTH * jnp.mean(logp))

def nesterov(weight, grad, mom, avg, rate):
    mom_new = MOMENTUM * mom + grad
    weight_new = weight - rate * (grad + MOMENTUM * mom_new)
    avg_new = AVERAGE_DECAY * avg + (1.0 - AVERAGE_DECAY) * weight_new
    return (grad, mom_new, weight_new, avg_new)

def reference(pixels, masks, valid, labels, square, kv_weight, head_weight, latents, small, square_mom, kv_mom, head_mom, latent_mom, small_mom, square_avg, kv_avg, head_avg, latent_avg, small_avg):
    flat_pix = pixels.astype(jnp.float32).reshape(MICRO * IMAGES, PIX, CIN)
    flat_mask = masks.reshape(MICRO * IMAGES, PIX)
    flat_valid = valid.reshape(MICRO * IMAGES)
    flat_label = labels.reshape(MICRO * IMAGES)

    def total(params):
        rounded = tuple((low(w) for w in params[:4])) + (params[4],)
        one = jax.checkpoint(lambda item: image_loss(rounded, item[0], item[1], item[2], item[3]))
        return jnp.sum(lax.map(one, (flat_pix, flat_mask, flat_valid, flat_label)))
    params = (square, kv_weight, head_weight, latents, small)
    loss_sum, pull = jax.vjp(total, params)
    grads = pull(jnp.ones((), loss_sum.dtype))[0]
    count = jnp.maximum(jnp.sum(valid.astype(jnp.float32)), 1.0)
    latent_rate = LATENTS * math.sqrt(D * MICRO * IMAGES) / 32.0
    rates = (LEARN_RATE, LEARN_RATE, LEARN_RATE, latent_rate, LEARN_RATE)
    results = [loss_sum, count]
    moms = (square_mom, kv_mom, head_mom, latent_mom, small_mom)
    avgs = (square_avg, kv_avg, head_avg, latent_avg, small_avg)
    for weight, grad, mom, avg, rate in zip(params, grads, moms, avgs, rates):
        results.extend(nesterov(weight, grad / count, mom, avg, rate))
    return tuple(results)
```

```python
import math

import jax
import jax.numpy as jnp
from jax import lax
from jax.sharding import PartitionSpec as P

D = 1024
CIN = 261
LATENTS = 512
HEADS = 8
HEAD_DIM = 128
MICRO = 4
IMG_DEV = 1


EPS = 1e-05
NEG_BIG = -1e30
SMOOTH = 0.1
LEARN_RATE = 20.0
MOMENTUM = 0.9
AVERAGE_DECAY = 0.6


def layer_norm(v, gain):
    mean = jnp.mean(v, axis=-1, keepdims=True)
    cent = v - mean
    var = jnp.mean(cent * cent, axis=-1, keepdims=True)
    return cent * lax.rsqrt(var + EPS) * gain


def dot_nn(left, right):
    return jnp.dot(left, right, preferred_element_type=jnp.float32)


def dot_tn(left, right):
    return lax.dot_general(
        left, right, (((0,), (0,)), ((), ())), preferred_element_type=jnp.float32
    )


def dot_nt(left, right):
    return lax.dot_general(
        left, right, (((1,), (1,)), ((), ())), preferred_element_type=jnp.float32
    )


def scores_of(query, keys, valid_keys):
    scores = jnp.einsum("qhd,khd->hqk", query, keys, preferred_element_type=jnp.float32)
    scores = scores * query.shape[-1] ** (-0.5)
    if valid_keys is not None:
        scores = jnp.where(valid_keys[None, None, :], scores, NEG_BIG)
    return scores


def attend(query, keys, values, valid_keys):
    scores = scores_of(query, keys, valid_keys)
    log_total = jax.nn.logsumexp(scores, axis=-1, keepdims=True)
    probs = jnp.exp(scores - log_total).astype(jnp.bfloat16)
    out = jnp.einsum("hqk,khd->qhd", probs, values, preferred_element_type=jnp.float32)
    return (out.astype(jnp.bfloat16), log_total)


def attend_back(query, keys, values, log_total, d_out, valid_keys):
    scale = query.shape[-1] ** (-0.5)
    probs = jnp.exp(scores_of(query, keys, valid_keys) - log_total)
    probs_b = probs.astype(jnp.bfloat16)
    d_probs = jnp.einsum("qhd,khd->hqk", d_out, values, preferred_element_type=jnp.float32)
    d_scores = probs * (d_probs - jnp.sum(probs * d_probs, axis=-1, keepdims=True))
    d_scores = d_scores.astype(jnp.bfloat16)
    d_query = jnp.einsum("hqk,khd->qhd", d_scores, keys, preferred_element_type=jnp.float32) * scale
    d_keys = jnp.einsum("hqk,qhd->khd", d_scores, query, preferred_element_type=jnp.float32) * scale
    d_values = jnp.einsum("hqk,qhd->khd", probs_b, d_out, preferred_element_type=jnp.float32)
    return (d_query, d_keys, d_values)


def mlp_forward(hidden, gain, w_in, w_out):
    normed = layer_norm(hidden, gain).astype(jnp.bfloat16)
    pre = dot_nn(normed, w_in)
    active = jax.nn.gelu(pre).astype(jnp.bfloat16)
    return (hidden + dot_nn(active, w_out), (normed, pre, active))


def mlp_backward(hidden, gain, w_in, w_out, saved, d_next):
    normed, pre, active = saved
    d_next_b = d_next.astype(jnp.bfloat16)
    d_w_out = dot_tn(active, d_next_b)
    d_active = dot_nt(d_next_b, w_out)
    d_pre = jax.vjp(jax.nn.gelu, pre)[1](d_active)[0].astype(jnp.bfloat16)
    d_w_in = dot_tn(normed, d_pre)
    d_normed = dot_nt(d_pre, w_in)
    d_hidden, d_gain = jax.vjp(layer_norm, hidden, gain)[1](d_normed)
    return (d_next + d_hidden, d_gain, d_w_in, d_w_out)


def image_grads(weights, small, pixel_own, mask_row, valid_one, label, loss_scale, head_first):
    square, kv_weight, head_weight, latent_all, w_qkv = weights
    gains = small[: 5 * D].reshape(5, D)
    pix_gain = small[5 * D : 5 * D + CIN]
    bias = small[5 * D + CIN :]
    rows = latent_all.shape[0] // lax.axis_size("head")
    start = lax.axis_index("head") * rows
    latent_own = lax.dynamic_slice_in_dim(latent_all, start, rows, 0).astype(jnp.float32)
    valid_keys = mask_row > 0
    pix_float = pixel_own.astype(jnp.float32)
    normed_pix = layer_norm(pix_float, pix_gain).astype(jnp.bfloat16)
    kv_own = dot_nn(normed_pix, kv_weight).astype(jnp.bfloat16)
    kv_all = lax.all_gather(kv_own, "head", axis=0, tiled=True)
    keys_px = kv_all[:, :D].reshape(-1, 1, D)
    values_px = kv_all[:, D:].reshape(-1, 1, D)
    query_norm = layer_norm(latent_own, gains[0]).astype(jnp.bfloat16)
    query = dot_nn(query_norm, square[0]).astype(jnp.bfloat16).reshape(rows, 1, D)
    cross_out, cross_total = attend(query, keys_px, values_px, valid_keys)
    cross_out = cross_out.reshape(rows, D)
    hidden1 = latent_own + dot_nn(cross_out, square[1])
    hidden2, mlp_first = mlp_forward(hidden1, gains[1], square[2], square[3])
    self_norm = layer_norm(hidden2, gains[2]).astype(jnp.bfloat16)
    qkv = dot_nn(self_norm, w_qkv).astype(jnp.bfloat16)
    kv_latent = lax.all_gather(qkv[:, D:], "head", axis=0, tiled=True)
    self_query = qkv[:, :D].reshape(rows, HEADS, HEAD_DIM)
    self_keys = kv_latent[:, :D].reshape(-1, HEADS, HEAD_DIM)
    self_values = kv_latent[:, D:].reshape(-1, HEADS, HEAD_DIM)
    self_out, self_total = attend(self_query, self_keys, self_values, None)
    self_out = self_out.reshape(rows, D)
    hidden3 = hidden2 + dot_nn(self_out, square[7])
    hidden4, mlp_second = mlp_forward(hidden3, gains[3], square[8], square[9])
    final = layer_norm(hidden4, gains[4])
    pooled = lax.psum(jnp.sum(final, axis=0), "head") / latent_all.shape[0]
    pooled_b = pooled.astype(jnp.bfloat16)
    logits = dot_nn(pooled_b[None, :], head_weight)[0] + bias
    logp = jax.nn.log_softmax(logits)
    picked = jnp.arange(logits.shape[0]) == label
    loss = -valid_one * (
        (1.0 - SMOOTH) * jnp.sum(jnp.where(picked, logp, 0.0)) + SMOOTH * jnp.mean(logp)
    )
    target = (1.0 - SMOOTH) * picked.astype(jnp.float32) + SMOOTH / logits.shape[0]
    d_logits = valid_one * loss_scale * (jnp.exp(logp) - target)
    d_bias = d_logits * head_first
    d_head = pooled_b.astype(jnp.float32)[:, None] * d_logits[None, :] * head_first
    d_pooled = jnp.dot(head_weight.astype(jnp.float32), d_logits)
    d_final = jnp.broadcast_to(d_pooled / latent_all.shape[0], final.shape)
    d_hidden4, d_gain4 = jax.vjp(layer_norm, hidden4, gains[4])[1](d_final)
    d_hidden3, d_gain3, d_w8, d_w9 = mlp_backward(
        hidden3, gains[3], square[8], square[9], mlp_second, d_hidden4
    )
    d_hidden3_b = d_hidden3.astype(jnp.bfloat16)
    d_w7 = dot_tn(self_out, d_hidden3_b)
    d_self_out = dot_nt(d_hidden3_b, square[7]).astype(jnp.bfloat16).reshape(rows, HEADS, HEAD_DIM)
    d_query, d_keys, d_values = attend_back(
        self_query, self_keys, self_values, self_total, d_self_out, None
    )
    d_kv_terms = jnp.concatenate([d_keys.reshape(-1, D), d_values.reshape(-1, D)], axis=1)
    d_kv_own = lax.psum_scatter(
        d_kv_terms.astype(jnp.bfloat16), "head", scatter_dimension=0, tiled=True
    ).astype(jnp.float32)
    d_qkv = jnp.concatenate([d_query.reshape(rows, D), d_kv_own], axis=1).astype(jnp.bfloat16)
    d_w_qkv = dot_tn(self_norm, d_qkv)
    d_self_norm = dot_nt(d_qkv, w_qkv)
    d_hidden2_norm, d_gain2 = jax.vjp(layer_norm, hidden2, gains[2])[1](d_self_norm)
    d_hidden2 = d_hidden3 + d_hidden2_norm
    d_hidden1, d_gain1, d_w2, d_w3 = mlp_backward(
        hidden1, gains[1], square[2], square[3], mlp_first, d_hidden2
    )
    d_hidden1_b = d_hidden1.astype(jnp.bfloat16)
    d_w1 = dot_tn(cross_out, d_hidden1_b)
    d_cross = dot_nt(d_hidden1_b, square[1]).astype(jnp.bfloat16).reshape(rows, 1, D)
    d_query, d_keys, d_values = attend_back(
        query, keys_px, values_px, cross_total, d_cross, valid_keys
    )
    d_px_terms = jnp.concatenate([d_keys.reshape(-1, D), d_values.reshape(-1, D)], axis=1)
    d_kv_px = lax.psum_scatter(
        d_px_terms.astype(jnp.bfloat16), "head", scatter_dimension=0, tiled=True
    )
    d_kv_turned = dot_tn(d_kv_px, normed_pix)
    d_normed_pix = dot_nt(d_kv_px, kv_weight)
    d_pix_gain = jax.vjp(layer_norm, pix_float, pix_gain)[1](d_normed_pix)[1]
    d_query_b = d_query.reshape(rows, D).astype(jnp.bfloat16)
    d_w0 = dot_tn(query_norm, d_query_b)
    d_query_norm = dot_nt(d_query_b, square[0])
    d_latent_norm, d_gain0 = jax.vjp(layer_norm, latent_own, gains[0])[1](d_query_norm)
    d_latent_own = d_hidden1 + d_latent_norm
    d_square = jnp.stack(
        [
            d_w0,
            d_w1,
            d_w2,
            d_w3,
            d_w_qkv[:, :D],
            d_w_qkv[:, D : 2 * D],
            d_w_qkv[:, 2 * D :],
            d_w7,
            d_w8,
            d_w9,
        ]
    )
    latent_turned = lax.dynamic_update_slice_in_dim(
        jnp.zeros((D, latent_all.shape[0]), jnp.float32), d_latent_own.T, start, 1
    )
    d_small = jnp.concatenate(
        [jnp.stack([d_gain0, d_gain1, d_gain2, d_gain3, d_gain4]).reshape(-1), d_pix_gain, d_bias]
    )
    return ((d_square, d_kv_turned[None], d_head[None], latent_turned[None], d_small), loss)


def owner_layout(reduced):
    return (reduced[0], reduced[1][0].T, reduced[2][0], reduced[3][0].T)


def nesterov(weight, grad, mom, avg, rate):
    mom_new = MOMENTUM * mom + grad
    weight_new = weight - rate * (grad + MOMENTUM * mom_new)
    avg_new = AVERAGE_DECAY * avg + (1.0 - AVERAGE_DECAY) * weight_new
    return (grad, mom_new, weight_new, avg_new)


def per_device_rows(
    pixels,
    masks,
    valid,
    labels,
    square,
    kv_weight,
    head_weight,
    latents,
    small,
    square_mom,
    kv_mom,
    head_mom,
    latent_mom,
    small_mom,
    square_avg,
    kv_avg,
    head_avg,
    latent_avg,
    small_avg,
):
    gathered = (
        lax.all_gather(square.astype(jnp.bfloat16), ("dp", "head"), axis=1, tiled=True),
        lax.all_gather(kv_weight.astype(jnp.bfloat16), ("dp", "head"), axis=1, tiled=True),
        lax.all_gather(head_weight.astype(jnp.bfloat16), ("dp", "head"), axis=0, tiled=True),
        lax.all_gather(latents.astype(jnp.bfloat16), ("dp", "head"), axis=1, tiled=True),
    )
    full_square = gathered[0]
    w_qkv = jnp.concatenate([full_square[4], full_square[5], full_square[6]], axis=1)
    weights = (full_square, gathered[1], gathered[2], gathered[3], w_qkv)
    head_first = (lax.axis_index("head") == 0).astype(jnp.float32)
    valid_float = valid.astype(jnp.float32)
    early_count = lax.psum(jnp.sum(valid_float), "dp")
    loss_scale = 1.0 / jnp.maximum(early_count, 1.0)
    kv_shape = gathered[1].shape
    lat_shape = gathered[3].shape
    big_zero = (
        jnp.zeros(full_square.shape, jnp.float32),
        jnp.zeros((1, kv_shape[1], kv_shape[0]), jnp.float32),
        jnp.zeros((1,) + gathered[2].shape, jnp.float32),
        jnp.zeros((1, lat_shape[1], lat_shape[0]), jnp.float32),
    )

    def micro_step(carry, batch):
        big, small_acc, loss_acc = carry
        pix_micro, mask_micro, valid_micro, label_micro = batch
        grads, loss_part = image_grads(
            weights,
            small,
            pix_micro[0],
            mask_micro[0],
            valid_micro[0],
            label_micro[0],
            loss_scale,
            head_first,
        )
        reduced = (grads[0], grads[1], grads[2], grads[3])
        big = tuple((a + b for a, b in zip(big, reduced)))
        return ((big, small_acc + grads[4], loss_acc + loss_part), None)

    start_carry = (big_zero, jnp.zeros(small.shape, jnp.float32), jnp.float32(0.0))
    (big, small_acc, loss_acc), _ = lax.scan(
        micro_step, start_carry, (pixels, masks, valid_float, labels)
    )
    big = owner_layout(
        (
            lax.psum_scatter(big[0], ("dp", "head"), scatter_dimension=1, tiled=True),
            lax.psum_scatter(big[1], ("dp", "head"), scatter_dimension=1, tiled=True),
            lax.psum_scatter(big[2], ("dp", "head"), scatter_dimension=1, tiled=True),
            lax.psum_scatter(big[3], ("dp", "head"), scatter_dimension=1, tiled=True),
        )
    )
    small_total, loss_sum, count = lax.psum(
        (small_acc, loss_acc * head_first, jnp.sum(valid_float) * head_first), ("dp", "head")
    )
    count = jnp.maximum(count, 1.0)
    latent_rate = LATENTS * math.sqrt(D * MICRO * IMG_DEV * lax.axis_size("dp")) / 32.0
    rates = (LEARN_RATE, LEARN_RATE, LEARN_RATE, latent_rate, LEARN_RATE)
    results = [loss_sum, count]
    params = (square, kv_weight, head_weight, latents, small)
    moms = (square_mom, kv_mom, head_mom, latent_mom, small_mom)
    avgs = (square_avg, kv_avg, head_avg, latent_avg, small_avg)
    for weight, grad, mom, avg, rate in zip(params, tuple(big) + (small_total,), moms, avgs, rates):
        results.extend(nesterov(weight, grad, mom, avg, rate))
    return tuple(results)


def image_forward_back(weights, small, pixels, mask_row, valid_one, label):
    square, kv_weight, head_weight, latent_all = weights
    gains = small[: 5 * D].reshape(5, D)
    pix_gain = small[5 * D : 5 * D + CIN]
    bias = small[5 * D + CIN :]
    rows = latent_all.shape[0]
    latent = latent_all.astype(jnp.float32)
    valid_keys = mask_row > 0
    pix_float = pixels.astype(jnp.float32)
    normed_pix = layer_norm(pix_float, pix_gain).astype(jnp.bfloat16)
    kv = dot_nn(normed_pix, kv_weight).astype(jnp.bfloat16)
    keys_px = kv[:, :D].reshape(-1, 1, D)
    values_px = kv[:, D:].reshape(-1, 1, D)
    query_norm = layer_norm(latent, gains[0]).astype(jnp.bfloat16)
    query = dot_nn(query_norm, square[0]).astype(jnp.bfloat16).reshape(rows, 1, D)
    cross_out, cross_total = attend(query, keys_px, values_px, valid_keys)
    cross_out = cross_out.reshape(rows, D)
    hidden1 = latent + dot_nn(cross_out, square[1])
    hidden2, mlp_first = mlp_forward(hidden1, gains[1], square[2], square[3])
    self_norm = layer_norm(hidden2, gains[2]).astype(jnp.bfloat16)
    qkv = [dot_nn(self_norm, square[i]).astype(jnp.bfloat16).reshape(rows, HEADS, HEAD_DIM) for i in (4, 5, 6)]
    self_out, self_total = attend(qkv[0], qkv[1], qkv[2], None)
    self_out = self_out.reshape(rows, D)
    hidden3 = hidden2 + dot_nn(self_out, square[7])
    hidden4, mlp_second = mlp_forward(hidden3, gains[3], square[8], square[9])
    final = layer_norm(hidden4, gains[4])
    pooled_b = (jnp.sum(final, axis=0) / rows).astype(jnp.bfloat16)
    logits = dot_nn(pooled_b[None, :], head_weight)[0] + bias
    logp = jax.nn.log_softmax(logits)
    picked = jnp.arange(logits.shape[0]) == label
    loss = -valid_one * (
        (1.0 - SMOOTH) * jnp.sum(jnp.where(picked, logp, 0.0)) + SMOOTH * jnp.mean(logp)
    )
    target = (1.0 - SMOOTH) * picked.astype(jnp.float32) + SMOOTH / logits.shape[0]
    d_logits = valid_one * (jnp.exp(logp) - target)
    d_pooled = jnp.dot(head_weight.astype(jnp.float32), d_logits)
    d_final = jnp.broadcast_to(d_pooled / rows, final.shape)
    d_hidden4, d_gain4 = jax.vjp(layer_norm, hidden4, gains[4])[1](d_final)
    d_hidden3, d_gain3, d_w8, d_w9 = mlp_backward(
        hidden3, gains[3], square[8], square[9], mlp_second, d_hidden4
    )
    d_hidden3_b = d_hidden3.astype(jnp.bfloat16)
    d_w7 = dot_tn(self_out, d_hidden3_b)
    d_self_out = dot_nt(d_hidden3_b, square[7]).astype(jnp.bfloat16).reshape(rows, HEADS, HEAD_DIM)
    d_parts = attend_back(qkv[0], qkv[1], qkv[2], self_total, d_self_out, None)
    d_parts = [d.reshape(rows, D).astype(jnp.bfloat16) for d in d_parts]
    d_w456 = [dot_tn(self_norm, d) for d in d_parts]
    d_self_norm = sum(dot_nt(d, square[4 + i]) for i, d in enumerate(d_parts))
    d_hidden2_norm, d_gain2 = jax.vjp(layer_norm, hidden2, gains[2])[1](d_self_norm)
    d_hidden2 = d_hidden3 + d_hidden2_norm
    d_hidden1, d_gain1, d_w2, d_w3 = mlp_backward(
        hidden1, gains[1], square[2], square[3], mlp_first, d_hidden2
    )
    d_hidden1_b = d_hidden1.astype(jnp.bfloat16)
    d_w1 = dot_tn(cross_out, d_hidden1_b)
    d_cross = dot_nt(d_hidden1_b, square[1]).astype(jnp.bfloat16).reshape(rows, 1, D)
    d_query, d_keys, d_values = attend_back(
        query, keys_px, values_px, cross_total, d_cross, valid_keys
    )
    d_kv_px = jnp.concatenate([d_keys.reshape(-1, D), d_values.reshape(-1, D)], axis=1).astype(jnp.bfloat16)
    d_kv_turned = dot_tn(d_kv_px, normed_pix)
    d_normed_pix = dot_nt(d_kv_px, kv_weight)
    d_pix_gain = jax.vjp(layer_norm, pix_float, pix_gain)[1](d_normed_pix)[1]
    d_query_b = d_query.reshape(rows, D).astype(jnp.bfloat16)
    d_w0 = dot_tn(query_norm, d_query_b)
    d_query_norm = dot_nt(d_query_b, square[0])
    d_latent_norm, d_gain0 = jax.vjp(layer_norm, latent, gains[0])[1](d_query_norm)
    d_latent = d_hidden1 + d_latent_norm
    d_square = [d_w0, d_w1, d_w2, d_w3] + d_w456 + [d_w7, d_w8, d_w9]
    d_small = jnp.concatenate(
        [d_gain0, d_gain1, d_gain2, d_gain3, d_gain4, d_pix_gain, d_logits]
    )
    return d_square, d_kv_turned, d_latent.T, d_small, pooled_b, d_logits, loss


ALL = ("dp", "head")


def gather_rows(shard):
    return lax.all_gather(shard, ALL, axis=0, tiled=True)


def scatter_rows(partial):
    return lax.psum_scatter(partial.astype(jnp.bfloat16), ALL, scatter_dimension=0, tiled=True).astype(jnp.float32)


def per_device_images(
    pixels,
    masks,
    valid,
    labels,
    square,
    kv_weight,
    head_weight,
    latents,
    small,
    square_mom,
    kv_mom,
    head_mom,
    latent_mom,
    small_mom,
    square_avg,
    kv_avg,
    head_avg,
    latent_avg,
    small_avg,
):
    bf = jnp.bfloat16
    micro = lax.axis_index("head")
    pick = lambda a: lax.dynamic_index_in_dim(a, micro, 0, keepdims=False)[0]
    image = lax.all_to_all(pixels[:, 0], "head", split_axis=0, concat_axis=1, tiled=True)[0]
    latent_all = gather_rows(latents.astype(bf).T).T
    kv_all = gather_rows(kv_weight.astype(bf).T).T
    square_all = [gather_rows(square[i].astype(bf)) for i in range(10)]
    head_all = gather_rows(head_weight.astype(bf))
    valid_float = valid.astype(jnp.float32)
    d_square, d_kv, d_lat, d_small, pooled_b, d_logits, loss = image_forward_back(
        (square_all, kv_all, head_all, latent_all), small, image, pick(masks), pick(valid_float), pick(labels)
    )
    small_total, loss_sum, count = lax.psum((d_small, loss, pick(valid_float)), ALL)
    count = jnp.maximum(count, 1.0)
    pooled_all = lax.all_gather(pooled_b, ALL, axis=0)
    logits_all = lax.all_gather(d_logits, ALL, axis=0)
    own = head_weight.shape[0]
    first = (lax.axis_index("dp") * lax.axis_size("head") + micro) * own
    pooled_own = lax.dynamic_slice_in_dim(pooled_all, first, own, 1).astype(jnp.float32)
    d_head = lax.dot_general(
        pooled_own, logits_all, (((0,), (0,)), ((), ())), precision=lax.Precision.HIGHEST
    )
    d_square = jnp.stack([scatter_rows(d) for d in d_square])
    grads = (d_square, scatter_rows(d_kv).T, d_head, scatter_rows(d_lat).T, small_total)
    latent_rate = LATENTS * math.sqrt(D * MICRO * IMG_DEV * lax.axis_size("dp")) / 32.0
    rates = (LEARN_RATE, LEARN_RATE, LEARN_RATE, latent_rate, LEARN_RATE)
    results = [loss_sum, count]
    params = (square, kv_weight, head_weight, latents, small)
    moms = (square_mom, kv_mom, head_mom, latent_mom, small_mom)
    avgs = (square_avg, kv_avg, head_avg, latent_avg, small_avg)
    for weight, grad, mom, avg, rate in zip(params, grads, moms, avgs, rates):
        results.extend(nesterov(weight, grad / count, mom, avg, rate))
    return tuple(results)


def solution(mesh):
    in_specs = (
        P(None, "dp", "head", None),
        P(None, "dp", None),
        P(None, "dp"),
        P(None, "dp"),
        P(None, ("dp", "head"), None),
        P(None, ("dp", "head")),
        P(("dp", "head"), None),
        P(None, ("dp", "head")),
        P(),
        P(None, ("dp", "head"), None),
        P(None, ("dp", "head")),
        P(("dp", "head"), None),
        P(None, ("dp", "head")),
        P(),
        P(None, ("dp", "head"), None),
        P(None, ("dp", "head")),
        P(("dp", "head"), None),
        P(None, ("dp", "head")),
        P(),
    )
    out_specs = (
        P(),
        P(),
        P(None, ("dp", "head"), None),
        P(None, ("dp", "head"), None),
        P(None, ("dp", "head"), None),
        P(None, ("dp", "head"), None),
        P(None, ("dp", "head")),
        P(None, ("dp", "head")),
        P(None, ("dp", "head")),
        P(None, ("dp", "head")),
        P(("dp", "head"), None),
        P(("dp", "head"), None),
        P(("dp", "head"), None),
        P(("dp", "head"), None),
        P(None, ("dp", "head")),
        P(None, ("dp", "head")),
        P(None, ("dp", "head")),
        P(None, ("dp", "head")),
        P(),
        P(),
        P(),
        P(),
    )
    whole_images = mesh.shape["head"] == MICRO
    per_device = per_device_images if whole_images else per_device_rows
    return jax.shard_map(
        per_device, mesh=mesh, in_specs=in_specs, out_specs=out_specs, check_vma=False
    )
```

```python
import functools
import math

import jax
import jax.numpy as jnp
from jax import lax
from jax.experimental import pallas as pl
from jax.experimental.pallas import tpu as pltpu
from jax.sharding import PartitionSpec as P

D = 1024
CIN = 261
LATENTS = 512
HEADS = 8
HEAD_DIM = 128
MICRO = 4
IMG_DEV = 1


EPS = 1e-05
NEG_BIG = -1e30
SMOOTH = 0.1
LEARN_RATE = 20.0
MOMENTUM = 0.9
AVERAGE_DECAY = 0.6


def layer_norm(v, gain):
    mean = jnp.mean(v, axis=-1, keepdims=True)
    cent = v - mean
    var = jnp.mean(cent * cent, axis=-1, keepdims=True)
    return cent * lax.rsqrt(var + EPS) * gain


def dot_nn(left, right):
    return jnp.dot(left, right, preferred_element_type=jnp.float32)


def dot_tn(left, right):
    return lax.dot_general(
        left, right, (((0,), (0,)), ((), ())), preferred_element_type=jnp.float32
    )


def dot_nt(left, right):
    return lax.dot_general(
        left, right, (((1,), (1,)), ((), ())), preferred_element_type=jnp.float32
    )


def scores_of(query, keys, valid_keys):
    scores = jnp.einsum("qhd,khd->hqk", query, keys, preferred_element_type=jnp.float32)
    scores = scores * query.shape[-1] ** (-0.5)
    if valid_keys is not None:
        scores = jnp.where(valid_keys[None, None, :], scores, NEG_BIG)
    return scores


def attend(query, keys, values, valid_keys):
    scores = scores_of(query, keys, valid_keys)
    log_total = jax.nn.logsumexp(scores, axis=-1, keepdims=True)
    probs = jnp.exp(scores - log_total).astype(jnp.bfloat16)
    out = jnp.einsum("hqk,khd->qhd", probs, values, preferred_element_type=jnp.float32)
    return (out.astype(jnp.bfloat16), log_total)


def attend_back(query, keys, values, log_total, d_out, valid_keys):
    scale = query.shape[-1] ** (-0.5)
    probs = jnp.exp(scores_of(query, keys, valid_keys) - log_total)
    probs_b = probs.astype(jnp.bfloat16)
    d_probs = jnp.einsum("qhd,khd->hqk", d_out, values, preferred_element_type=jnp.float32)
    d_scores = probs * (d_probs - jnp.sum(probs * d_probs, axis=-1, keepdims=True))
    d_scores = d_scores.astype(jnp.bfloat16)
    d_query = jnp.einsum("hqk,khd->qhd", d_scores, keys, preferred_element_type=jnp.float32) * scale
    d_keys = jnp.einsum("hqk,qhd->khd", d_scores, query, preferred_element_type=jnp.float32) * scale
    d_values = jnp.einsum("hqk,qhd->khd", probs_b, d_out, preferred_element_type=jnp.float32)
    return (d_query, d_keys, d_values)


def mlp_forward(hidden, gain, w_in, w_out):
    normed = layer_norm(hidden, gain).astype(jnp.bfloat16)
    pre = dot_nn(normed, w_in)
    active = jax.nn.gelu(pre).astype(jnp.bfloat16)
    return (hidden + dot_nn(active, w_out), (normed, pre, active))


def mlp_backward(hidden, gain, w_in, w_out, saved, d_next):
    normed, pre, active = saved
    d_next_b = d_next.astype(jnp.bfloat16)
    d_w_out = dot_tn(active, d_next_b)
    d_active = dot_nt(d_next_b, w_out)
    d_pre = jax.vjp(jax.nn.gelu, pre)[1](d_active)[0].astype(jnp.bfloat16)
    d_w_in = dot_tn(normed, d_pre)
    d_normed = dot_nt(d_pre, w_in)
    d_hidden, d_gain = jax.vjp(layer_norm, hidden, gain)[1](d_normed)
    return (d_next + d_hidden, d_gain, d_w_in, d_w_out)


def image_grads(weights, small, pixel_own, mask_row, valid_one, label, loss_scale, head_first):
    square, kv_weight, head_weight, latent_all, w_qkv = weights
    gains = small[: 5 * D].reshape(5, D)
    pix_gain = small[5 * D : 5 * D + CIN]
    bias = small[5 * D + CIN :]
    rows = latent_all.shape[0] // lax.axis_size("head")
    start = lax.axis_index("head") * rows
    latent_own = lax.dynamic_slice_in_dim(latent_all, start, rows, 0).astype(jnp.float32)
    valid_keys = mask_row > 0
    pix_float = pixel_own.astype(jnp.float32)
    normed_pix = layer_norm(pix_float, pix_gain).astype(jnp.bfloat16)
    kv_own = dot_nn(normed_pix, kv_weight).astype(jnp.bfloat16)
    kv_all = lax.all_gather(kv_own, "head", axis=0, tiled=True)
    keys_px = kv_all[:, :D].reshape(-1, 1, D)
    values_px = kv_all[:, D:].reshape(-1, 1, D)
    query_norm = layer_norm(latent_own, gains[0]).astype(jnp.bfloat16)
    query = dot_nn(query_norm, square[0]).astype(jnp.bfloat16).reshape(rows, 1, D)
    cross_out, cross_total = attend(query, keys_px, values_px, valid_keys)
    cross_out = cross_out.reshape(rows, D)
    hidden1 = latent_own + dot_nn(cross_out, square[1])
    hidden2, mlp_first = mlp_forward(hidden1, gains[1], square[2], square[3])
    self_norm = layer_norm(hidden2, gains[2]).astype(jnp.bfloat16)
    qkv = dot_nn(self_norm, w_qkv).astype(jnp.bfloat16)
    kv_latent = lax.all_gather(qkv[:, D:], "head", axis=0, tiled=True)
    self_query = qkv[:, :D].reshape(rows, HEADS, HEAD_DIM)
    self_keys = kv_latent[:, :D].reshape(-1, HEADS, HEAD_DIM)
    self_values = kv_latent[:, D:].reshape(-1, HEADS, HEAD_DIM)
    self_out, self_total = attend(self_query, self_keys, self_values, None)
    self_out = self_out.reshape(rows, D)
    hidden3 = hidden2 + dot_nn(self_out, square[7])
    hidden4, mlp_second = mlp_forward(hidden3, gains[3], square[8], square[9])
    final = layer_norm(hidden4, gains[4])
    pooled = lax.psum(jnp.sum(final, axis=0), "head") / latent_all.shape[0]
    pooled_b = pooled.astype(jnp.bfloat16)
    logits = dot_nn(pooled_b[None, :], head_weight)[0] + bias
    logp = jax.nn.log_softmax(logits)
    picked = jnp.arange(logits.shape[0]) == label
    loss = -valid_one * (
        (1.0 - SMOOTH) * jnp.sum(jnp.where(picked, logp, 0.0)) + SMOOTH * jnp.mean(logp)
    )
    target = (1.0 - SMOOTH) * picked.astype(jnp.float32) + SMOOTH / logits.shape[0]
    d_logits = valid_one * loss_scale * (jnp.exp(logp) - target)
    d_bias = d_logits * head_first
    d_head = pooled_b.astype(jnp.float32)[:, None] * d_logits[None, :] * head_first
    d_pooled = jnp.dot(head_weight.astype(jnp.float32), d_logits)
    d_final = jnp.broadcast_to(d_pooled / latent_all.shape[0], final.shape)
    d_hidden4, d_gain4 = jax.vjp(layer_norm, hidden4, gains[4])[1](d_final)
    d_hidden3, d_gain3, d_w8, d_w9 = mlp_backward(
        hidden3, gains[3], square[8], square[9], mlp_second, d_hidden4
    )
    d_hidden3_b = d_hidden3.astype(jnp.bfloat16)
    d_w7 = dot_tn(self_out, d_hidden3_b)
    d_self_out = dot_nt(d_hidden3_b, square[7]).astype(jnp.bfloat16).reshape(rows, HEADS, HEAD_DIM)
    d_query, d_keys, d_values = attend_back(
        self_query, self_keys, self_values, self_total, d_self_out, None
    )
    d_kv_terms = jnp.concatenate([d_keys.reshape(-1, D), d_values.reshape(-1, D)], axis=1)
    d_kv_own = lax.psum_scatter(
        d_kv_terms.astype(jnp.bfloat16), "head", scatter_dimension=0, tiled=True
    ).astype(jnp.float32)
    d_qkv = jnp.concatenate([d_query.reshape(rows, D), d_kv_own], axis=1).astype(jnp.bfloat16)
    d_w_qkv = dot_tn(self_norm, d_qkv)
    d_self_norm = dot_nt(d_qkv, w_qkv)
    d_hidden2_norm, d_gain2 = jax.vjp(layer_norm, hidden2, gains[2])[1](d_self_norm)
    d_hidden2 = d_hidden3 + d_hidden2_norm
    d_hidden1, d_gain1, d_w2, d_w3 = mlp_backward(
        hidden1, gains[1], square[2], square[3], mlp_first, d_hidden2
    )
    d_hidden1_b = d_hidden1.astype(jnp.bfloat16)
    d_w1 = dot_tn(cross_out, d_hidden1_b)
    d_cross = dot_nt(d_hidden1_b, square[1]).astype(jnp.bfloat16).reshape(rows, 1, D)
    d_query, d_keys, d_values = attend_back(
        query, keys_px, values_px, cross_total, d_cross, valid_keys
    )
    d_px_terms = jnp.concatenate([d_keys.reshape(-1, D), d_values.reshape(-1, D)], axis=1)
    d_kv_px = lax.psum_scatter(
        d_px_terms.astype(jnp.bfloat16), "head", scatter_dimension=0, tiled=True
    )
    d_kv_turned = dot_tn(d_kv_px, normed_pix)
    d_normed_pix = dot_nt(d_kv_px, kv_weight)
    d_pix_gain = jax.vjp(layer_norm, pix_float, pix_gain)[1](d_normed_pix)[1]
    d_query_b = d_query.reshape(rows, D).astype(jnp.bfloat16)
    d_w0 = dot_tn(query_norm, d_query_b)
    d_query_norm = dot_nt(d_query_b, square[0])
    d_latent_norm, d_gain0 = jax.vjp(layer_norm, latent_own, gains[0])[1](d_query_norm)
    d_latent_own = d_hidden1 + d_latent_norm
    d_square = jnp.stack(
        [
            d_w0,
            d_w1,
            d_w2,
            d_w3,
            d_w_qkv[:, :D],
            d_w_qkv[:, D : 2 * D],
            d_w_qkv[:, 2 * D :],
            d_w7,
            d_w8,
            d_w9,
        ]
    )
    latent_turned = lax.dynamic_update_slice_in_dim(
        jnp.zeros((D, latent_all.shape[0]), jnp.float32), d_latent_own.T, start, 1
    )
    d_small = jnp.concatenate(
        [jnp.stack([d_gain0, d_gain1, d_gain2, d_gain3, d_gain4]).reshape(-1), d_pix_gain, d_bias]
    )
    return ((d_square, d_kv_turned[None], d_head[None], latent_turned[None], d_small), loss)


def owner_layout(reduced):
    return (reduced[0], reduced[1][0].T, reduced[2][0], reduced[3][0].T)


def nesterov(weight, grad, mom, avg, rate):
    mom_new = MOMENTUM * mom + grad
    weight_new = weight - rate * (grad + MOMENTUM * mom_new)
    avg_new = AVERAGE_DECAY * avg + (1.0 - AVERAGE_DECAY) * weight_new
    return (grad, mom_new, weight_new, avg_new)


def per_device_rows(
    pixels,
    masks,
    valid,
    labels,
    square,
    kv_weight,
    head_weight,
    latents,
    small,
    square_mom,
    kv_mom,
    head_mom,
    latent_mom,
    small_mom,
    square_avg,
    kv_avg,
    head_avg,
    latent_avg,
    small_avg,
):
    gathered = (
        lax.all_gather(square.astype(jnp.bfloat16), ("dp", "head"), axis=1, tiled=True),
        lax.all_gather(kv_weight.astype(jnp.bfloat16), ("dp", "head"), axis=1, tiled=True),
        lax.all_gather(head_weight.astype(jnp.bfloat16), ("dp", "head"), axis=0, tiled=True),
        lax.all_gather(latents.astype(jnp.bfloat16), ("dp", "head"), axis=1, tiled=True),
    )
    full_square = gathered[0]
    w_qkv = jnp.concatenate([full_square[4], full_square[5], full_square[6]], axis=1)
    weights = (full_square, gathered[1], gathered[2], gathered[3], w_qkv)
    head_first = (lax.axis_index("head") == 0).astype(jnp.float32)
    valid_float = valid.astype(jnp.float32)
    early_count = lax.psum(jnp.sum(valid_float), "dp")
    loss_scale = 1.0 / jnp.maximum(early_count, 1.0)
    kv_shape = gathered[1].shape
    lat_shape = gathered[3].shape
    big_zero = (
        jnp.zeros(full_square.shape, jnp.float32),
        jnp.zeros((1, kv_shape[1], kv_shape[0]), jnp.float32),
        jnp.zeros((1,) + gathered[2].shape, jnp.float32),
        jnp.zeros((1, lat_shape[1], lat_shape[0]), jnp.float32),
    )

    def micro_step(carry, batch):
        big, small_acc, loss_acc = carry
        pix_micro, mask_micro, valid_micro, label_micro = batch
        grads, loss_part = image_grads(
            weights,
            small,
            pix_micro[0],
            mask_micro[0],
            valid_micro[0],
            label_micro[0],
            loss_scale,
            head_first,
        )
        reduced = (grads[0], grads[1], grads[2], grads[3])
        big = tuple((a + b for a, b in zip(big, reduced)))
        return ((big, small_acc + grads[4], loss_acc + loss_part), None)

    start_carry = (big_zero, jnp.zeros(small.shape, jnp.float32), jnp.float32(0.0))
    (big, small_acc, loss_acc), _ = lax.scan(
        micro_step, start_carry, (pixels, masks, valid_float, labels)
    )
    big = owner_layout(
        (
            lax.psum_scatter(big[0], ("dp", "head"), scatter_dimension=1, tiled=True),
            lax.psum_scatter(big[1], ("dp", "head"), scatter_dimension=1, tiled=True),
            lax.psum_scatter(big[2], ("dp", "head"), scatter_dimension=1, tiled=True),
            lax.psum_scatter(big[3], ("dp", "head"), scatter_dimension=1, tiled=True),
        )
    )
    small_total, loss_sum, count = lax.psum(
        (small_acc, loss_acc * head_first, jnp.sum(valid_float) * head_first), ("dp", "head")
    )
    count = jnp.maximum(count, 1.0)
    latent_rate = LATENTS * math.sqrt(D * MICRO * IMG_DEV * lax.axis_size("dp")) / 32.0
    rates = (LEARN_RATE, LEARN_RATE, LEARN_RATE, latent_rate, LEARN_RATE)
    results = [loss_sum, count]
    params = (square, kv_weight, head_weight, latents, small)
    moms = (square_mom, kv_mom, head_mom, latent_mom, small_mom)
    avgs = (square_avg, kv_avg, head_avg, latent_avg, small_avg)
    for weight, grad, mom, avg, rate in zip(params, tuple(big) + (small_total,), moms, avgs, rates):
        results.extend(nesterov(weight, grad, mom, avg, rate))
    return tuple(results)


MESH=pl.DeviceIdType.MESH
MB=1<<20
GAP=2

def where_am_i():
    dp=lax.axis_index("dp"); h=lax.axis_index("head")
    return dict(dp=dp,h=h,z=dp//2,y=dp%2,x=h//2,c=h%2)

def neighbours(me):
    return dict(zu=(me["dp"]+2,me["h"]),zd=(me["dp"]-2,me["h"]),y=(me["dp"]+1-2*me["y"],me["h"]),
                x=(me["dp"],me["h"]+2-4*me["x"]),c=(me["dp"],me["h"]+1-2*me["c"]))

def entry_barrier(me,nb,others=()):
    z=me["z"]
    bar=pltpu.get_barrier_semaphore()
    for k in ("x","y","c"):
        pl.semaphore_signal(bar,inc=1,device_id=nb[k],device_id_type=MESH)
    @pl.when(z<3)
    def _(): pl.semaphore_signal(bar,inc=1,device_id=nb["zu"],device_id_type=MESH)
    @pl.when(z>0)
    def _(): pl.semaphore_signal(bar,inc=1,device_id=nb["zd"],device_id_type=MESH)
    for other in others:
        pl.semaphore_signal(bar,inc=1,device_id=other,device_id_type=MESH)
    pl.semaphore_wait(bar,4+(z+1)//2%2+len(others))

class Gather:
    def __init__(self,me,nb,buf,groups,ssem,rsem):
        self.me,self.nb,self.buf,self.groups,self.ssem,self.rsem=me,nb,buf,groups,ssem,rsem
        self.pending=[]
    def copy(self,src,dst,slot,dev):
        return pltpu.make_async_remote_copy(src_ref=src,dst_ref=dst,send_sem=self.ssem.at[slot],recv_sem=self.rsem.at[slot],device_id=dev,device_id_type=MESH)
    def view(self,r,*ix):
        return self.buf.at[(*ix,slice(None),pl.ds(*self.groups[r]))]
    def hop(self,r,k,op):
        z,y,x,c=(self.me[i] for i in "zyxc")
        rest=(y,x,c) if r<2 else (slice(None),slice(None),c)
        su,sd=8*r+k-1,8*r+3+k-1
        if op=="start":
            @pl.when((z<3)&(z>=k-1))
            def _():
                v=self.view(r,z-(k-1),*rest); self.copy(v,v,su,self.nb["zu"]).start()
            @pl.when((z>0)&(z+k-1<=3))
            def _():
                v=self.view(r,z+(k-1),*rest); self.copy(v,v,sd,self.nb["zd"]).start()
        elif op=="recv":
            @pl.when(z>=k)
            def _():
                v=self.view(r,z-k,*rest); self.copy(v,v,su,self.nb["zd"]).wait_recv()
            @pl.when(z+k<=3)
            def _():
                v=self.view(r,z+k,*rest); self.copy(v,v,sd,self.nb["zu"]).wait_recv()
        else:
            @pl.when((z<3)&(z>=k-1))
            def _():
                v=self.view(r,z-(k-1),*rest); self.copy(v,v,su,self.nb["zu"]).wait_send()
            @pl.when((z>0)&(z+k-1<=3))
            def _():
                v=self.view(r,z+(k-1),*rest); self.copy(v,v,sd,self.nb["zd"]).wait_send()
    def flat(self,r,axis,op):
        z,y,x,c=(self.me[i] for i in "zyxc")
        A=slice(None)
        if axis=="y":
            mine={0:(A,y,x,c),1:(A,y,A,c),2:(z,y,A,c)}[r]; other={0:(A,1-y,x,c),1:(A,1-y,A,c),2:(z,1-y,A,c)}[r]; slot=8*r+6
        elif axis=="x":
            mine={0:(A,A,x,c),1:(A,y,x,c),2:(z,y,x,c)}[r]; other={0:(A,A,1-x,c),1:(A,y,1-x,c),2:(z,y,1-x,c)}[r]; slot=8*r+7
        if op=="start":
            v=self.view(r,*mine); self.copy(v,v,slot,self.nb[axis]).start()
        elif op=="recv":
            v=self.view(r,*other); self.copy(v,v,slot,self.nb[axis]).wait_recv()
        else:
            v=self.view(r,*mine); self.copy(v,v,slot,self.nb[axis]).wait_send()
    def core(self,op):
        c=self.me["c"]; A=slice(None)
        if op=="recv":
            v=self.buf.at[A,A,A,1-c]; self.copy(v,v,24,self.nb["c"]).wait_recv()
        else:
            v=self.buf.at[A,A,A,c]; d=self.copy(v,v,24,self.nb["c"])
            d.start() if op=="start" else d.wait_send()
    ORDER=[["h1","h2","h3","y","x"],["h1","h2","h3","x","y"],["x","y","h1","h2","h3"]]
    def do(self,r,p,op):
        n=self.ORDER[r][p]
        if n[0]=="h": self.hop(r,int(n[1]),op)
        else: self.flat(r,n,op)
    NPH=6
    def phase(self,p):
        if p>0 and p<=5:
            for r in range(3):
                if self.groups[r][1]: self.do(r,p-1,"recv")
                if p<5 and self.groups[r][1]: self.do(r,p,"start")
        if p==0:
            for r in range(3):
                if self.groups[r][1]: self.do(r,0,"start")
        if p==5: self.core("start")
        if p==6: self.core("recv")
    def sends(self):
        for r in range(3):
            if self.groups[r][1]:
                for p in range(5): self.do(r,p,"send")
        self.core("send")

SPLIT={1024:((0,384),(384,384),(768,256)),512:((0,128),(128,256),(384,128)),384:((0,128),(128,128),(256,128))}

def gather_kernel(nt,*refs):
    shards=refs[:nt]; bufs=refs[nt:2*nt]; lsem,ssem,rsem=refs[2*nt:]
    me=where_am_i(); nb=neighbours(me)
    z,y,x,c=(me[i] for i in "zyxc")
    local=[pltpu.make_async_copy(s,b.at[z,y,x,c],lsem.at[i]) for i,(s,b) in enumerate(zip(shards,bufs))]
    for l in local: l.start()
    entry_barrier(me,nb)
    gs=[Gather(me,nb,b,SPLIT[b.shape[-1]],ssem.at[i],rsem.at[i]) for i,b in enumerate(bufs)]
    for tick in range(nt+6*GAP):
        for t in range(nt):
            p=tick-t
            if p==0: local[t].wait()
            if p>=0 and p%GAP==0 and p//GAP<=6: gs[t].phase(p//GAP)
    for g in gs: g.sends()

def gather_all(shards,cid=0):
    nt=len(shards)
    outs=[jax.ShapeDtypeStruct((4,2,2,2)+s.shape,s.dtype) for s in shards]
    return pl.pallas_call(functools.partial(gather_kernel,nt),out_shape=outs,
        in_specs=[pl.BlockSpec(memory_space=pl.ANY)]*nt,out_specs=[pl.BlockSpec(memory_space=pl.ANY)]*nt,
        scratch_shapes=[pltpu.SemaphoreType.DMA((nt,)),pltpu.SemaphoreType.DMA((nt,25)),pltpu.SemaphoreType.DMA((nt,25))],
        compiler_params=pltpu.CompilerParams(collective_id=cid,has_side_effects=True,vmem_limit_bytes=60*MB))(*shards)


ALLS=slice(None)

def recv_shapes(r,n):
    (_,a),(_,b),(_,c)=SPLIT[n]
    return dict(core=(4,2,2,r,n),A0=(4,2,r,a),A1=(4,r,a),Ah=(6,r,a),B0=(4,2,r,b),B1=(4,r,b),Bh=(6,r,b),Ch=(6,2,2,r,c),C0=(2,r,c),C1=(r,c))
RNAMES=("core","A0","A1","Ah","B0","B1","Bh","Ch","C0","C1")

def add_into(dst,src,cols,lead):
    for di,si in lead:
        dst[(*di,ALLS,cols)]=dst[(*di,ALLS,cols)]+src[si]

class Scatter:
    def __init__(self,me,nb,part,send_half,bufs,out,groups,ssem,rsem):
        self.me,self.nb,self.part,self.half,self.b,self.out,self.groups,self.ssem,self.rsem=me,nb,part,send_half,bufs,out,groups,ssem,rsem
    def copy(self,src,dst,slot,dev):
        return pltpu.make_async_remote_copy(src_ref=src,dst_ref=dst,send_sem=self.ssem.at[slot],recv_sem=self.rsem.at[slot],device_id=dev,device_id_type=MESH)
    def cols(self,r): return pl.ds(*self.groups[r])
    def hop(self,r,k,op):
        z,y,x=(self.me[i] for i in "zyx")
        rest=(y,x) if r<2 else (ALLS,ALLS)
        buf=self.b["ABC"[r]+"h"]; cols=self.cols(r)
        su,sd=8*r+k-1,8*r+3+k-1
        up=lambda: self.copy(self.part.at[(z+k,*rest,ALLS,cols)],buf.at[k-1],su,self.nb["zu"])
        dn=lambda: self.copy(self.part.at[(z-k,*rest,ALLS,cols)],buf.at[3+k-1],sd,self.nb["zd"])
        if op in("start","send"):
            @pl.when(z+k<=3)
            def _():
                d=up(); d.start() if op=="start" else d.wait_send()
            @pl.when(z-k>=0)
            def _():
                d=dn(); d.start() if op=="start" else d.wait_send()
        else:
            last=(k==1 and r<2)
            @pl.when((z>=1)&(z-1+k<=3))
            def _():
                self.copy(buf.at[k-1],buf.at[k-1],su,self.nb["zd"]).wait_recv()
                self.hopadd(r,z-1+k,buf.at[k-1],cols)
            @pl.when((z<=2)&(z+1-k>=0))
            def _():
                self.copy(buf.at[3+k-1],buf.at[3+k-1],sd,self.nb["zu"]).wait_recv()
                self.hopadd(r,z+1-k,buf.at[3+k-1],cols)
    def hopadd(self,r,d,src,cols):
        y,x=self.me["y"],self.me["x"]
        if r<2: add_into(self.part,src,cols,[((d,y,x),(ALLS,ALLS))])
        else: add_into(self.part,src,cols,[((d,i,j),(i,j)) for i in range(2) for j in range(2)])
    def flat(self,r,axis,op):
        z,y,x=(self.me[i] for i in "zyx"); cols=self.cols(r)
        name="ABC"[r]
        if axis=="x":
            mine={0:(ALLS,ALLS,1-x),1:(ALLS,y,1-x),2:(z,y,1-x)}[r]; slot=8*r+7; buf=self.b[{0:"A0",1:"B1",2:"C1"}[r]]
        else:
            mine={0:(ALLS,1-y,x),1:(ALLS,1-y),2:(z,1-y)}[r]; slot=8*r+6; buf=self.b[{0:"A1",1:"B0",2:"C0"}[r]]
        if op=="recv":
            self.copy(buf,buf,slot,self.nb[axis]).wait_recv()
            if axis=="x":
                lead={0:[((i,j,x),(i,j)) for i in range(4) for j in range(2)],1:[((i,y,x),(i,)) for i in range(4)],2:[((z,y,x),(ALLS,ALLS))]}[r]
            else:
                lead={0:[((i,y,x),(i,)) for i in range(4)],1:[((i,y,j),(i,j)) for i in range(4) for j in range(2)],2:[((z,y,j),(j,)) for j in range(2)]}[r]
            add_into(self.part,buf,cols,lead)
        else:
            d=self.copy(self.part.at[(*mine,)+(ALLS,)*(4-len(mine))+(cols,)],buf,slot,self.nb[axis])
            d.start() if op=="start" else d.wait_send()
    def core(self,op):
        buf=self.b["core"]
        if op=="recv":
            self.copy(buf,buf,24,self.nb["c"]).wait_recv()
            @pl.loop(0,4)
            def _(i):
                for j in range(2):
                    for k in range(2):
                        self.part[i,j,k]=self.part[i,j,k]+buf[i,j,k]
        else:
            d=self.copy(self.half,buf,24,self.nb["c"]); d.start() if op=="start" else d.wait_send()
    ORDER=[["x","y","h3","h2","h1"],["y","x","h3","h2","h1"],["h3","h2","h1","y","x"]]
    def do(self,r,p,op):
        n=self.ORDER[r][p]
        if n[0]=="h": self.hop(r,int(n[1]),op)
        else: self.flat(r,n,op)
    def phase(self,p):
        if p==0: self.core("start"); return
        if p==1: self.core("recv")
        for r in range(3):
            if p>=2: self.do(r,p-2,"recv")
            if p<=5: self.do(r,p-1,"start")
        if p==6:
            z,y,x=(self.me[i] for i in "zyx")
            self.out[...]=self.part[z,y,x].astype(jnp.float32)
    def sends(self):
        self.core("send")
        for r in range(3):
            for p in range(5): self.do(r,p,"send")

def small_steps(me):
    dp,h=me["dp"],me["h"]
    z=me["z"]
    return [(dp,h+1-2*me["c"]),(dp,h+2-4*me["x"]),(dp+1-2*me["y"],h),(dp+2-4*(z%2),h),(dp+4-8*(z//2),h)]

def scatter_kernel(nt,gap,*refs):
    parts_in=refs[:nt]; vec,small=refs[nt:nt+2]
    outs=refs[nt+2:2*nt+2]; vec_out,small_out=refs[2*nt+2:2*nt+4]
    rest=list(refs[2*nt+4:])
    part=[rest.pop(0) for _ in range(nt)]
    bufs=[{k:rest.pop(0) for k in RNAMES} for _ in range(nt)]
    vbuf,srecv,ssend,lsem,ssem,rsem,vs,vr,sms,smr=rest
    me=where_am_i(); nb=neighbours(me)
    z,y,x,c=(me[i] for i in "zyxc")
    local=[pltpu.make_async_copy(d.at[:,:,:,c],p,lsem.at[i]) for i,(d,p) in enumerate(zip(parts_in,part))]
    for l in local: l.start()
    vbuf[z,y,x,c]=vec[...]
    entry_barrier(me,nb,small_steps(me)[4:])
    gs=[Scatter(me,nb,part[i],parts_in[i].at[:,:,:,1-c],bufs[i],outs[i],SPLIT[part[i].shape[-1]],ssem.at[i],rsem.at[i]) for i in range(nt)]
    gv=Gather(me,nb,vbuf,[(0,0),(0,0),(0,vbuf.shape[-1])],vs,vr)
    acc=small[...]
    sm=[]
    for i,p in enumerate(small_steps(me)):
        sm.append(pltpu.make_async_remote_copy(src_ref=ssend.at[i],dst_ref=srecv.at[i],send_sem=sms.at[i],recv_sem=smr.at[i],device_id=p,device_id_type=MESH))
    ssend[0]=small[...]
    for tick in range(nt+6*gap):
        if tick%2==0 and tick//2<=5:
            i=tick//2
            if i>0:
                sm[i-1].wait_recv()
                s=ssend[i-1]+srecv[i-1]
                if i<5: ssend[i]=s
                else: small_out[...]=s
            if i<5: sm[i].start()
        if tick%gap==0 and tick//gap<=6: gv.phase(tick//gap)
        for t in range(nt):
            p=tick-t
            if p==0: local[t].wait()
            if p>=0 and p%gap==0 and p//gap<=6: gs[t].phase(p//gap)
    for s in sm: s.wait_send()
    gv.sends()
    vec_out[...]=vbuf[...]
    for g in gs: g.sends()

def scatter_all(parts,vec,small,cid=1,gap=2):
    nt=len(parts)
    outs=[jax.ShapeDtypeStruct(p.shape[-2:],jnp.float32) for p in parts]+[jax.ShapeDtypeStruct((4,2,2,2)+vec.shape,vec.dtype),jax.ShapeDtypeStruct(small.shape,small.dtype)]
    V=pl.BlockSpec(memory_space=pltpu.VMEM)
    D=pltpu.SemaphoreType.DMA
    scr=[pltpu.VMEM((4,2,2)+p.shape[-2:],jnp.bfloat16) for p in parts]
    for p in parts:
        sh=recv_shapes(*p.shape[-2:])
        scr+=[pltpu.VMEM(sh[k],jnp.bfloat16) for k in RNAMES]
    scr+=[pltpu.VMEM((4,2,2,2)+vec.shape,vec.dtype),pltpu.VMEM((5,)+small.shape,small.dtype),pltpu.VMEM((5,)+small.shape,small.dtype),
          D((nt,)),D((nt,25)),D((nt,25)),D((25,)),D((25,)),D((5,)),D((5,))]
    return pl.pallas_call(functools.partial(scatter_kernel,nt,gap),out_shape=outs,
        in_specs=[pl.BlockSpec(memory_space=pl.ANY)]*nt+[V,V],out_specs=[V]*(nt+2),scratch_shapes=scr,
        compiler_params=pltpu.CompilerParams(collective_id=cid,has_side_effects=True,vmem_limit_bytes=62*MB))(*parts,vec,small)


def image_forward_back(weights, small, pixels, mask_row, valid_one, label):
    square, kv_weight, head_weight, latent_all = weights
    gains = small[: 5 * D].reshape(5, D)
    pix_gain = small[5 * D : 5 * D + CIN]
    bias = small[5 * D + CIN :]
    rows = latent_all.shape[0]
    latent = latent_all.astype(jnp.float32)
    valid_keys = mask_row > 0
    pix_float = pixels.astype(jnp.float32)
    normed_pix = layer_norm(pix_float, pix_gain).astype(jnp.bfloat16)
    normed_pix = jnp.pad(normed_pix, ((0, 0), (0, kv_weight.shape[1] - CIN)))
    kv = dot_nt(normed_pix, kv_weight).astype(jnp.bfloat16)
    keys_px = kv[:, :D].reshape(-1, 1, D)
    values_px = kv[:, D:].reshape(-1, 1, D)
    query_norm = layer_norm(latent, gains[0]).astype(jnp.bfloat16)
    query = dot_nn(query_norm, square[0]).astype(jnp.bfloat16).reshape(rows, 1, D)
    cross_out, cross_total = attend(query, keys_px, values_px, valid_keys)
    cross_out = cross_out.reshape(rows, D)
    hidden1 = latent + dot_nn(cross_out, square[1])
    hidden2, mlp_first = mlp_forward(hidden1, gains[1], square[2], square[3])
    self_norm = layer_norm(hidden2, gains[2]).astype(jnp.bfloat16)
    qkv = [dot_nn(self_norm, square[i]).astype(jnp.bfloat16).reshape(rows, HEADS, HEAD_DIM) for i in (4, 5, 6)]
    self_out, self_total = attend(qkv[0], qkv[1], qkv[2], None)
    self_out = self_out.reshape(rows, D)
    hidden3 = hidden2 + dot_nn(self_out, square[7])
    hidden4, mlp_second = mlp_forward(hidden3, gains[3], square[8], square[9])
    final = layer_norm(hidden4, gains[4])
    pooled_b = (jnp.sum(final, axis=0) / rows).astype(jnp.bfloat16)
    logits = dot_nn(pooled_b[None, :], head_weight)[0, : bias.shape[0]] + bias
    logp = jax.nn.log_softmax(logits)
    picked = jnp.arange(logits.shape[0]) == label
    loss = -valid_one * (
        (1.0 - SMOOTH) * jnp.sum(jnp.where(picked, logp, 0.0)) + SMOOTH * jnp.mean(logp)
    )
    target = (1.0 - SMOOTH) * picked.astype(jnp.float32) + SMOOTH / logits.shape[0]
    d_logits = valid_one * (jnp.exp(logp) - target)
    d_pooled = jnp.dot(head_weight[:, : bias.shape[0]].astype(jnp.float32), d_logits)
    d_final = jnp.broadcast_to(d_pooled / rows, final.shape)
    d_hidden4, d_gain4 = jax.vjp(layer_norm, hidden4, gains[4])[1](d_final)
    d_hidden3, d_gain3, d_w8, d_w9 = mlp_backward(
        hidden3, gains[3], square[8], square[9], mlp_second, d_hidden4
    )
    d_hidden3_b = d_hidden3.astype(jnp.bfloat16)
    d_w7 = dot_tn(self_out, d_hidden3_b)
    d_self_out = dot_nt(d_hidden3_b, square[7]).astype(jnp.bfloat16).reshape(rows, HEADS, HEAD_DIM)
    d_parts = attend_back(qkv[0], qkv[1], qkv[2], self_total, d_self_out, None)
    d_parts = [d.reshape(rows, D).astype(jnp.bfloat16) for d in d_parts]
    d_w456 = [dot_tn(self_norm, d) for d in d_parts]
    d_self_norm = sum(dot_nt(d, square[4 + i]) for i, d in enumerate(d_parts))
    d_hidden2_norm, d_gain2 = jax.vjp(layer_norm, hidden2, gains[2])[1](d_self_norm)
    d_hidden2 = d_hidden3 + d_hidden2_norm
    d_hidden1, d_gain1, d_w2, d_w3 = mlp_backward(
        hidden1, gains[1], square[2], square[3], mlp_first, d_hidden2
    )
    d_hidden1_b = d_hidden1.astype(jnp.bfloat16)
    d_w1 = dot_tn(cross_out, d_hidden1_b)
    d_cross = dot_nt(d_hidden1_b, square[1]).astype(jnp.bfloat16).reshape(rows, 1, D)
    d_query, d_keys, d_values = attend_back(
        query, keys_px, values_px, cross_total, d_cross, valid_keys
    )
    d_kv_px = jnp.concatenate([d_keys.reshape(-1, D), d_values.reshape(-1, D)], axis=1).astype(jnp.bfloat16)
    d_kv_turned = dot_tn(d_kv_px, normed_pix)
    d_normed_pix = dot_nn(d_kv_px, kv_weight)[:, :CIN]
    d_pix_gain = jax.vjp(layer_norm, pix_float, pix_gain)[1](d_normed_pix)[1]
    d_query_b = d_query.reshape(rows, D).astype(jnp.bfloat16)
    d_w0 = dot_tn(query_norm, d_query_b)
    d_query_norm = dot_nt(d_query_b, square[0])
    d_latent_norm, d_gain0 = jax.vjp(layer_norm, latent, gains[0])[1](d_query_norm)
    d_latent = d_hidden1 + d_latent_norm
    d_square = [d_w0, d_w1, d_w2, d_w3] + d_w456 + [d_w7, d_w8, d_w9]
    d_small = jnp.concatenate(
        [d_gain0, d_gain1, d_gain2, d_gain3, d_gain4, d_pix_gain, d_logits]
    )
    return d_square, d_kv_turned, d_latent.T, d_small, pooled_b, d_logits, loss


def per_device_images(
    pixels,
    masks,
    valid,
    labels,
    square,
    kv_weight,
    head_weight,
    latents,
    small,
    square_mom,
    kv_mom,
    head_mom,
    latent_mom,
    small_mom,
    square_avg,
    kv_avg,
    head_avg,
    latent_avg,
    small_avg,
):
    bf = jnp.bfloat16
    micro = lax.axis_index("head")
    pick = lambda a: lax.dynamic_index_in_dim(a, micro, 0, keepdims=False)[0]
    image = lax.all_to_all(pixels[:, 0], "head", split_axis=0, concat_axis=1, tiled=True)[0]
    classes = head_weight.shape[1]
    shards = [latents.astype(bf).T, jnp.pad(kv_weight.astype(bf).T, ((0, 0), (0, 384 - CIN)))]
    shards += [square[i].astype(bf) for i in range(10)]
    shards += [jnp.pad(head_weight.astype(bf), ((0, 0), (0, D - classes)))]
    whole = [w.reshape(-1, w.shape[-1]) for w in gather_all(shards)]
    d_square, d_kv, d_lat, d_small, pooled_b, d_logits, loss = image_forward_back(
        (whole[2:12], whole[1], whole[12], whole[0].T), small, image,
        pick(masks), pick(valid.astype(jnp.float32)), pick(labels),
    )
    parts = [d.astype(bf).reshape((4, 2, 2, 2, -1, d.shape[-1])) for d in d_square + [d_kv, d_lat]]
    pad = lambda v, n: jnp.pad(v, (0, n - v.shape[0]))
    vec = jnp.concatenate([pooled_b.astype(jnp.float32), pad(d_logits, D)]).reshape(8, 256)
    counted = jnp.stack([loss, pick(valid.astype(jnp.float32))])
    packed = pad(jnp.concatenate([d_small, counted]), 56 * 128).reshape(56, 128)
    *own, vec_all, packed = scatter_all(parts, vec, packed)
    packed = packed.reshape(-1)
    small_total, loss_sum, count = packed[: small.shape[0]], packed[small.shape[0]], packed[small.shape[0] + 1]
    count = jnp.maximum(count, 1.0)
    vec_all = vec_all.reshape(-1, 2 * D)
    rows = head_weight.shape[0]
    first = (lax.axis_index("dp") * lax.axis_size("head") + micro) * rows
    pooled_own = lax.dynamic_slice_in_dim(vec_all, first, rows, 1)
    d_head = lax.dot_general(
        pooled_own, vec_all[:, D : D + classes], (((0,), (0,)), ((), ())), precision=lax.Precision.HIGHEST
    )
    grads = (jnp.stack(own[:10]), own[10][:, :CIN].T, d_head, own[11].T, small_total)
    latent_rate = LATENTS * math.sqrt(D * MICRO * IMG_DEV * lax.axis_size("dp")) / 32.0
    rates = (LEARN_RATE, LEARN_RATE, LEARN_RATE, latent_rate, LEARN_RATE)
    results = [loss_sum, count]
    params = (square, kv_weight, head_weight, latents, small)
    moms = (square_mom, kv_mom, head_mom, latent_mom, small_mom)
    avgs = (square_avg, kv_avg, head_avg, latent_avg, small_avg)
    for weight, grad, mom, avg, rate in zip(params, grads, moms, avgs, rates):
        results.extend(nesterov(weight, grad / count, mom, avg, rate))
    return tuple(results)


def solution(mesh):
    in_specs = (
        P(None, "dp", "head", None),
        P(None, "dp", None),
        P(None, "dp"),
        P(None, "dp"),
        P(None, ("dp", "head"), None),
        P(None, ("dp", "head")),
        P(("dp", "head"), None),
        P(None, ("dp", "head")),
        P(),
        P(None, ("dp", "head"), None),
        P(None, ("dp", "head")),
        P(("dp", "head"), None),
        P(None, ("dp", "head")),
        P(),
        P(None, ("dp", "head"), None),
        P(None, ("dp", "head")),
        P(("dp", "head"), None),
        P(None, ("dp", "head")),
        P(),
    )
    out_specs = (
        P(),
        P(),
        P(None, ("dp", "head"), None),
        P(None, ("dp", "head"), None),
        P(None, ("dp", "head"), None),
        P(None, ("dp", "head"), None),
        P(None, ("dp", "head")),
        P(None, ("dp", "head")),
        P(None, ("dp", "head")),
        P(None, ("dp", "head")),
        P(("dp", "head"), None),
        P(("dp", "head"), None),
        P(("dp", "head"), None),
        P(("dp", "head"), None),
        P(None, ("dp", "head")),
        P(None, ("dp", "head")),
        P(None, ("dp", "head")),
        P(None, ("dp", "head")),
        P(),
        P(),
        P(),
        P(),
    )
    whole_images = dict(mesh.shape) == {"dp": 8, "head": MICRO}
    per_device = per_device_images if whole_images else per_device_rows
    return jax.shard_map(
        per_device, mesh=mesh, in_specs=in_specs, out_specs=out_specs, check_vma=False
    )
```

```python
import functools
import math

import jax
import jax.numpy as jnp
from jax import lax
from jax.experimental import pallas as pl
from jax.experimental.pallas import tpu as pltpu
from jax.sharding import PartitionSpec as P

D = 1024
CIN = 261
LATENTS = 512
HEADS = 8
HEAD_DIM = 128
MICRO = 4
IMG_DEV = 1


EPS = 1e-05
NEG_BIG = -1e30
SMOOTH = 0.1
LEARN_RATE = 20.0
MOMENTUM = 0.9
AVERAGE_DECAY = 0.6


def layer_norm(v, gain):
    mean = jnp.mean(v, axis=-1, keepdims=True)
    cent = v - mean
    var = jnp.mean(cent * cent, axis=-1, keepdims=True)
    return cent * lax.rsqrt(var + EPS) * gain


def dot_nn(left, right):
    return jnp.dot(left, right, preferred_element_type=jnp.float32)


def dot_tn(left, right):
    return lax.dot_general(
        left, right, (((0,), (0,)), ((), ())), preferred_element_type=jnp.float32
    )


def dot_nt(left, right):
    return lax.dot_general(
        left, right, (((1,), (1,)), ((), ())), preferred_element_type=jnp.float32
    )


def scores_of(query, keys, valid_keys):
    scores = jnp.einsum("qhd,khd->hqk", query, keys, preferred_element_type=jnp.float32)
    scores = scores * query.shape[-1] ** (-0.5)
    if valid_keys is not None:
        scores = jnp.where(valid_keys[None, None, :], scores, NEG_BIG)
    return scores


def attend(query, keys, values, valid_keys):
    scores = scores_of(query, keys, valid_keys)
    log_total = jax.nn.logsumexp(scores, axis=-1, keepdims=True)
    probs = jnp.exp(scores - log_total).astype(jnp.bfloat16)
    out = jnp.einsum("hqk,khd->qhd", probs, values, preferred_element_type=jnp.float32)
    return (out.astype(jnp.bfloat16), log_total)


def attend_back(query, keys, values, log_total, d_out, valid_keys):
    scale = query.shape[-1] ** (-0.5)
    probs = jnp.exp(scores_of(query, keys, valid_keys) - log_total)
    probs_b = probs.astype(jnp.bfloat16)
    d_probs = jnp.einsum("qhd,khd->hqk", d_out, values, preferred_element_type=jnp.float32)
    d_scores = probs * (d_probs - jnp.sum(probs * d_probs, axis=-1, keepdims=True))
    d_scores = d_scores.astype(jnp.bfloat16)
    d_query = jnp.einsum("hqk,khd->qhd", d_scores, keys, preferred_element_type=jnp.float32) * scale
    d_keys = jnp.einsum("hqk,qhd->khd", d_scores, query, preferred_element_type=jnp.float32) * scale
    d_values = jnp.einsum("hqk,qhd->khd", probs_b, d_out, preferred_element_type=jnp.float32)
    return (d_query, d_keys, d_values)


def mlp_forward(hidden, gain, w_in, w_out):
    normed = layer_norm(hidden, gain).astype(jnp.bfloat16)
    pre = dot_nn(normed, w_in)
    active = jax.nn.gelu(pre).astype(jnp.bfloat16)
    return (hidden + dot_nn(active, w_out), (normed, pre, active))


def mlp_backward(hidden, gain, w_in, w_out, saved, d_next):
    normed, pre, active = saved
    d_next_b = d_next.astype(jnp.bfloat16)
    d_w_out = dot_tn(active, d_next_b)
    d_active = dot_nt(d_next_b, w_out)
    d_pre = jax.vjp(jax.nn.gelu, pre)[1](d_active)[0].astype(jnp.bfloat16)
    d_w_in = dot_tn(normed, d_pre)
    d_normed = dot_nt(d_pre, w_in)
    d_hidden, d_gain = jax.vjp(layer_norm, hidden, gain)[1](d_normed)
    return (d_next + d_hidden, d_gain, d_w_in, d_w_out)


def image_grads(weights, small, pixel_own, mask_row, valid_one, label, loss_scale, head_first):
    square, kv_weight, head_weight, latent_all, w_qkv = weights
    gains = small[: 5 * D].reshape(5, D)
    pix_gain = small[5 * D : 5 * D + CIN]
    bias = small[5 * D + CIN :]
    rows = latent_all.shape[0] // lax.axis_size("head")
    start = lax.axis_index("head") * rows
    latent_own = lax.dynamic_slice_in_dim(latent_all, start, rows, 0).astype(jnp.float32)
    valid_keys = mask_row > 0
    pix_float = pixel_own.astype(jnp.float32)
    normed_pix = layer_norm(pix_float, pix_gain).astype(jnp.bfloat16)
    kv_own = dot_nn(normed_pix, kv_weight).astype(jnp.bfloat16)
    kv_all = lax.all_gather(kv_own, "head", axis=0, tiled=True)
    keys_px = kv_all[:, :D].reshape(-1, 1, D)
    values_px = kv_all[:, D:].reshape(-1, 1, D)
    query_norm = layer_norm(latent_own, gains[0]).astype(jnp.bfloat16)
    query = dot_nn(query_norm, square[0]).astype(jnp.bfloat16).reshape(rows, 1, D)
    cross_out, cross_total = attend(query, keys_px, values_px, valid_keys)
    cross_out = cross_out.reshape(rows, D)
    hidden1 = latent_own + dot_nn(cross_out, square[1])
    hidden2, mlp_first = mlp_forward(hidden1, gains[1], square[2], square[3])
    self_norm = layer_norm(hidden2, gains[2]).astype(jnp.bfloat16)
    qkv = dot_nn(self_norm, w_qkv).astype(jnp.bfloat16)
    kv_latent = lax.all_gather(qkv[:, D:], "head", axis=0, tiled=True)
    self_query = qkv[:, :D].reshape(rows, HEADS, HEAD_DIM)
    self_keys = kv_latent[:, :D].reshape(-1, HEADS, HEAD_DIM)
    self_values = kv_latent[:, D:].reshape(-1, HEADS, HEAD_DIM)
    self_out, self_total = attend(self_query, self_keys, self_values, None)
    self_out = self_out.reshape(rows, D)
    hidden3 = hidden2 + dot_nn(self_out, square[7])
    hidden4, mlp_second = mlp_forward(hidden3, gains[3], square[8], square[9])
    final = layer_norm(hidden4, gains[4])
    pooled = lax.psum(jnp.sum(final, axis=0), "head") / latent_all.shape[0]
    pooled_b = pooled.astype(jnp.bfloat16)
    logits = dot_nn(pooled_b[None, :], head_weight)[0] + bias
    logp = jax.nn.log_softmax(logits)
    picked = jnp.arange(logits.shape[0]) == label
    loss = -valid_one * (
        (1.0 - SMOOTH) * jnp.sum(jnp.where(picked, logp, 0.0)) + SMOOTH * jnp.mean(logp)
    )
    target = (1.0 - SMOOTH) * picked.astype(jnp.float32) + SMOOTH / logits.shape[0]
    d_logits = valid_one * loss_scale * (jnp.exp(logp) - target)
    d_bias = d_logits * head_first
    d_head = pooled_b.astype(jnp.float32)[:, None] * d_logits[None, :] * head_first
    d_pooled = jnp.dot(head_weight.astype(jnp.float32), d_logits)
    d_final = jnp.broadcast_to(d_pooled / latent_all.shape[0], final.shape)
    d_hidden4, d_gain4 = jax.vjp(layer_norm, hidden4, gains[4])[1](d_final)
    d_hidden3, d_gain3, d_w8, d_w9 = mlp_backward(
        hidden3, gains[3], square[8], square[9], mlp_second, d_hidden4
    )
    d_hidden3_b = d_hidden3.astype(jnp.bfloat16)
    d_w7 = dot_tn(self_out, d_hidden3_b)
    d_self_out = dot_nt(d_hidden3_b, square[7]).astype(jnp.bfloat16).reshape(rows, HEADS, HEAD_DIM)
    d_query, d_keys, d_values = attend_back(
        self_query, self_keys, self_values, self_total, d_self_out, None
    )
    d_kv_terms = jnp.concatenate([d_keys.reshape(-1, D), d_values.reshape(-1, D)], axis=1)
    d_kv_own = lax.psum_scatter(
        d_kv_terms.astype(jnp.bfloat16), "head", scatter_dimension=0, tiled=True
    ).astype(jnp.float32)
    d_qkv = jnp.concatenate([d_query.reshape(rows, D), d_kv_own], axis=1).astype(jnp.bfloat16)
    d_w_qkv = dot_tn(self_norm, d_qkv)
    d_self_norm = dot_nt(d_qkv, w_qkv)
    d_hidden2_norm, d_gain2 = jax.vjp(layer_norm, hidden2, gains[2])[1](d_self_norm)
    d_hidden2 = d_hidden3 + d_hidden2_norm
    d_hidden1, d_gain1, d_w2, d_w3 = mlp_backward(
        hidden1, gains[1], square[2], square[3], mlp_first, d_hidden2
    )
    d_hidden1_b = d_hidden1.astype(jnp.bfloat16)
    d_w1 = dot_tn(cross_out, d_hidden1_b)
    d_cross = dot_nt(d_hidden1_b, square[1]).astype(jnp.bfloat16).reshape(rows, 1, D)
    d_query, d_keys, d_values = attend_back(
        query, keys_px, values_px, cross_total, d_cross, valid_keys
    )
    d_px_terms = jnp.concatenate([d_keys.reshape(-1, D), d_values.reshape(-1, D)], axis=1)
    d_kv_px = lax.psum_scatter(
        d_px_terms.astype(jnp.bfloat16), "head", scatter_dimension=0, tiled=True
    )
    d_kv_turned = dot_tn(d_kv_px, normed_pix)
    d_normed_pix = dot_nt(d_kv_px, kv_weight)
    d_pix_gain = jax.vjp(layer_norm, pix_float, pix_gain)[1](d_normed_pix)[1]
    d_query_b = d_query.reshape(rows, D).astype(jnp.bfloat16)
    d_w0 = dot_tn(query_norm, d_query_b)
    d_query_norm = dot_nt(d_query_b, square[0])
    d_latent_norm, d_gain0 = jax.vjp(layer_norm, latent_own, gains[0])[1](d_query_norm)
    d_latent_own = d_hidden1 + d_latent_norm
    d_square = jnp.stack(
        [
            d_w0,
            d_w1,
            d_w2,
            d_w3,
            d_w_qkv[:, :D],
            d_w_qkv[:, D : 2 * D],
            d_w_qkv[:, 2 * D :],
            d_w7,
            d_w8,
            d_w9,
        ]
    )
    latent_turned = lax.dynamic_update_slice_in_dim(
        jnp.zeros((D, latent_all.shape[0]), jnp.float32), d_latent_own.T, start, 1
    )
    d_small = jnp.concatenate(
        [jnp.stack([d_gain0, d_gain1, d_gain2, d_gain3, d_gain4]).reshape(-1), d_pix_gain, d_bias]
    )
    return ((d_square, d_kv_turned[None], d_head[None], latent_turned[None], d_small), loss)


def owner_layout(reduced):
    return (reduced[0], reduced[1][0].T, reduced[2][0], reduced[3][0].T)


def nesterov(weight, grad, mom, avg, rate):
    mom_new = MOMENTUM * mom + grad
    weight_new = weight - rate * (grad + MOMENTUM * mom_new)
    avg_new = AVERAGE_DECAY * avg + (1.0 - AVERAGE_DECAY) * weight_new
    return (grad, mom_new, weight_new, avg_new)


def per_device_rows(
    pixels,
    masks,
    valid,
    labels,
    square,
    kv_weight,
    head_weight,
    latents,
    small,
    square_mom,
    kv_mom,
    head_mom,
    latent_mom,
    small_mom,
    square_avg,
    kv_avg,
    head_avg,
    latent_avg,
    small_avg,
):
    gathered = (
        lax.all_gather(square.astype(jnp.bfloat16), ("dp", "head"), axis=1, tiled=True),
        lax.all_gather(kv_weight.astype(jnp.bfloat16), ("dp", "head"), axis=1, tiled=True),
        lax.all_gather(head_weight.astype(jnp.bfloat16), ("dp", "head"), axis=0, tiled=True),
        lax.all_gather(latents.astype(jnp.bfloat16), ("dp", "head"), axis=1, tiled=True),
    )
    full_square = gathered[0]
    w_qkv = jnp.concatenate([full_square[4], full_square[5], full_square[6]], axis=1)
    weights = (full_square, gathered[1], gathered[2], gathered[3], w_qkv)
    head_first = (lax.axis_index("head") == 0).astype(jnp.float32)
    valid_float = valid.astype(jnp.float32)
    early_count = lax.psum(jnp.sum(valid_float), "dp")
    loss_scale = 1.0 / jnp.maximum(early_count, 1.0)
    kv_shape = gathered[1].shape
    lat_shape = gathered[3].shape
    big_zero = (
        jnp.zeros(full_square.shape, jnp.float32),
        jnp.zeros((1, kv_shape[1], kv_shape[0]), jnp.float32),
        jnp.zeros((1,) + gathered[2].shape, jnp.float32),
        jnp.zeros((1, lat_shape[1], lat_shape[0]), jnp.float32),
    )

    def micro_step(carry, batch):
        big, small_acc, loss_acc = carry
        pix_micro, mask_micro, valid_micro, label_micro = batch
        grads, loss_part = image_grads(
            weights,
            small,
            pix_micro[0],
            mask_micro[0],
            valid_micro[0],
            label_micro[0],
            loss_scale,
            head_first,
        )
        reduced = (grads[0], grads[1], grads[2], grads[3])
        big = tuple((a + b for a, b in zip(big, reduced)))
        return ((big, small_acc + grads[4], loss_acc + loss_part), None)

    start_carry = (big_zero, jnp.zeros(small.shape, jnp.float32), jnp.float32(0.0))
    (big, small_acc, loss_acc), _ = lax.scan(
        micro_step, start_carry, (pixels, masks, valid_float, labels)
    )
    big = owner_layout(
        (
            lax.psum_scatter(big[0], ("dp", "head"), scatter_dimension=1, tiled=True),
            lax.psum_scatter(big[1], ("dp", "head"), scatter_dimension=1, tiled=True),
            lax.psum_scatter(big[2], ("dp", "head"), scatter_dimension=1, tiled=True),
            lax.psum_scatter(big[3], ("dp", "head"), scatter_dimension=1, tiled=True),
        )
    )
    small_total, loss_sum, count = lax.psum(
        (small_acc, loss_acc * head_first, jnp.sum(valid_float) * head_first), ("dp", "head")
    )
    count = jnp.maximum(count, 1.0)
    latent_rate = LATENTS * math.sqrt(D * MICRO * IMG_DEV * lax.axis_size("dp")) / 32.0
    rates = (LEARN_RATE, LEARN_RATE, LEARN_RATE, latent_rate, LEARN_RATE)
    results = [loss_sum, count]
    params = (square, kv_weight, head_weight, latents, small)
    moms = (square_mom, kv_mom, head_mom, latent_mom, small_mom)
    avgs = (square_avg, kv_avg, head_avg, latent_avg, small_avg)
    for weight, grad, mom, avg, rate in zip(params, tuple(big) + (small_total,), moms, avgs, rates):
        results.extend(nesterov(weight, grad, mom, avg, rate))
    return tuple(results)


class Names:
    def __getattr__(self, name):
        return name


N = Names()


MESH=pl.DeviceIdType.MESH
MB=1<<20

def where_am_i():
    dp=lax.axis_index(N.dp); h=lax.axis_index(N.head)
    return dict(dp=dp,h=h,z=dp//2,y=dp%2,x=h//2,c=h%2)

def neighbours(me):
    return dict(zu=(me[N.dp]+2,me[N.h]),zd=(me[N.dp]-2,me[N.h]),y=(me[N.dp]+1-2*me[N.y],me[N.h]),
                x=(me[N.dp],me[N.h]+2-4*me[N.x]),c=(me[N.dp],me[N.h]+1-2*me[N.c]))

def entry_barrier(me,nb,others=()):
    z=me[N.z]
    bar=pltpu.get_barrier_semaphore()
    for k in (N.x,N.y,N.c):
        pl.semaphore_signal(bar,inc=1,device_id=nb[k],device_id_type=MESH)
    @pl.when(z<3)
    def _(): pl.semaphore_signal(bar,inc=1,device_id=nb[N.zu],device_id_type=MESH)
    @pl.when(z>0)
    def _(): pl.semaphore_signal(bar,inc=1,device_id=nb[N.zd],device_id_type=MESH)
    for other in others:
        pl.semaphore_signal(bar,inc=1,device_id=other,device_id_type=MESH)
    pl.semaphore_wait(bar,4+(z+1)//2%2+len(others))

class Gather:
    def __init__(self,me,nb,buf,groups,ssem,rsem):
        self.me,self.nb,self.buf,self.groups,self.ssem,self.rsem=me,nb,buf,groups,ssem,rsem
        self.pending=[]
    def copy(self,src,dst,slot,dev):
        return pltpu.make_async_remote_copy(src_ref=src,dst_ref=dst,send_sem=self.ssem.at[slot],recv_sem=self.rsem.at[slot],device_id=dev,device_id_type=MESH)
    def view(self,r,*ix):
        return self.buf.at[(*ix,slice(None),pl.ds(*self.groups[r]))]
    def hop(self,r,k,op):
        z,y,x,c=(self.me[i] for i in N.zyxc)
        rest=(y,x,c) if r<2 else (slice(None),slice(None),c)
        su,sd=8*r+k-1,8*r+3+k-1
        if op==N.start:
            @pl.when((z<3)&(z>=k-1))
            def _():
                v=self.view(r,z-(k-1),*rest); self.copy(v,v,su,self.nb[N.zu]).start()
            @pl.when((z>0)&(z+k-1<=3))
            def _():
                v=self.view(r,z+(k-1),*rest); self.copy(v,v,sd,self.nb[N.zd]).start()
        elif op==N.recv:
            @pl.when(z>=k)
            def _():
                v=self.view(r,z-k,*rest); self.copy(v,v,su,self.nb[N.zd]).wait_recv()
            @pl.when(z+k<=3)
            def _():
                v=self.view(r,z+k,*rest); self.copy(v,v,sd,self.nb[N.zu]).wait_recv()
        else:
            @pl.when((z<3)&(z>=k-1))
            def _():
                v=self.view(r,z-(k-1),*rest); self.copy(v,v,su,self.nb[N.zu]).wait_send()
            @pl.when((z>0)&(z+k-1<=3))
            def _():
                v=self.view(r,z+(k-1),*rest); self.copy(v,v,sd,self.nb[N.zd]).wait_send()
    def flat(self,r,axis,op):
        z,y,x,c=(self.me[i] for i in N.zyxc)
        A=slice(None)
        if axis==N.y:
            mine={0:(A,y,x,c),1:(A,y,A,c),2:(z,y,A,c)}[r]; other={0:(A,1-y,x,c),1:(A,1-y,A,c),2:(z,1-y,A,c)}[r]; slot=8*r+6
        elif axis==N.x:
            mine={0:(A,A,x,c),1:(A,y,x,c),2:(z,y,x,c)}[r]; other={0:(A,A,1-x,c),1:(A,y,1-x,c),2:(z,y,1-x,c)}[r]; slot=8*r+7
        if op==N.start:
            v=self.view(r,*mine); self.copy(v,v,slot,self.nb[axis]).start()
        elif op==N.recv:
            v=self.view(r,*other); self.copy(v,v,slot,self.nb[axis]).wait_recv()
        else:
            v=self.view(r,*mine); self.copy(v,v,slot,self.nb[axis]).wait_send()
    def core(self,op):
        c=self.me[N.c]; A=slice(None)
        if op==N.recv:
            v=self.buf.at[A,A,A,1-c]; self.copy(v,v,24,self.nb[N.c]).wait_recv()
        else:
            v=self.buf.at[A,A,A,c]; d=self.copy(v,v,24,self.nb[N.c])
            d.start() if op==N.start else d.wait_send()
    ORDER=[[N.h1,N.h2,N.h3,N.y,N.x],[N.h1,N.h2,N.h3,N.x,N.y],[N.x,N.y,N.h1,N.h2,N.h3]]
    def do(self,r,p,op):
        n=self.ORDER[r][p]
        if n[0]==N.h: self.hop(r,int(n[1]),op)
        else: self.flat(r,n,op)
    NPH=6
    def phase(self,p):
        if p>0 and p<=5:
            for r in range(3):
                if self.groups[r][1]: self.do(r,p-1,N.recv)
                if p<5 and self.groups[r][1]: self.do(r,p,N.start)
        if p==0:
            for r in range(3):
                if self.groups[r][1]: self.do(r,0,N.start)
        if p==5: self.core(N.start)
        if p==6: self.core(N.recv)
    def sends(self):
        for r in range(3):
            if self.groups[r][1]:
                for p in range(5): self.do(r,p,N.send)
        self.core(N.send)

SPLIT={1024:((0,384),(384,384),(768,256)),512:((0,128),(128,256),(384,128)),384:((0,128),(128,128),(256,128))}


ALLS=slice(None)

def recv_shapes(r,n):
    (_,a),(_,b),(_,c)=SPLIT[n]
    return dict(core=(4,2,2,r,n),A0=(4,2,r,a),A1=(4,r,a),Ah=(6,r,a),B0=(4,2,r,b),B1=(4,r,b),Bh=(6,r,b),Ch=(6,2,2,r,c),C0=(2,r,c),C1=(r,c))
RNAMES=(N.core,N.A0,N.A1,N.Ah,N.B0,N.B1,N.Bh,N.Ch,N.C0,N.C1)

def add_into(dst,src,cols,lead):
    for di,si in lead:
        dst[(*di,ALLS,cols)]=dst[(*di,ALLS,cols)]+src[si]

class Scatter:
    def __init__(self,me,nb,part,send_half,bufs,out,groups,ssem,rsem):
        self.me,self.nb,self.part,self.half,self.b,self.out,self.groups,self.ssem,self.rsem=me,nb,part,send_half,bufs,out,groups,ssem,rsem
    def copy(self,src,dst,slot,dev):
        return pltpu.make_async_remote_copy(src_ref=src,dst_ref=dst,send_sem=self.ssem.at[slot],recv_sem=self.rsem.at[slot],device_id=dev,device_id_type=MESH)
    def cols(self,r): return pl.ds(*self.groups[r])
    def hop(self,r,k,op):
        z,y,x=(self.me[i] for i in N.zyx)
        rest=(y,x) if r<2 else (ALLS,ALLS)
        buf=self.b[N.ABC[r]+N.h]; cols=self.cols(r)
        su,sd=8*r+k-1,8*r+3+k-1
        up=lambda: self.copy(self.part.at[(z+k,*rest,ALLS,cols)],buf.at[k-1],su,self.nb[N.zu])
        dn=lambda: self.copy(self.part.at[(z-k,*rest,ALLS,cols)],buf.at[3+k-1],sd,self.nb[N.zd])
        if op in(N.start,N.send):
            @pl.when(z+k<=3)
            def _():
                d=up(); d.start() if op==N.start else d.wait_send()
            @pl.when(z-k>=0)
            def _():
                d=dn(); d.start() if op==N.start else d.wait_send()
        else:
            last=(k==1 and r<2)
            @pl.when((z>=1)&(z-1+k<=3))
            def _():
                self.copy(buf.at[k-1],buf.at[k-1],su,self.nb[N.zd]).wait_recv()
                self.hopadd(r,z-1+k,buf.at[k-1],cols)
            @pl.when((z<=2)&(z+1-k>=0))
            def _():
                self.copy(buf.at[3+k-1],buf.at[3+k-1],sd,self.nb[N.zu]).wait_recv()
                self.hopadd(r,z+1-k,buf.at[3+k-1],cols)
    def hopadd(self,r,d,src,cols):
        y,x=self.me[N.y],self.me[N.x]
        if r<2: add_into(self.part,src,cols,[((d,y,x),(ALLS,ALLS))])
        else: add_into(self.part,src,cols,[((d,i,j),(i,j)) for i in range(2) for j in range(2)])
    def flat(self,r,axis,op):
        z,y,x=(self.me[i] for i in N.zyx); cols=self.cols(r)
        name=N.ABC[r]
        if axis==N.x:
            mine={0:(ALLS,ALLS,1-x),1:(ALLS,y,1-x),2:(z,y,1-x)}[r]; slot=8*r+7; buf=self.b[{0:N.A0,1:N.B1,2:N.C1}[r]]
        else:
            mine={0:(ALLS,1-y,x),1:(ALLS,1-y),2:(z,1-y)}[r]; slot=8*r+6; buf=self.b[{0:N.A1,1:N.B0,2:N.C0}[r]]
        if op==N.recv:
            self.copy(buf,buf,slot,self.nb[axis]).wait_recv()
            if axis==N.x:
                lead={0:[((i,j,x),(i,j)) for i in range(4) for j in range(2)],1:[((i,y,x),(i,)) for i in range(4)],2:[((z,y,x),(ALLS,ALLS))]}[r]
            else:
                lead={0:[((i,y,x),(i,)) for i in range(4)],1:[((i,y,j),(i,j)) for i in range(4) for j in range(2)],2:[((z,y,j),(j,)) for j in range(2)]}[r]
            add_into(self.part,buf,cols,lead)
        else:
            d=self.copy(self.part.at[(*mine,)+(ALLS,)*(4-len(mine))+(cols,)],buf,slot,self.nb[axis])
            d.start() if op==N.start else d.wait_send()
    def core(self,op):
        buf=self.b[N.core]
        if op==N.recv:
            self.copy(buf,buf,24,self.nb[N.c]).wait_recv()
            @pl.loop(0,4)
            def _(i):
                for j in range(2):
                    for k in range(2):
                        self.part[i,j,k]=self.part[i,j,k]+buf[i,j,k]
        else:
            d=self.copy(self.half,buf,24,self.nb[N.c]); d.start() if op==N.start else d.wait_send()
    ORDER=[[N.x,N.y,N.h3,N.h2,N.h1],[N.y,N.x,N.h3,N.h2,N.h1],[N.h3,N.h2,N.h1,N.y,N.x]]
    def do(self,r,p,op):
        n=self.ORDER[r][p]
        if n[0]==N.h: self.hop(r,int(n[1]),op)
        else: self.flat(r,n,op)
    def phase(self,p):
        if p==0: self.core(N.start); return
        if p==1: self.core(N.recv)
        for r in range(3):
            if p>=2: self.do(r,p-2,N.recv)
            if p<=5: self.do(r,p-1,N.start)
        if p==6:
            z,y,x=(self.me[i] for i in N.zyx)
            if self.out is not None: self.out[...]=self.part[z,y,x].astype(jnp.float32)
    def sends(self):
        self.core(N.send)
        for r in range(3):
            for p in range(5): self.do(r,p,N.send)

def small_steps(me):
    dp,h=me[N.dp],me[N.h]
    z=me[N.z]
    return [(dp,h+1-2*me[N.c]),(dp,h+2-4*me[N.x]),(dp+1-2*me[N.y],h),(dp+2-4*(z%2),h),(dp+4-8*(z//2),h)]


BF=jnp.bfloat16; F32=jnp.float32
PADC=384
NN=(((1,),(0,)),((),())); NT=(((1,),(1,)),((),())); TN=(((0,),(0,)),((),()))
def dot(a,b,dims=NN): return lax.dot_general(a,b,dims,preferred_element_type=F32)
ROWS=512; TILE=512; RB=128

def norm_rows(load,gain,xhat,rstd,normed,width=D,store_sum=None):
    def body(i,tot):
        rows=pl.ds(i*RB,RB)
        v=load(rows)
        mean=jnp.sum(v,-1,keepdims=True)/width
        cent=v-mean
        var=jnp.sum(cent*cent,-1,keepdims=True)/width
        r=lax.rsqrt(var+1e-5)
        xh=cent*r
        lanes=pl.ds(0,width)
        xhat[rows,lanes]=xh.astype(BF)
        if rstd is not None: rstd[rows]=jnp.broadcast_to(r,(RB,128))
        if normed is not None: normed[rows,lanes]=(xh*gain).astype(BF)
        if tot is None: return None
        return tot+jnp.sum(xh,0,keepdims=True)
    tot=jnp.zeros((1,D),F32) if store_sum else None
    for i in range(ROWS//RB): tot=body(i,tot)
    return tot

def mm(lhs,w,epi):
    for j in range(D//TILE):
        cols=pl.ds(j*TILE,TILE)
        epi(cols,dot(lhs[...],w[:,:,:,:,:,cols].reshape(D,TILE)))

def gelu_pair(v):
    k=math.sqrt(2/math.pi)
    v2=v*v
    t=jnp.tanh(k*v*(1+0.044715*v2))
    h=0.5*(1+t)
    return v*h, h+0.5*v*(1-t*t)*(k*(1+3*0.044715*v2))

SAVED=dict(xb=((512,PADC),BF),xhp=((512,PADC),BF),kv=((512,2048),BF),q=((512,D),BF),qn=((512,D),BF),
  xh0=((512,D),BF),p=((512,512),BF),o=((512,D),BF),
  xh1=((512,D),BF),n1=((512,D),BF),a1=((512,D),BF),dg1=((512,D),BF),
  xh2=((512,D),BF),n2=((512,D),BF),qkv=((3,512,D),BF),ph=((8,512,512),BF),so=((512,D),BF),
  xh3=((512,D),BF),n3=((512,D),BF),a2=((512,D),BF),dg2=((512,D),BF),xh4=((512,D),BF),
  rs0=((512,128),F32),rs1=((512,128),F32),rs2=((512,128),F32),rs3=((512,128),F32),rs4=((512,128),F32))
NAMES=list(SAVED)
TENS=[N.lat,N.kvw]+[(N.w+str(i)) for i in range(8)]+[N.head,N.w8,N.w9]
def tshape(n): return {N.lat:(32,512),N.kvw:(64,PADC)}.get(n,(32,1024))

def forward_kernel(comm,gap,*refs):
    refs=list(refs)
    nt=len(TENS)
    square,kvw,hw_own,lat_own,pixels,masks,valids,labels,aux=[refs.pop(0) for _ in range(9)]
    whole=[refs.pop(0) for _ in range(nt)]
    out={n:refs.pop(0) for n in NAMES}
    vec,tail=refs.pop(0),refs.pop(0)
    bufs=[refs.pop(0) for _ in range(nt)]
    s={n:refs.pop(0) for n in NAMES}
    z,h,pix,turn,ssem,rsem,wsem,osem,psend,precv=refs
    me=where_am_i(); nb=neighbours(me)
    zz,yy,xx,cc=(me[i] for i in N.zyxc)
    micro=me[N.h]
    classes=hw_own.shape[1]
    own={n:bufs[TENS.index(n)].at[zz,yy,xx,cc] for n in TENS}
    turn[...]=jnp.zeros_like(turn)
    turn[:,0:lat_own.shape[1]]=lat_own[...]
    own[N.lat][...]=turn[...].T[0:32].astype(BF)
    turn[...]=jnp.zeros_like(turn)
    turn[0:CIN,0:kvw.shape[1]]=kvw[...]
    own[N.kvw][...]=turn[0:PADC].T[0:64].astype(BF)
    own[N.head][...]=jnp.zeros((32,D),BF)
    own[N.head][:,0:classes]=hw_own[...].astype(BF)
    for i in range(10): own[(N.w+str(i))][...]=square[i].astype(BF)
    for m in (N.xb,N.xhp): s[m][...]=jnp.zeros_like(s[m])
    ev=[]
    ready={}
    if comm:
        dp_,h_=me[N.dp],me[N.h]
        diag=(dp_,(h_+1-2*cc)+2-4*xx)
        entry_barrier(me,nb,[diag])
        peers=[nb[N.c],nb[N.x],diag]
        swaps=[pltpu.make_async_remote_copy(src_ref=pixels.at[p[1],0],dst_ref=pix.at[pl.ds(pl.multiple_of(micro*128,128),128)],send_sem=psend.at[i],recv_sem=precv.at[i],device_id=p,device_id_type=MESH) for i,p in enumerate(peers)]
        for k in swaps: k.start()
        keep_own=pltpu.make_async_copy(pixels.at[micro,0],pix.at[pl.ds(pl.multiple_of(micro*128,128),128)],psend.at[3])
        keep_own.start()
        gs=[Gather(me,nb,b,SPLIT[b.shape[-1]],ssem.at[i],rsem.at[i]) for i,b in enumerate(bufs)]
        for tick in range(nt+6*gap):
            for t in range(nt):
                p=tick-t
                if p>=0 and p%gap==0 and p//gap<=6:
                    ev.append(functools.partial(gs[t].phase,p//gap))
                    if p//gap==6: ready[t]=len(ev)
    else:
        for t in range(nt): ready[t]=0
    pos=[0]
    def pump(k):
        for e in ev[pos[0]:pos[0]+k]: e()
        pos[0]=min(pos[0]+k,len(ev))
    outs=[]
    def weight(name):
        t=TENS.index(name)
        if pos[0]<ready[t]: pump(ready[t]-pos[0])
        if name not in(N.lat,N.head):
            c=pltpu.make_async_copy(bufs[t],whole[t],wsem.at[t]); c.start(); outs.append(c)
        return bufs[t]
    def keep(*names):
        for m in names:
            c=pltpu.make_async_copy(s[m],out[m],osem.at[NAMES.index(m)]); c.start(); outs.append(c)
    gain=lambda i: aux[i:i+1,:]
    pump(14)
    if comm:
        keep_own.wait()
        for i,p in enumerate(peers):
            got=pix.at[pl.ds(pl.multiple_of(p[1]*128,128),128)]
            pltpu.make_async_remote_copy(src_ref=got,dst_ref=got,send_sem=psend.at[0],recv_sem=precv.at[i],device_id=p,device_id_type=MESH).wait_recv()
    norm_rows(lambda r: pix[r].astype(F32),aux[6:7,0:CIN],s[N.xhp],None,s[N.xb],width=CIN)
    keep(N.xb,N.xhp)
    lt=weight(N.lat)
    @pl.loop(0,8)
    def _(i):
        z[:,pl.ds(pl.multiple_of(i*128,128),128)]=lt[i//2,i%2].reshape(128,ROWS).T
    pump(3)
    norm_rows(lambda r: z[r].astype(F32),gain(0),s[N.xh0],s[N.rs0],s[N.qn])
    keep(N.qn,N.xh0,N.rs0)
    kt=weight(N.kvw)
    for j in range(4):
        rows=kt[j].reshape(512,PADC)
        s[N.kv][:,j*512:(j+1)*512]=dot(s[N.xb][...],rows,NT).astype(BF)
    keep(N.kv)
    pump(3)
    w=weight(N.w0)
    def epi(cols,acc): s[N.q][:,cols]=acc.astype(BF)
    mm(s[N.qn],w,epi)
    keep(N.q)
    pump(3)
    for i in range(2):
        rows=pl.ds(i*256,256)
        sc=dot(s[N.q][rows],s[N.kv][:,:D],NT)*(1/32)
        sc=jnp.where(masks[micro]>0,sc,-1e30)
        e=jnp.exp(sc-jnp.max(sc,-1,keepdims=True))
        p=(e*(1/jnp.sum(e,-1,keepdims=True))).astype(BF)
        s[N.p][rows]=p
        s[N.o][rows]=dot(p,s[N.kv][:,D:]).astype(BF)
    pump(2)
    keep(N.p,N.o)
    w=weight(N.w1)
    def epi(cols,acc): h[:,cols]=z[:,cols].astype(F32)+acc
    mm(s[N.o],w,epi)
    pump(3)
    norm_rows(lambda r: h[r],gain(1),s[N.xh1],s[N.rs1],s[N.n1])
    keep(N.xh1,N.rs1,N.n1)
    def addh(cols,acc): h[:,cols]=h[:,cols]+acc
    def mlp(wi,wo,nn,dg,act):
        w=weight(wi)
        def epi(cols,acc):
            a,d=gelu_pair(acc)
            s[act][:,cols]=a.astype(BF); s[dg][:,cols]=d.astype(BF)
        mm(s[nn],w,epi)
        keep(dg,act)
        pump(3)
        w=weight(wo)
        mm(s[act],w,addh)
    mlp(N.w2,N.w3,N.n1,N.dg1,N.a1)
    pump(3)
    norm_rows(lambda r: h[r],gain(2),s[N.xh2],s[N.rs2],s[N.n2])
    keep(N.xh2,N.rs2,N.n2)
    for i in range(3):
        w=weight((N.w+str(4+i)))
        def epi(cols,acc,i=i): s[N.qkv][i,:,cols]=acc.astype(BF)
        mm(s[N.n2],w,epi)
        pump(2)
    keep(N.qkv)
    for i in range(8):
        cols=pl.ds(i*128,128)
        sc=dot(s[N.qkv][0,:,cols],s[N.qkv][1,:,cols],NT)*(128**-0.5)
        e=jnp.exp(sc-jnp.max(sc,-1,keepdims=True))
        p=(e*(1/jnp.sum(e,-1,keepdims=True))).astype(BF)
        s[N.ph][i]=p
        s[N.so][:,cols]=dot(p,s[N.qkv][2,:,cols]).astype(BF)
        if i%4==3: pump(2)
    keep(N.ph,N.so)
    w=weight(N.w7)
    mm(s[N.so],w,addh)
    pump(3)
    norm_rows(lambda r: h[r],gain(3),s[N.xh3],s[N.rs3],s[N.n3])
    keep(N.xh3,N.rs3,N.n3)
    mlp(N.w8,N.w9,N.n3,N.dg2,N.a2)
    tot=norm_rows(lambda r: h[r],gain(4),s[N.xh4],s[N.rs4],None,store_sum=True)
    keep(N.xh4,N.rs4)
    pooled=(tot*gain(4)/ROWS).astype(BF)
    hw=weight(N.head)
    logits=dot(jnp.broadcast_to(pooled,(16,D)),hw[...].reshape(D,D))[0:1]+aux[5:6,:]
    mx=jnp.max(logits,-1,keepdims=True)
    logp=logits-mx-jnp.log(jnp.sum(jnp.exp(logits-mx),-1,keepdims=True))
    lane=lax.broadcasted_iota(jnp.int32,(1,D),1)
    target=jnp.where(lane<classes,jnp.where(lane==labels[micro,0],1.0-SMOOTH,0.0)+SMOOTH/classes,0.0)
    valid=jnp.full((1,D),valids[micro,0].astype(F32))
    loss=-valid*jnp.sum(target*logp,-1,keepdims=True)
    dl=valid*(jnp.exp(logp)-target)
    hi=dl.astype(BF); lo=(dl-hi.astype(F32)).astype(BF)
    dp=dot(jnp.concatenate([jnp.broadcast_to(hi,(16,D)),jnp.broadcast_to(lo,(16,D))],0),hw[...].reshape(D,D),NT)
    pf=pooled.astype(F32)
    shown=jnp.where(lane==classes,valid,dl)
    for i in range(4):
        vec[i:i+1]=pf[:,i*256:(i+1)*256]; vec[4+i:5+i]=shown[:,i*256:(i+1)*256]
    tail[0:1]=dp[0:1]+dp[16:17]; tail[1:2]=dl
    tail[2:3]=jnp.where(lane==0,loss,jnp.where(lane==1,valid,0.0))
    tail[3:4]=tot; tail[4:8]=jnp.zeros((4,D),F32)
    pump(len(ev))
    for c in outs: c.wait()
    if comm:
        for k in swaps: k.wait_send()
        for g in gs: g.sends()

def forward_all(square,kvw,head,lat,pixels,masks,valid,labels,aux,cid=0,comm=True,gap=2):
    nt=len(TENS)
    A=pl.BlockSpec(memory_space=pl.ANY); V=pl.BlockSpec(memory_space=pltpu.VMEM); S=pl.BlockSpec(memory_space=pltpu.SMEM)
    whole=[(4,2,2,2)+tshape(n) for n in TENS]
    outs=[jax.ShapeDtypeStruct(w,BF) for w in whole]
    outs+=[jax.ShapeDtypeStruct(*SAVED[m]) for m in NAMES]+[jax.ShapeDtypeStruct((8,256),F32),jax.ShapeDtypeStruct((8,D),F32)]
    DS=pltpu.SemaphoreType.DMA
    scr=[pltpu.VMEM(w,BF) for w in whole]+[pltpu.VMEM(*SAVED[m]) for m in NAMES]
    scr+=[pltpu.VMEM((512,D),BF),pltpu.VMEM((512,D),F32),pltpu.VMEM((512,CIN),BF),pltpu.VMEM((512,128),F32),
          DS((nt,25)),DS((nt,25)),DS((nt,)),DS((len(NAMES),)),DS((4,)),DS((3,))]
    cp=dict(has_side_effects=True,vmem_limit_bytes=63*MB)
    if comm: cp.update(collective_id=cid)
    r=pl.pallas_call(functools.partial(forward_kernel,comm,gap),out_shape=outs,
        in_specs=[V]*4+[A,V,S,S,V],out_specs=[A]*(nt+len(NAMES))+[V,V],scratch_shapes=scr,
        compiler_params=pltpu.CompilerParams(**cp))(square,kvw,head,lat,pixels,masks,valid,labels,aux)
    return dict(zip(TENS,r[:nt])),dict(zip(NAMES,r[nt:-2])),r[-2],r[-1]


GRADS=[N.w9,N.w8,N.w7,N.w4,N.w5,N.w6,N.w3,N.w2,N.w1,N.w0,N.kvw,N.lat]
WORDER=[N.w9,N.w8,N.w7,N.w4,N.w5,N.w6,N.w3,N.w2,N.w1,N.w0,N.kvw]
NEEDED=[N.a2,N.dg2,N.n3,N.xh3,N.rs3,N.so,N.ph,N.qkv,N.n2,N.xh2,N.rs2,N.a1,N.dg1,N.n1,N.xh1,N.rs1,N.o,N.p,N.kv,N.q,N.xb,N.xhp,N.qn,N.xh0,N.rs0,N.xh4,N.rs4]
def gshape(n): return {N.lat:(32,512),N.kvw:(64,PADC)}.get(n,(32,D))
RING=4; SRING=2; GAP=2

def backward_kernel(comm,classes,*refs):
    refs=list(refs)
    wt={n:refs.pop(0) for n in WORDER}
    sv={n:refs.pop(0) for n in NEEDED}
    vec,tail,aux,sq_w,sq_m,sq_a=[refs.pop(0) for _ in range(6)]
    sq_new=[refs.pop(0) for _ in range(4)]
    kv_out,lat_out,vec_out,small_out=[refs.pop(0) for _ in range(4)]
    nt=len(GRADS)
    part=[refs.pop(0) for _ in range(nt)]
    send_ring=[refs.pop(0) for _ in range(SRING)]; send_kv,send_lat=refs.pop(0),refs.pop(0)
    core_ring=[refs.pop(0) for _ in range(RING)]; core_kv,core_lat=refs.pop(0),refs.pop(0)
    rbuf=[{k:refs.pop(0) for k in RNAMES[1:]} for _ in range(nt)]
    wslot=[refs.pop(0) for _ in range(2)]; kslot=refs.pop(0)
    aslot=[refs.pop(0) for _ in range(2)]; xslot,rslot=refs.pop(0),refs.pop(0)
    gslot,hslot,qkvslot,xbslot,xhpslot=[refs.pop(0) for _ in range(5)]
    dh,dn,g,dp,dqkv=[refs.pop(0) for _ in range(5)]
    vbuf,srecv,ssend=[refs.pop(0) for _ in range(3)]
    wsem,asem,hsem,ssem,rsem,vs,vr,sms,smr,usem=refs
    me=where_am_i(); nb=neighbours(me)
    z,y,x,c=(me[i] for i in N.zyxc)
    first=c==0
    A=[N.a2,N.n3,N.so,N.n2,N.a1,N.n1,N.o,N.qn]
    X=[N.xh4,N.xh3,N.xh2,N.xh1,N.xh0]; R=[N.rs4,N.rs3,N.rs2,N.rs1,N.rs0]
    place={n:aslot[i%2] for i,n in enumerate(A)}
    place.update({n:xslot for n in X}); place.update({n:rslot for n in R})
    place.update(dg2=gslot,dg1=gslot,p=hslot.at[1],qkv=qkvslot,xb=xbslot,xhp=xhpslot)
    wi=[n for n in WORDER if n!=N.kvw]
    place.update({n:wslot[i%2] for i,n in enumerate(wi)}); place[N.kvw]=kslot
    live={}
    def load(*names):
        for n in names:
            if n in WORDER: cs=[pltpu.make_async_copy(wt[n],place[n],wsem.at[WORDER.index(n)])]
            elif n==N.kv:
                cs=[pltpu.make_async_copy(sv[n].at[:,pl.ds(0,D)],qkvslot.at[1],asem.at[NEEDED.index(n)]),
                    pltpu.make_async_copy(sv[n].at[:,pl.ds(D,D)],qkvslot.at[2],asem.at[len(NEEDED)])]
            elif n==N.q: cs=[pltpu.make_async_copy(sv[n],qkvslot.at[0],asem.at[NEEDED.index(n)])]
            else: cs=[pltpu.make_async_copy(sv[n],place[n],asem.at[NEEDED.index(n)])]
            for k in cs: k.start()
            live[n]=cs
    def use(n):
        for k in live.pop(n): k.wait()
        return place.get(n)
    def load_head(i):
        k=pltpu.make_async_copy(sv[N.ph].at[i],hslot.at[i%2],hsem.at[i]); k.start(); live[(N.ph+str(i))]=[k]
    load(N.xh4,N.rs4,N.w9,N.a2,N.dg2,N.w8,N.n3,N.qkv)
    for i in range(2): load_head(i)
    vbuf[z,y,x,c]=vec[...]
    if comm: entry_barrier(me,nb,small_steps(me)[4:])
    gs=[]
    rings={}
    for t,n in enumerate(GRADS):
        if n==N.kvw: sb,cb=send_kv,core_kv
        elif n==N.lat: sb,cb=send_lat,core_lat
        else:
            k=wi.index(n); sb,cb=send_ring[k%SRING],core_ring[k%RING]
        out={N.kvw:kv_out,N.lat:lat_out}.get(n)
        gs.append(Scatter(me,nb,part[t],sb,dict(rbuf[t],core=cb),out,SPLIT[gshape(n)[1]],ssem.at[t],rsem.at[t]))
    gv=Gather(me,nb,vbuf,[(0,0),(0,0),(0,vbuf.shape[-1])],vs,vr)
    queue={}
    for tick in range(nt+6*GAP+1):
        q=[]
        if tick%2==0 and tick//2<=6: q.append(functools.partial(gv.phase,tick//2))
        for t in range(nt):
            p=tick-t
            if p>0 and p%GAP==0 and p//GAP<=6: q.append(functools.partial(gs[t].phase,p//GAP))
        queue[tick]=q
    now=[0]
    def pump(k):
        if not comm: return
        for _ in range(k):
            if queue[now[0]]: queue[now[0]].pop(0)()
    waited=set()
    def before_store(n):
        if n in wi and wi.index(n)>=SRING and comm:
            o=GRADS.index(wi[wi.index(n)-SRING]); gs[o].core(N.send); waited.add(o)
    def push(n):
        if not comm: return
        pump(len(queue[now[0]]))
        assert GRADS[now[0]]==n
        gs[now[0]].phase(0)
        now[0]+=1
    def store(n,v,r0,cols):
        t=GRADS.index(n); r=gshape(n)[0]; k=v.shape[0]//(2*r)
        v=v.astype(BF).reshape(k,2,r,v.shape[1])
        own=jnp.where(first,v[:,0],v[:,1]); other=jnp.where(first,v[:,1],v[:,0])
        b0=r0//(2*r)
        for ref,val in ((part[t],own),(gs[t].half,other)):
            if k==16: ref[:,:,:,:,cols]=val.reshape(4,2,2,r,v.shape[-1])
            elif k>=4: ref[b0//4:(b0+k)//4,:,:,:,cols]=val.reshape(k//4,2,2,r,v.shape[-1])
            else: ref[b0//4,(b0%4)//2,:,:,cols]=val.reshape(2,r,v.shape[-1])
    def weight_grad(n,a,dy):
        before_store(n)
        for j in range(2):
            cols=pl.ds(j*512,512)
            store(n,dot(a[...],dy[:,cols],TN),0,cols)
            pump(1)
        push(n)
    def back(dy,w,epi):
        for j in range(2):
            rows=w[2*j:2*j+2].reshape(512,D)
            epi(pl.ds(j*512,512),dot(dy[...],rows,NT))
            pump(1)
    gain=lambda i: aux[i:i+1,:]
    def norm_back(load_dn,gn,xh,rs,base,store_to):
        def body(i,tot):
            rows=pl.ds(i*RB,RB)
            d=load_dn(rows); xv=xh[rows].astype(F32)
            dx=d*gn
            m1=jnp.sum(dx,-1,keepdims=True)/D; m2=jnp.sum(dx*xv,-1,keepdims=True)/D
            r=rs[rows][:,0:1]*(dx-m1-xv*m2)
            if base is not None: r=r+base[rows]
            store_to(rows,r)
            return tot+jnp.sum(d*xv,0,keepdims=True)
        tot=jnp.zeros((1,D),F32)
        for i in range(ROWS//RB): tot=body(i,tot)
        return tot
    def to_dh(rows,r):
        dh[rows]=r; g[rows]=r.astype(BF)
    def to_dn(cols,acc): dn[:,cols]=acc
    def to_dp(cols,acc): dp[:,cols]=acc.astype(BF)
    small=ssend.at[0]
    const=tail[0:1]*(1/ROWS)
    use(N.rs4)
    dg=norm_back(lambda r: jnp.broadcast_to(const,(RB,D)),gain(4),use(N.xh4),place[N.rs4],None,to_dh)
    small[4:5]=dg
    small[5:8]=jnp.zeros((3,D),F32)
    small[6:8]=tail[1:3]
    load(N.xh3,N.rs3)
    def mlp_back(wo,wi_,act,normed,dgn,xh,rs,row,nxt):
        a=use(act)
        weight_grad(wo,a,g)
        load(*nxt[0])
        w=use(wo); d=use(dgn)
        def epi(cols,acc): dp[:,cols]=(acc*d[:,cols].astype(F32)).astype(BF)
        back(g,w,epi)
        load(*nxt[1])
        weight_grad(wi_,use(normed),dp)
        load(*nxt[2])
        back(dp,use(wi_),to_dn)
        load(*nxt[3])
        use(rs)
        small[row:row+1]=norm_back(lambda r: dn[r],gain(row),use(xh),place[rs],dh,to_dh)
    mlp_back(N.w9,N.w8,N.a2,N.n3,N.dg2,N.xh3,N.rs3,3,([ N.so],[N.w7,N.dg1],[N.n2],[N.w4]))
    load(N.xh2,N.rs2)
    weight_grad(N.w7,use(N.so),g)
    load(N.a1)
    back(g,use(N.w7),to_dp)
    load(N.w5)
    use(N.qkv)
    sc=128**-0.5
    for i in range(8):
        cols=pl.ds(i*128,128)
        use((N.ph+str(i))); ph=hslot.at[i%2]
        qh,kh,vh=(qkvslot[k,:,cols] for k in range(3)); do=dp[:,cols]
        pf=ph[...].astype(F32)
        dpr=dot(do,vh,NT)
        ds=(pf*(dpr-jnp.sum(pf*dpr,-1,keepdims=True)/jnp.sum(pf,-1,keepdims=True))).astype(BF)
        dqkv[0,:,cols]=(dot(ds,kh)*sc).astype(BF)
        dqkv[1,:,cols]=(dot(ds,qh,TN)*sc).astype(BF)
        dqkv[2,:,cols]=dot(ph[...],do,TN).astype(BF)
        if i+2<8: load_head(i+2)
        pump(1)
    load(N.q,N.kv,N.p,N.xb,N.xhp)
    n2=use(N.n2)
    for i in range(3):
        weight_grad((N.w+str(4+i)),n2,dqkv.at[i])
        if i==2: load(N.n1)
        if i==0: back(dqkv.at[0],use(N.w4),to_dn)
        else:
            def add_dn(cols,acc): dn[:,cols]=dn[:,cols]+acc
            back(dqkv.at[i],use((N.w+str(4+i))),add_dn)
        load((N.w6,N.w3,N.w2)[i])
    use(N.rs2)
    small[2:3]=norm_back(lambda r: dn[r],gain(2),use(N.xh2),place[N.rs2],dh,to_dh)
    load(N.xh1,N.rs1)
    mlp_back(N.w3,N.w2,N.a1,N.n1,N.dg1,N.xh1,N.rs1,1,([N.o],[N.w1,N.kvw],[N.qn],[N.w0]))
    load(N.xh0,N.rs0)
    weight_grad(N.w1,use(N.o),g)
    back(g,use(N.w1),to_dp)
    use(N.q); use(N.kv); p=use(N.p)
    q,k,v=(qkvslot.at[i] for i in range(3))
    dpr=dot(dp[...],v[...],NT)
    pf=p[...].astype(F32)
    ds=(pf*(dpr-jnp.sum(pf*dpr,-1,keepdims=True)/jnp.sum(pf,-1,keepdims=True))).astype(BF)
    for j in range(2):
        cols=pl.ds(j*512,512)
        dqkv[0,:,cols]=(dot(ds,k[:,cols])*(1/32)).astype(BF)
        pump(1)
    weight_grad(N.w0,use(N.qn),dqkv.at[0])
    for j in range(2):
        cols=pl.ds(j*512,512)
        dqkv[1,:,cols]=(dot(ds,q[:,cols],TN)*(1/32)).astype(BF)
        dqkv[2,:,cols]=dot(p[...],dp[:,cols],TN).astype(BF)
        pump(1)
    xb=use(N.xb)
    for i in (0,1):
        store(N.kvw,dot(dqkv[1+i],xb[...],TN),i*D,pl.ds(0,PADC))
        pump(1)
    push(N.kvw)
    back(dqkv.at[0],use(N.w0),to_dn)
    use(N.rs0)
    def to_h(rows,r): dh[rows]=r
    small[0:1]=norm_back(lambda r: dn[r],gain(0),use(N.xh0),place[N.rs0],dh,to_h)
    for i in range(8):
        store(N.lat,dh[:,i*128:(i+1)*128].T,i*128,pl.ds(0,512))
    push(N.lat)
    kw=use(N.kvw); xp=use(N.xhp)
    dx=dot(dqkv[1],kw[0:2].reshape(D,PADC))+dot(dqkv[2],kw[2:4].reshape(D,PADC))
    small[5:6,0:PADC]=jnp.sum(dx*xp[...].astype(F32),0,keepdims=True)
    if comm:
        sm=[pltpu.make_async_remote_copy(src_ref=ssend.at[i],dst_ref=srecv.at[i],send_sem=sms.at[i],recv_sem=smr.at[i],device_id=q_,device_id_type=MESH) for i,q_ in enumerate(small_steps(me))]
        def small_step(i):
            if i>0:
                sm[i-1].wait_recv()
                r=ssend[i-1]+srecv[i-1]
                if i<5: ssend[i]=r
                else: small_out[...]=r
            if i<5: sm[i].start()
        slot=lambda u,k: (dh,dn)[u%8//4].at[pl.ds(u%4*128+k*32,32)]
        order=[n for n in GRADS if n[0]==N.w]
        reads,writes={},{}
        def read(u):
            i=int(order[u][1])
            reads[u]=[pltpu.make_async_copy(r.at[i],slot(u,k+1),usem.at[u,k]) for k,r in enumerate((sq_m,sq_w,sq_a))]
            for k in reads[u]: k.start()
        def update(t):
            u=order.index(GRADS[t]); i=int(GRADS[t][1])
            for k in reads[u]: k.wait()
            gr=part[t][z,y,x].astype(F32)/count[0]
            mom=MOMENTUM*slot(u,1)[...]+gr
            new=slot(u,2)[...]-LEARN_RATE*(gr+MOMENTUM*mom)
            slot(u,0)[...]=gr; slot(u,1)[...]=mom
            slot(u,3)[...]=AVERAGE_DECAY*slot(u,3)[...]+(1.0-AVERAGE_DECAY)*new
            slot(u,2)[...]=new
            writes[u]=[pltpu.make_async_copy(slot(u,k),r.at[i],usem.at[u,3+k]) for k,r in enumerate(sq_new)]
            for k in writes[u]: k.start()
            if u==3:
                for v in (0,1):
                    for k in writes[v]: k.wait()
                    writes[v]=[]
                    read(8+v)
        for u in range(8): read(u)
        count=[]
        step=0
        for tick in range(now[0],nt+6*GAP+1):
            if step<=5: small_step(step); step+=1
            for e in queue[tick]: e()
            if tick==6*GAP:
                lane=lax.broadcasted_iota(jnp.int32,(1,256),1)
                seen=jnp.sum(vbuf[:,:,:,:,7:8,:].reshape(32,256),0,keepdims=True)
                seen=jnp.sum(jnp.where(lane==classes-768,seen,0.0),-1,keepdims=True)
                count.append(jnp.maximum(seen,1.0))
            t=tick-6*GAP
            if 0<=t<nt and GRADS[t][0]==N.w: update(t)
        while step<=5: small_step(step); step+=1
        for w_ in writes.values():
            for k in w_: k.wait()
        for s_ in sm: s_.wait_send()
        gv.sends()
        for t,s_ in enumerate(gs):
            if t not in waited: s_.core(N.send)
            for r in range(3):
                for ph_ in range(5): s_.do(r,ph_,N.send)
    else:
        small_out[...]=ssend[0]
        kv_out[...]=jnp.zeros_like(kv_out); lat_out[...]=jnp.zeros_like(lat_out)
    vec_out[...]=vbuf[...]

def backward_all(w,sv,vec,tail,aux,sq_w,sq_m,sq_a,classes,cid=1,comm=True):
    A=pl.BlockSpec(memory_space=pl.ANY); V=pl.BlockSpec(memory_space=pltpu.VMEM)
    DS=pltpu.SemaphoreType.DMA
    M=pltpu.VMEM
    nt=len(GRADS)
    outs=[jax.ShapeDtypeStruct(sq_w.shape,F32)]*4+[jax.ShapeDtypeStruct((64,PADC),F32),jax.ShapeDtypeStruct((32,512),F32),
          jax.ShapeDtypeStruct((4,2,2,2,8,256),F32),jax.ShapeDtypeStruct((8,D),F32)]
    scr=[M((4,2,2)+gshape(n),BF) for n in GRADS]
    half=lambda n: M((4,2,2)+gshape(n),BF)
    scr+=[half(N.w0)]*SRING+[half(N.kvw),half(N.lat)]+[half(N.w0)]*RING+[half(N.kvw),half(N.lat)]
    for n in GRADS:
        sh=recv_shapes(*gshape(n)); scr+=[M(sh[k],BF) for k in RNAMES[1:]]
    scr+=[M((4,2,2,2,32,D),BF)]*2+[M((4,2,2,2,64,PADC),BF)]
    scr+=[M((512,D),BF)]*3+[M((512,128),F32)]
    scr+=[M((512,D),BF),M((2,512,512),BF),M((3,512,D),BF),M((512,PADC),BF),M((512,PADC),BF)]
    scr+=[M((512,D),F32),M((512,D),F32),M((512,D),BF),M((512,D),BF),M((3,512,D),BF)]
    scr+=[M((4,2,2,2,8,256),F32),M((5,8,D),F32),M((5,8,D),F32)]
    scr+=[DS((len(WORDER),)),DS((len(NEEDED)+1,)),DS((8,)),DS((nt,25)),DS((nt,25)),DS((25,)),DS((25,)),DS((5,)),DS((5,)),DS((10,7))]
    cp=dict(has_side_effects=True,vmem_limit_bytes=63*MB+MB//2)
    if comm: cp[N.collective_id]=cid
    return pl.pallas_call(functools.partial(backward_kernel,comm,classes),out_shape=outs,
        in_specs=[A]*(len(WORDER)+len(NEEDED))+[V]*3+[A]*3,out_specs=[A]*4+[V]*4,scratch_shapes=scr,
        compiler_params=pltpu.CompilerParams(**cp))(*[w[n] for n in WORDER],*[sv[n] for n in NEEDED],vec,tail,aux,sq_w,sq_m,sq_a)


def per_device_images(
    pixels,
    masks,
    valid,
    labels,
    square,
    kv_weight,
    head_weight,
    latents,
    small,
    square_mom,
    kv_mom,
    head_mom,
    latent_mom,
    small_mom,
    square_avg,
    kv_avg,
    head_avg,
    latent_avg,
    small_avg,
):
    micro = lax.axis_index(N.head)
    classes = head_weight.shape[1]
    bias = jnp.pad(small[5 * D + CIN :], (0, D - classes), constant_values=NEG_BIG)
    pixel_gain = jnp.pad(small[5 * D : 5 * D + CIN], (0, D - CIN))
    aux = jnp.concatenate([small[: 5 * D], bias, pixel_gain, jnp.zeros((D,), F32)]).reshape(8, D)
    weights, saved, vec, tail = forward_all(
        square, kv_weight, head_weight, latents, pixels, masks, valid, labels, aux
    )
    *square_new, d_kv, d_lat, vec_all, packed = backward_all(
        weights, saved, vec, tail, aux, square, square_mom, square_avg, classes
    )
    small_total = jnp.concatenate([packed[:5].reshape(-1), packed[5, :CIN], packed[6, :classes]])
    loss_sum, count = packed[7, 0], jnp.maximum(packed[7, 1], 1.0)
    vec_all = vec_all.reshape(-1, 2 * D)
    own = head_weight.shape[0]
    first = (lax.axis_index(N.dp) * lax.axis_size(N.head) + micro) * own
    pooled_own = lax.dynamic_slice_in_dim(vec_all, first, own, 1)
    d_head = lax.dot_general(
        pooled_own, vec_all[:, D : D + classes], (((0,), (0,)), ((), ())), precision=lax.Precision.HIGHEST
    )
    grads = (d_kv[:, :CIN].T, d_head, d_lat.T, small_total)
    latent_rate = LATENTS * math.sqrt(D * MICRO * IMG_DEV * lax.axis_size(N.dp)) / 32.0
    rates = (LEARN_RATE, LEARN_RATE, latent_rate, LEARN_RATE)
    results = [loss_sum, count, *square_new]
    params = (kv_weight, head_weight, latents, small)
    moms = (kv_mom, head_mom, latent_mom, small_mom)
    avgs = (kv_avg, head_avg, latent_avg, small_avg)
    for weight, grad, mom, avg, rate in zip(params, grads, moms, avgs, rates):
        results.extend(nesterov(weight, grad / count, mom, avg, rate))
    return tuple(results)


def solution(mesh):
    in_specs = (
        P(None, "dp", "head", None),
        P(None, "dp", None),
        P(None, "dp"),
        P(None, "dp"),
        P(None, ("dp", "head"), None),
        P(None, ("dp", "head")),
        P(("dp", "head"), None),
        P(None, ("dp", "head")),
        P(),
        P(None, ("dp", "head"), None),
        P(None, ("dp", "head")),
        P(("dp", "head"), None),
        P(None, ("dp", "head")),
        P(),
        P(None, ("dp", "head"), None),
        P(None, ("dp", "head")),
        P(("dp", "head"), None),
        P(None, ("dp", "head")),
        P(),
    )
    out_specs = (
        P(),
        P(),
        P(None, ("dp", "head"), None),
        P(None, ("dp", "head"), None),
        P(None, ("dp", "head"), None),
        P(None, ("dp", "head"), None),
        P(None, ("dp", "head")),
        P(None, ("dp", "head")),
        P(None, ("dp", "head")),
        P(None, ("dp", "head")),
        P(("dp", "head"), None),
        P(("dp", "head"), None),
        P(("dp", "head"), None),
        P(("dp", "head"), None),
        P(None, ("dp", "head")),
        P(None, ("dp", "head")),
        P(None, ("dp", "head")),
        P(None, ("dp", "head")),
        P(),
        P(),
        P(),
        P(),
    )
    whole_images = dict(mesh.shape) == {"dp": 8, "head": MICRO}
    per_device = per_device_images if whole_images else per_device_rows
    return jax.shard_map(
        per_device, mesh=mesh, in_specs=in_specs, out_specs=out_specs, check_vma=False
    )
```

```python
import functools
import math

import jax
import jax.numpy as jnp
from jax import lax
from jax.experimental import pallas as pl
from jax.experimental.pallas import tpu as pltpu
from jax.sharding import PartitionSpec as P

D = 1024
CIN = 261
LATENTS = 512
HEADS = 8
HEAD_DIM = 128
MICRO = 4
IMG_DEV = 1


EPS = 1e-05
NEG_BIG = -1e30
SMOOTH = 0.1
LEARN_RATE = 20.0
MOMENTUM = 0.9
AVERAGE_DECAY = 0.6


def layer_norm(v, gain):
    mean = jnp.mean(v, axis=-1, keepdims=True)
    cent = v - mean
    var = jnp.mean(cent * cent, axis=-1, keepdims=True)
    return cent * lax.rsqrt(var + EPS) * gain


def dot_nn(left, right):
    return jnp.dot(left, right, preferred_element_type=jnp.float32)


def dot_tn(left, right):
    return lax.dot_general(
        left, right, (((0,), (0,)), ((), ())), preferred_element_type=jnp.float32
    )


def dot_nt(left, right):
    return lax.dot_general(
        left, right, (((1,), (1,)), ((), ())), preferred_element_type=jnp.float32
    )


def scores_of(query, keys, valid_keys):
    scores = jnp.einsum("qhd,khd->hqk", query, keys, preferred_element_type=jnp.float32)
    scores = scores * query.shape[-1] ** (-0.5)
    if valid_keys is not None:
        scores = jnp.where(valid_keys[None, None, :], scores, NEG_BIG)
    return scores


def attend(query, keys, values, valid_keys):
    scores = scores_of(query, keys, valid_keys)
    log_total = jax.nn.logsumexp(scores, axis=-1, keepdims=True)
    probs = jnp.exp(scores - log_total).astype(jnp.bfloat16)
    out = jnp.einsum("hqk,khd->qhd", probs, values, preferred_element_type=jnp.float32)
    return (out.astype(jnp.bfloat16), log_total)


def attend_back(query, keys, values, log_total, d_out, valid_keys):
    scale = query.shape[-1] ** (-0.5)
    probs = jnp.exp(scores_of(query, keys, valid_keys) - log_total)
    probs_b = probs.astype(jnp.bfloat16)
    d_probs = jnp.einsum("qhd,khd->hqk", d_out, values, preferred_element_type=jnp.float32)
    d_scores = probs * (d_probs - jnp.sum(probs * d_probs, axis=-1, keepdims=True))
    d_scores = d_scores.astype(jnp.bfloat16)
    d_query = jnp.einsum("hqk,khd->qhd", d_scores, keys, preferred_element_type=jnp.float32) * scale
    d_keys = jnp.einsum("hqk,qhd->khd", d_scores, query, preferred_element_type=jnp.float32) * scale
    d_values = jnp.einsum("hqk,qhd->khd", probs_b, d_out, preferred_element_type=jnp.float32)
    return (d_query, d_keys, d_values)


def mlp_forward(hidden, gain, w_in, w_out):
    normed = layer_norm(hidden, gain).astype(jnp.bfloat16)
    pre = dot_nn(normed, w_in)
    active = jax.nn.gelu(pre).astype(jnp.bfloat16)
    return (hidden + dot_nn(active, w_out), (normed, pre, active))


def mlp_backward(hidden, gain, w_in, w_out, saved, d_next):
    normed, pre, active = saved
    d_next_b = d_next.astype(jnp.bfloat16)
    d_w_out = dot_tn(active, d_next_b)
    d_active = dot_nt(d_next_b, w_out)
    d_pre = jax.vjp(jax.nn.gelu, pre)[1](d_active)[0].astype(jnp.bfloat16)
    d_w_in = dot_tn(normed, d_pre)
    d_normed = dot_nt(d_pre, w_in)
    d_hidden, d_gain = jax.vjp(layer_norm, hidden, gain)[1](d_normed)
    return (d_next + d_hidden, d_gain, d_w_in, d_w_out)


def image_grads(weights, small, pixel_own, mask_row, valid_one, label, loss_scale, head_first):
    square, kv_weight, head_weight, latent_all, w_qkv = weights
    gains = small[: 5 * D].reshape(5, D)
    pix_gain = small[5 * D : 5 * D + CIN]
    bias = small[5 * D + CIN :]
    rows = latent_all.shape[0] // lax.axis_size("head")
    start = lax.axis_index("head") * rows
    latent_own = lax.dynamic_slice_in_dim(latent_all, start, rows, 0).astype(jnp.float32)
    valid_keys = mask_row > 0
    pix_float = pixel_own.astype(jnp.float32)
    normed_pix = layer_norm(pix_float, pix_gain).astype(jnp.bfloat16)
    kv_own = dot_nn(normed_pix, kv_weight).astype(jnp.bfloat16)
    kv_all = lax.all_gather(kv_own, "head", axis=0, tiled=True)
    keys_px = kv_all[:, :D].reshape(-1, 1, D)
    values_px = kv_all[:, D:].reshape(-1, 1, D)
    query_norm = layer_norm(latent_own, gains[0]).astype(jnp.bfloat16)
    query = dot_nn(query_norm, square[0]).astype(jnp.bfloat16).reshape(rows, 1, D)
    cross_out, cross_total = attend(query, keys_px, values_px, valid_keys)
    cross_out = cross_out.reshape(rows, D)
    hidden1 = latent_own + dot_nn(cross_out, square[1])
    hidden2, mlp_first = mlp_forward(hidden1, gains[1], square[2], square[3])
    self_norm = layer_norm(hidden2, gains[2]).astype(jnp.bfloat16)
    qkv = dot_nn(self_norm, w_qkv).astype(jnp.bfloat16)
    kv_latent = lax.all_gather(qkv[:, D:], "head", axis=0, tiled=True)
    self_query = qkv[:, :D].reshape(rows, HEADS, HEAD_DIM)
    self_keys = kv_latent[:, :D].reshape(-1, HEADS, HEAD_DIM)
    self_values = kv_latent[:, D:].reshape(-1, HEADS, HEAD_DIM)
    self_out, self_total = attend(self_query, self_keys, self_values, None)
    self_out = self_out.reshape(rows, D)
    hidden3 = hidden2 + dot_nn(self_out, square[7])
    hidden4, mlp_second = mlp_forward(hidden3, gains[3], square[8], square[9])
    final = layer_norm(hidden4, gains[4])
    pooled = lax.psum(jnp.sum(final, axis=0), "head") / latent_all.shape[0]
    pooled_b = pooled.astype(jnp.bfloat16)
    logits = dot_nn(pooled_b[None, :], head_weight)[0] + bias
    logp = jax.nn.log_softmax(logits)
    picked = jnp.arange(logits.shape[0]) == label
    loss = -valid_one * (
        (1.0 - SMOOTH) * jnp.sum(jnp.where(picked, logp, 0.0)) + SMOOTH * jnp.mean(logp)
    )
    target = (1.0 - SMOOTH) * picked.astype(jnp.float32) + SMOOTH / logits.shape[0]
    d_logits = valid_one * loss_scale * (jnp.exp(logp) - target)
    d_bias = d_logits * head_first
    d_head = pooled_b.astype(jnp.float32)[:, None] * d_logits[None, :] * head_first
    d_pooled = jnp.dot(head_weight.astype(jnp.float32), d_logits)
    d_final = jnp.broadcast_to(d_pooled / latent_all.shape[0], final.shape)
    d_hidden4, d_gain4 = jax.vjp(layer_norm, hidden4, gains[4])[1](d_final)
    d_hidden3, d_gain3, d_w8, d_w9 = mlp_backward(
        hidden3, gains[3], square[8], square[9], mlp_second, d_hidden4
    )
    d_hidden3_b = d_hidden3.astype(jnp.bfloat16)
    d_w7 = dot_tn(self_out, d_hidden3_b)
    d_self_out = dot_nt(d_hidden3_b, square[7]).astype(jnp.bfloat16).reshape(rows, HEADS, HEAD_DIM)
    d_query, d_keys, d_values = attend_back(
        self_query, self_keys, self_values, self_total, d_self_out, None
    )
    d_kv_terms = jnp.concatenate([d_keys.reshape(-1, D), d_values.reshape(-1, D)], axis=1)
    d_kv_own = lax.psum_scatter(
        d_kv_terms.astype(jnp.bfloat16), "head", scatter_dimension=0, tiled=True
    ).astype(jnp.float32)
    d_qkv = jnp.concatenate([d_query.reshape(rows, D), d_kv_own], axis=1).astype(jnp.bfloat16)
    d_w_qkv = dot_tn(self_norm, d_qkv)
    d_self_norm = dot_nt(d_qkv, w_qkv)
    d_hidden2_norm, d_gain2 = jax.vjp(layer_norm, hidden2, gains[2])[1](d_self_norm)
    d_hidden2 = d_hidden3 + d_hidden2_norm
    d_hidden1, d_gain1, d_w2, d_w3 = mlp_backward(
        hidden1, gains[1], square[2], square[3], mlp_first, d_hidden2
    )
    d_hidden1_b = d_hidden1.astype(jnp.bfloat16)
    d_w1 = dot_tn(cross_out, d_hidden1_b)
    d_cross = dot_nt(d_hidden1_b, square[1]).astype(jnp.bfloat16).reshape(rows, 1, D)
    d_query, d_keys, d_values = attend_back(
        query, keys_px, values_px, cross_total, d_cross, valid_keys
    )
    d_px_terms = jnp.concatenate([d_keys.reshape(-1, D), d_values.reshape(-1, D)], axis=1)
    d_kv_px = lax.psum_scatter(
        d_px_terms.astype(jnp.bfloat16), "head", scatter_dimension=0, tiled=True
    )
    d_kv_turned = dot_tn(d_kv_px, normed_pix)
    d_normed_pix = dot_nt(d_kv_px, kv_weight)
    d_pix_gain = jax.vjp(layer_norm, pix_float, pix_gain)[1](d_normed_pix)[1]
    d_query_b = d_query.reshape(rows, D).astype(jnp.bfloat16)
    d_w0 = dot_tn(query_norm, d_query_b)
    d_query_norm = dot_nt(d_query_b, square[0])
    d_latent_norm, d_gain0 = jax.vjp(layer_norm, latent_own, gains[0])[1](d_query_norm)
    d_latent_own = d_hidden1 + d_latent_norm
    d_square = jnp.stack(
        [
            d_w0,
            d_w1,
            d_w2,
            d_w3,
            d_w_qkv[:, :D],
            d_w_qkv[:, D : 2 * D],
            d_w_qkv[:, 2 * D :],
            d_w7,
            d_w8,
            d_w9,
        ]
    )
    latent_turned = lax.dynamic_update_slice_in_dim(
        jnp.zeros((D, latent_all.shape[0]), jnp.float32), d_latent_own.T, start, 1
    )
    d_small = jnp.concatenate(
        [jnp.stack([d_gain0, d_gain1, d_gain2, d_gain3, d_gain4]).reshape(-1), d_pix_gain, d_bias]
    )
    return ((d_square, d_kv_turned[None], d_head[None], latent_turned[None], d_small), loss)


def owner_layout(reduced):
    return (reduced[0], reduced[1][0].T, reduced[2][0], reduced[3][0].T)


def nesterov(weight, grad, mom, avg, rate):
    mom_new = MOMENTUM * mom + grad
    weight_new = weight - rate * (grad + MOMENTUM * mom_new)
    avg_new = AVERAGE_DECAY * avg + (1.0 - AVERAGE_DECAY) * weight_new
    return (grad, mom_new, weight_new, avg_new)


def per_device_rows(
    pixels,
    masks,
    valid,
    labels,
    square,
    kv_weight,
    head_weight,
    latents,
    small,
    square_mom,
    kv_mom,
    head_mom,
    latent_mom,
    small_mom,
    square_avg,
    kv_avg,
    head_avg,
    latent_avg,
    small_avg,
):
    gathered = (
        lax.all_gather(square.astype(jnp.bfloat16), ("dp", "head"), axis=1, tiled=True),
        lax.all_gather(kv_weight.astype(jnp.bfloat16), ("dp", "head"), axis=1, tiled=True),
        lax.all_gather(head_weight.astype(jnp.bfloat16), ("dp", "head"), axis=0, tiled=True),
        lax.all_gather(latents.astype(jnp.bfloat16), ("dp", "head"), axis=1, tiled=True),
    )
    full_square = gathered[0]
    w_qkv = jnp.concatenate([full_square[4], full_square[5], full_square[6]], axis=1)
    weights = (full_square, gathered[1], gathered[2], gathered[3], w_qkv)
    head_first = (lax.axis_index("head") == 0).astype(jnp.float32)
    valid_float = valid.astype(jnp.float32)
    early_count = lax.psum(jnp.sum(valid_float), "dp")
    loss_scale = 1.0 / jnp.maximum(early_count, 1.0)
    kv_shape = gathered[1].shape
    lat_shape = gathered[3].shape
    big_zero = (
        jnp.zeros(full_square.shape, jnp.float32),
        jnp.zeros((1, kv_shape[1], kv_shape[0]), jnp.float32),
        jnp.zeros((1,) + gathered[2].shape, jnp.float32),
        jnp.zeros((1, lat_shape[1], lat_shape[0]), jnp.float32),
    )

    def micro_step(carry, batch):
        big, small_acc, loss_acc = carry
        pix_micro, mask_micro, valid_micro, label_micro = batch
        grads, loss_part = image_grads(
            weights,
            small,
            pix_micro[0],
            mask_micro[0],
            valid_micro[0],
            label_micro[0],
            loss_scale,
            head_first,
        )
        reduced = (grads[0], grads[1], grads[2], grads[3])
        big = tuple((a + b for a, b in zip(big, reduced)))
        return ((big, small_acc + grads[4], loss_acc + loss_part), None)

    start_carry = (big_zero, jnp.zeros(small.shape, jnp.float32), jnp.float32(0.0))
    (big, small_acc, loss_acc), _ = lax.scan(
        micro_step, start_carry, (pixels, masks, valid_float, labels)
    )
    big = owner_layout(
        (
            lax.psum_scatter(big[0], ("dp", "head"), scatter_dimension=1, tiled=True),
            lax.psum_scatter(big[1], ("dp", "head"), scatter_dimension=1, tiled=True),
            lax.psum_scatter(big[2], ("dp", "head"), scatter_dimension=1, tiled=True),
            lax.psum_scatter(big[3], ("dp", "head"), scatter_dimension=1, tiled=True),
        )
    )
    small_total, loss_sum, count = lax.psum(
        (small_acc, loss_acc * head_first, jnp.sum(valid_float) * head_first), ("dp", "head")
    )
    count = jnp.maximum(count, 1.0)
    latent_rate = LATENTS * math.sqrt(D * MICRO * IMG_DEV * lax.axis_size("dp")) / 32.0
    rates = (LEARN_RATE, LEARN_RATE, LEARN_RATE, latent_rate, LEARN_RATE)
    results = [loss_sum, count]
    params = (square, kv_weight, head_weight, latents, small)
    moms = (square_mom, kv_mom, head_mom, latent_mom, small_mom)
    avgs = (square_avg, kv_avg, head_avg, latent_avg, small_avg)
    for weight, grad, mom, avg, rate in zip(params, tuple(big) + (small_total,), moms, avgs, rates):
        results.extend(nesterov(weight, grad, mom, avg, rate))
    return tuple(results)


class Names:
    def __getattr__(self, name):
        return name


N = Names()


MESH=pl.DeviceIdType.MESH
MB=1<<20

def where_am_i():
    dp=lax.axis_index(N.dp); h=lax.axis_index(N.head)
    return dict(dp=dp,h=h,z=dp//2,y=dp%2,x=h//2,c=h%2)

def neighbours(me):
    return dict(zu=(me[N.dp]+2,me[N.h]),zd=(me[N.dp]-2,me[N.h]),y=(me[N.dp]+1-2*me[N.y],me[N.h]),
                x=(me[N.dp],me[N.h]+2-4*me[N.x]),c=(me[N.dp],me[N.h]+1-2*me[N.c]))

def entry_barrier(me,nb,others=()):
    z=me[N.z]
    bar=pltpu.get_barrier_semaphore()
    for k in (N.x,N.y,N.c):
        pl.semaphore_signal(bar,inc=1,device_id=nb[k],device_id_type=MESH)
    @pl.when(z<3)
    def _(): pl.semaphore_signal(bar,inc=1,device_id=nb[N.zu],device_id_type=MESH)
    @pl.when(z>0)
    def _(): pl.semaphore_signal(bar,inc=1,device_id=nb[N.zd],device_id_type=MESH)
    for other in others:
        pl.semaphore_signal(bar,inc=1,device_id=other,device_id_type=MESH)
    pl.semaphore_wait(bar,4+(z+1)//2%2+len(others))

class Gather:
    def __init__(self,me,nb,buf,groups,ssem,rsem):
        self.me,self.nb,self.buf,self.groups,self.ssem,self.rsem=me,nb,buf,groups,ssem,rsem
        self.pending=[]
    def copy(self,src,dst,slot,dev):
        return pltpu.make_async_remote_copy(src_ref=src,dst_ref=dst,send_sem=self.ssem.at[slot],recv_sem=self.rsem.at[slot],device_id=dev,device_id_type=MESH)
    def view(self,r,*ix):
        return self.buf.at[(*ix,slice(None),pl.ds(*self.groups[r]))]
    def hop(self,r,k,op):
        z,y,x,c=(self.me[i] for i in N.zyxc)
        rest=(y,x,c) if r<2 else (slice(None),slice(None),c)
        su,sd=8*r+k-1,8*r+3+k-1
        if op==N.start:
            @pl.when((z<3)&(z>=k-1))
            def _():
                v=self.view(r,z-(k-1),*rest); self.copy(v,v,su,self.nb[N.zu]).start()
            @pl.when((z>0)&(z+k-1<=3))
            def _():
                v=self.view(r,z+(k-1),*rest); self.copy(v,v,sd,self.nb[N.zd]).start()
        elif op==N.recv:
            @pl.when(z>=k)
            def _():
                v=self.view(r,z-k,*rest); self.copy(v,v,su,self.nb[N.zd]).wait_recv()
            @pl.when(z+k<=3)
            def _():
                v=self.view(r,z+k,*rest); self.copy(v,v,sd,self.nb[N.zu]).wait_recv()
        else:
            @pl.when((z<3)&(z>=k-1))
            def _():
                v=self.view(r,z-(k-1),*rest); self.copy(v,v,su,self.nb[N.zu]).wait_send()
            @pl.when((z>0)&(z+k-1<=3))
            def _():
                v=self.view(r,z+(k-1),*rest); self.copy(v,v,sd,self.nb[N.zd]).wait_send()
    def flat(self,r,axis,op):
        z,y,x,c=(self.me[i] for i in N.zyxc)
        A=slice(None)
        if axis==N.y:
            mine={0:(A,y,x,c),1:(A,y,A,c),2:(z,y,A,c)}[r]; other={0:(A,1-y,x,c),1:(A,1-y,A,c),2:(z,1-y,A,c)}[r]; slot=8*r+6
        elif axis==N.x:
            mine={0:(A,A,x,c),1:(A,y,x,c),2:(z,y,x,c)}[r]; other={0:(A,A,1-x,c),1:(A,y,1-x,c),2:(z,y,1-x,c)}[r]; slot=8*r+7
        if op==N.start:
            v=self.view(r,*mine); self.copy(v,v,slot,self.nb[axis]).start()
        elif op==N.recv:
            v=self.view(r,*other); self.copy(v,v,slot,self.nb[axis]).wait_recv()
        else:
            v=self.view(r,*mine); self.copy(v,v,slot,self.nb[axis]).wait_send()
    def core(self,op):
        c=self.me[N.c]; A=slice(None)
        if op==N.recv:
            v=self.buf.at[A,A,A,1-c]; self.copy(v,v,24,self.nb[N.c]).wait_recv()
        else:
            v=self.buf.at[A,A,A,c]; d=self.copy(v,v,24,self.nb[N.c])
            d.start() if op==N.start else d.wait_send()
    ORDER=[[N.h1,N.h2,N.h3,N.y,N.x],[N.h1,N.h2,N.h3,N.x,N.y],[N.x,N.y,N.h1,N.h2,N.h3]]
    def do(self,r,p,op):
        n=self.ORDER[r][p]
        if n[0]==N.h: self.hop(r,int(n[1]),op)
        else: self.flat(r,n,op)
    NPH=6
    def phase(self,p):
        if p>0 and p<=5:
            for r in range(3):
                if self.groups[r][1]: self.do(r,p-1,N.recv)
                if p<5 and self.groups[r][1]: self.do(r,p,N.start)
        if p==0:
            for r in range(3):
                if self.groups[r][1]: self.do(r,0,N.start)
        if p==5: self.core(N.start)
        if p==6: self.core(N.recv)
    def sends(self):
        for r in range(3):
            if self.groups[r][1]:
                for p in range(5): self.do(r,p,N.send)
        self.core(N.send)

SPLIT={1024:((0,384),(384,384),(768,256)),512:((0,128),(128,256),(384,128)),384:((0,128),(128,128),(256,128))}


ALLS=slice(None)

def recv_shapes(r,n):
    (_,a),(_,b),(_,c)=SPLIT[n]
    return dict(core=(4,2,2,r,n),A0=(4,2,r,a),A1=(4,r,a),Ah=(6,r,a),B0=(4,2,r,b),B1=(4,r,b),Bh=(6,r,b),Ch=(6,2,2,r,c),C0=(2,r,c),C1=(r,c))
RNAMES=(N.core,N.A0,N.A1,N.Ah,N.B0,N.B1,N.Bh,N.Ch,N.C0,N.C1)

def add_into(dst,src,cols,lead):
    for di,si in lead:
        dst[(*di,ALLS,cols)]=dst[(*di,ALLS,cols)]+src[si]

class Scatter:
    def __init__(self,me,nb,part,send_half,bufs,out,groups,ssem,rsem):
        self.me,self.nb,self.part,self.half,self.b,self.out,self.groups,self.ssem,self.rsem=me,nb,part,send_half,bufs,out,groups,ssem,rsem
    def copy(self,src,dst,slot,dev):
        return pltpu.make_async_remote_copy(src_ref=src,dst_ref=dst,send_sem=self.ssem.at[slot],recv_sem=self.rsem.at[slot],device_id=dev,device_id_type=MESH)
    def cols(self,r): return pl.ds(*self.groups[r])
    def hop(self,r,k,op):
        z,y,x=(self.me[i] for i in N.zyx)
        rest=(y,x) if r<2 else (ALLS,ALLS)
        buf=self.b[N.ABC[r]+N.h]; cols=self.cols(r)
        su,sd=8*r+k-1,8*r+3+k-1
        up=lambda: self.copy(self.part.at[(z+k,*rest,ALLS,cols)],buf.at[k-1],su,self.nb[N.zu])
        dn=lambda: self.copy(self.part.at[(z-k,*rest,ALLS,cols)],buf.at[3+k-1],sd,self.nb[N.zd])
        if op in(N.start,N.send):
            @pl.when(z+k<=3)
            def _():
                d=up(); d.start() if op==N.start else d.wait_send()
            @pl.when(z-k>=0)
            def _():
                d=dn(); d.start() if op==N.start else d.wait_send()
        else:
            last=(k==1 and r<2)
            @pl.when((z>=1)&(z-1+k<=3))
            def _():
                self.copy(buf.at[k-1],buf.at[k-1],su,self.nb[N.zd]).wait_recv()
                self.hopadd(r,z-1+k,buf.at[k-1],cols)
            @pl.when((z<=2)&(z+1-k>=0))
            def _():
                self.copy(buf.at[3+k-1],buf.at[3+k-1],sd,self.nb[N.zu]).wait_recv()
                self.hopadd(r,z+1-k,buf.at[3+k-1],cols)
    def hopadd(self,r,d,src,cols):
        y,x=self.me[N.y],self.me[N.x]
        if r<2: add_into(self.part,src,cols,[((d,y,x),(ALLS,ALLS))])
        else: add_into(self.part,src,cols,[((d,i,j),(i,j)) for i in range(2) for j in range(2)])
    def flat(self,r,axis,op):
        z,y,x=(self.me[i] for i in N.zyx); cols=self.cols(r)
        name=N.ABC[r]
        if axis==N.x:
            mine={0:(ALLS,ALLS,1-x),1:(ALLS,y,1-x),2:(z,y,1-x)}[r]; slot=8*r+7; buf=self.b[{0:N.A0,1:N.B1,2:N.C1}[r]]
        else:
            mine={0:(ALLS,1-y,x),1:(ALLS,1-y),2:(z,1-y)}[r]; slot=8*r+6; buf=self.b[{0:N.A1,1:N.B0,2:N.C0}[r]]
        if op==N.recv:
            self.copy(buf,buf,slot,self.nb[axis]).wait_recv()
            if axis==N.x:
                lead={0:[((i,j,x),(i,j)) for i in range(4) for j in range(2)],1:[((i,y,x),(i,)) for i in range(4)],2:[((z,y,x),(ALLS,ALLS))]}[r]
            else:
                lead={0:[((i,y,x),(i,)) for i in range(4)],1:[((i,y,j),(i,j)) for i in range(4) for j in range(2)],2:[((z,y,j),(j,)) for j in range(2)]}[r]
            add_into(self.part,buf,cols,lead)
        else:
            d=self.copy(self.part.at[(*mine,)+(ALLS,)*(4-len(mine))+(cols,)],buf,slot,self.nb[axis])
            d.start() if op==N.start else d.wait_send()
    def core(self,op):
        buf=self.b[N.core]
        if op==N.recv:
            self.copy(buf,buf,24,self.nb[N.c]).wait_recv()
            @pl.loop(0,4)
            def _(i):
                for j in range(2):
                    for k in range(2):
                        self.part[i,j,k]=self.part[i,j,k]+buf[i,j,k]
        else:
            d=self.copy(self.half,buf,24,self.nb[N.c]); d.start() if op==N.start else d.wait_send()
    ORDER=[[N.x,N.y,N.h3,N.h2,N.h1],[N.y,N.x,N.h3,N.h2,N.h1],[N.h3,N.h2,N.h1,N.y,N.x]]
    def do(self,r,p,op):
        n=self.ORDER[r][p]
        if n[0]==N.h: self.hop(r,int(n[1]),op)
        else: self.flat(r,n,op)
    def phase(self,p):
        if p==0: self.core(N.start); return
        if p==1: self.core(N.recv)
        for r in range(3):
            if p>=2: self.do(r,p-2,N.recv)
            if p<=5: self.do(r,p-1,N.start)
        if p==6:
            z,y,x=(self.me[i] for i in N.zyx)
            if self.out is not None: self.out[...]=self.part[z,y,x].astype(jnp.float32)
    def sends(self):
        self.core(N.send)
        for r in range(3):
            for p in range(5): self.do(r,p,N.send)

def small_steps(me):
    dp,h=me[N.dp],me[N.h]
    z=me[N.z]
    return [(dp,h+1-2*me[N.c]),(dp,h+2-4*me[N.x]),(dp+1-2*me[N.y],h),(dp+2-4*(z%2),h),(dp+4-8*(z//2),h)]


BF=jnp.bfloat16; F32=jnp.float32
PADC=384
NN=(((1,),(0,)),((),())); NT=(((1,),(1,)),((),())); TN=(((0,),(0,)),((),()))
def dot(a,b,dims=NN): return lax.dot_general(a,b,dims,preferred_element_type=F32)
ROWS=512; TILE=512; RB=128

def norm_rows(load,gain,xhat,rstd,normed,width=D,store_sum=None):
    def body(i,tot):
        rows=pl.ds(i*RB,RB)
        v=load(rows)
        mean=jnp.sum(v,-1,keepdims=True)/width
        cent=v-mean
        var=jnp.sum(cent*cent,-1,keepdims=True)/width
        r=lax.rsqrt(var+1e-5)
        xh=cent*r
        lanes=pl.ds(0,width)
        xhat[rows,lanes]=xh.astype(BF)
        if rstd is not None: rstd[rows]=jnp.broadcast_to(r,(RB,128))
        if normed is not None: normed[rows,lanes]=(xh*gain).astype(BF)
        if tot is None: return None
        return tot+jnp.sum(xh,0,keepdims=True)
    tot=jnp.zeros((1,D),F32) if store_sum else None
    for i in range(ROWS//RB): tot=body(i,tot)
    return tot

def mm(lhs,w,epi):
    for j in range(D//TILE):
        cols=pl.ds(j*TILE,TILE)
        epi(cols,dot(lhs[...],w[:,:,:,:,:,cols].reshape(D,TILE)))

def gelu_pair(v):
    k=math.sqrt(2/math.pi)
    v2=v*v
    t=jnp.tanh(k*v*(1+0.044715*v2))
    h=0.5*(1+t)
    return v*h, h+0.5*v*(1-t*t)*(k*(1+3*0.044715*v2))

SAVED=dict(xb=((512,PADC),BF),xhp=((512,PADC),BF),kv=((512,2048),BF),q=((512,D),BF),qn=((512,D),BF),
  xh0=((512,D),BF),p=((512,512),BF),o=((512,D),BF),
  xh1=((512,D),BF),n1=((512,D),BF),a1=((512,D),BF),dg1=((512,D),BF),
  xh2=((512,D),BF),n2=((512,D),BF),qkv=((3,512,D),BF),ph=((8,512,512),BF),so=((512,D),BF),
  xh3=((512,D),BF),n3=((512,D),BF),a2=((512,D),BF),dg2=((512,D),BF),xh4=((512,D),BF),
  rs0=((512,128),F32),rs1=((512,128),F32),rs2=((512,128),F32),rs3=((512,128),F32),rs4=((512,128),F32))
NAMES=list(SAVED)
TENS=[N.lat,N.kvw]+[(N.w+str(i)) for i in range(8)]+[N.head,N.w8,N.w9]
def tshape(n): return {N.lat:(32,512),N.kvw:(64,PADC)}.get(n,(32,1024))

def forward_kernel(comm,gap,*refs):
    refs=list(refs)
    nt=len(TENS)
    square,kvw,hw_own,lat_own,pixels,masks,valids,labels,aux=[refs.pop(0) for _ in range(9)]
    whole=[refs.pop(0) for _ in range(nt)]
    out={n:refs.pop(0) for n in NAMES}
    vec,tail=refs.pop(0),refs.pop(0)
    bufs=[refs.pop(0) for _ in range(nt)]
    s={n:refs.pop(0) for n in NAMES}
    z,h,pix,ssem,rsem,wsem,osem,psend,precv=refs
    me=where_am_i(); nb=neighbours(me)
    zz,yy,xx,cc=(me[i] for i in N.zyxc)
    micro=me[N.h]
    classes=hw_own.shape[1]
    own={n:bufs[TENS.index(n)].at[zz,yy,xx,cc] for n in TENS}
    own[N.lat][...]=lat_own[...].astype(BF)
    own[N.kvw][...]=jnp.zeros((64,PADC),BF)
    own[N.kvw][:,0:CIN]=kvw[...].astype(BF)
    own[N.head][...]=jnp.zeros((32,D),BF)
    own[N.head][:,0:classes]=hw_own[...].astype(BF)
    for i in range(10): own[(N.w+str(i))][...]=square[i].astype(BF)
    for m in (N.xb,N.xhp): s[m][...]=jnp.zeros_like(s[m])
    ev=[]
    ready={}
    if comm:
        dp_,h_=me[N.dp],me[N.h]
        diag=(dp_,(h_+1-2*cc)+2-4*xx)
        entry_barrier(me,nb,[diag])
        peers=[nb[N.c],nb[N.x],diag]
        swaps=[pltpu.make_async_remote_copy(src_ref=pixels.at[p[1],0],dst_ref=pix.at[pl.ds(pl.multiple_of(micro*128,128),128)],send_sem=psend.at[i],recv_sem=precv.at[i],device_id=p,device_id_type=MESH) for i,p in enumerate(peers)]
        for k in swaps: k.start()
        keep_own=pltpu.make_async_copy(pixels.at[micro,0],pix.at[pl.ds(pl.multiple_of(micro*128,128),128)],psend.at[3])
        keep_own.start()
        gs=[Gather(me,nb,b,SPLIT[b.shape[-1]],ssem.at[i],rsem.at[i]) for i,b in enumerate(bufs)]
        for tick in range(nt+6*gap):
            for t in range(nt):
                p=tick-t
                if p>=0 and p%gap==0 and p//gap<=6:
                    ev.append(functools.partial(gs[t].phase,p//gap))
                    if p//gap==6: ready[t]=len(ev)
    else:
        for t in range(nt): ready[t]=0
    pos=[0]
    def pump(k):
        for e in ev[pos[0]:pos[0]+k]: e()
        pos[0]=min(pos[0]+k,len(ev))
    outs=[]
    def weight(name):
        t=TENS.index(name)
        if pos[0]<ready[t]: pump(ready[t]-pos[0])
        if name not in(N.lat,N.head):
            c=pltpu.make_async_copy(bufs[t],whole[t],wsem.at[t]); c.start(); outs.append(c)
        return bufs[t]
    def keep(*names):
        for m in names:
            c=pltpu.make_async_copy(s[m],out[m],osem.at[NAMES.index(m)]); c.start(); outs.append(c)
    gain=lambda i: aux[i:i+1,:]
    pump(14)
    if comm:
        keep_own.wait()
        for i,p in enumerate(peers):
            got=pix.at[pl.ds(pl.multiple_of(p[1]*128,128),128)]
            pltpu.make_async_remote_copy(src_ref=got,dst_ref=got,send_sem=psend.at[0],recv_sem=precv.at[i],device_id=p,device_id_type=MESH).wait_recv()
    norm_rows(lambda r: pix[r].astype(F32),aux[5:6,0:CIN],s[N.xhp],None,s[N.xb],width=CIN)
    keep(N.xb,N.xhp)
    lt=weight(N.lat)
    @pl.loop(0,8)
    def _(i):
        z[:,pl.ds(pl.multiple_of(i*128,128),128)]=lt[i//2,i%2].reshape(128,ROWS).T
    pump(3)
    norm_rows(lambda r: z[r].astype(F32),gain(0),s[N.xh0],s[N.rs0],s[N.qn])
    keep(N.qn,N.xh0,N.rs0)
    kt=weight(N.kvw)
    for j in range(4):
        rows=kt[j].reshape(512,PADC)
        s[N.kv][:,j*512:(j+1)*512]=dot(s[N.xb][...],rows,NT).astype(BF)
    keep(N.kv)
    pump(3)
    w=weight(N.w0)
    def epi(cols,acc): s[N.q][:,cols]=acc.astype(BF)
    mm(s[N.qn],w,epi)
    keep(N.q)
    pump(3)
    for i in range(2):
        rows=pl.ds(i*256,256)
        sc=dot(s[N.q][rows],s[N.kv][:,:D],NT)*(1/32)
        sc=jnp.where(masks[micro]>0,sc,-1e30)
        e=jnp.exp(sc-jnp.max(sc,-1,keepdims=True))
        p=(e*(1/jnp.sum(e,-1,keepdims=True))).astype(BF)
        s[N.p][rows]=p
        s[N.o][rows]=dot(p,s[N.kv][:,D:]).astype(BF)
    pump(2)
    keep(N.p,N.o)
    w=weight(N.w1)
    def epi(cols,acc): h[:,cols]=z[:,cols].astype(F32)+acc
    mm(s[N.o],w,epi)
    pump(3)
    norm_rows(lambda r: h[r],gain(1),s[N.xh1],s[N.rs1],s[N.n1])
    keep(N.xh1,N.rs1,N.n1)
    def addh(cols,acc): h[:,cols]=h[:,cols]+acc
    def mlp(wi,wo,nn,dg,act):
        w=weight(wi)
        def epi(cols,acc):
            a,d=gelu_pair(acc)
            s[act][:,cols]=a.astype(BF); s[dg][:,cols]=d.astype(BF)
        mm(s[nn],w,epi)
        keep(dg,act)
        pump(3)
        w=weight(wo)
        mm(s[act],w,addh)
    mlp(N.w2,N.w3,N.n1,N.dg1,N.a1)
    pump(3)
    norm_rows(lambda r: h[r],gain(2),s[N.xh2],s[N.rs2],s[N.n2])
    keep(N.xh2,N.rs2,N.n2)
    for i in range(3):
        w=weight((N.w+str(4+i)))
        def epi(cols,acc,i=i): s[N.qkv][i,:,cols]=acc.astype(BF)
        mm(s[N.n2],w,epi)
        pump(2)
    keep(N.qkv)
    for i in range(8):
        cols=pl.ds(i*128,128)
        sc=dot(s[N.qkv][0,:,cols],s[N.qkv][1,:,cols],NT)*(128**-0.5)
        e=jnp.exp(sc-jnp.max(sc,-1,keepdims=True))
        p=(e*(1/jnp.sum(e,-1,keepdims=True))).astype(BF)
        s[N.ph][i]=p
        s[N.so][:,cols]=dot(p,s[N.qkv][2,:,cols]).astype(BF)
        if i%4==3: pump(2)
    keep(N.ph,N.so)
    w=weight(N.w7)
    mm(s[N.so],w,addh)
    pump(3)
    norm_rows(lambda r: h[r],gain(3),s[N.xh3],s[N.rs3],s[N.n3])
    keep(N.xh3,N.rs3,N.n3)
    mlp(N.w8,N.w9,N.n3,N.dg2,N.a2)
    tot=norm_rows(lambda r: h[r],gain(4),s[N.xh4],s[N.rs4],None,store_sum=True)
    keep(N.xh4,N.rs4)
    pooled=(tot*gain(4)/ROWS).astype(BF)
    hw=weight(N.head)
    lane=lax.broadcasted_iota(jnp.int32,(1,D),1)
    turned=pltpu.roll(aux[...],D-CIN,1)
    bias=jnp.where(lane<D-CIN,turned[5:6],turned[6:7])
    logits=dot(jnp.broadcast_to(pooled,(16,D)),hw[...].reshape(D,D))[0:1]+bias
    logits=jnp.where(lane<classes,logits,-1e30)
    mx=jnp.max(logits,-1,keepdims=True)
    logp=logits-mx-jnp.log(jnp.sum(jnp.exp(logits-mx),-1,keepdims=True))
    target=jnp.where(lane<classes,jnp.where(lane==labels[0,micro],1.0-SMOOTH,0.0)+SMOOTH/classes,0.0)
    valid=jnp.full((1,D),valids[0,micro].astype(F32))
    loss=-valid*jnp.sum(target*logp,-1,keepdims=True)
    dl=valid*(jnp.exp(logp)-target)
    hi=dl.astype(BF); lo=(dl-hi.astype(F32)).astype(BF)
    dp=dot(jnp.concatenate([jnp.broadcast_to(hi,(16,D)),jnp.broadcast_to(lo,(16,D))],0),hw[...].reshape(D,D),NT)
    pf=pooled.astype(F32)
    shown=jnp.where(lane==classes,valid,dl)
    for i in range(4):
        vec[i:i+1]=pf[:,i*256:(i+1)*256]; vec[4+i:5+i]=shown[:,i*256:(i+1)*256]
    tail[0:1]=dp[0:1]+dp[16:17]; tail[1:2]=dl
    tail[2:3]=jnp.where(lane==0,loss,jnp.where(lane==1,valid,0.0))
    tail[3:4]=tot; tail[4:8]=jnp.zeros((4,D),F32)
    pump(len(ev))
    for c in outs: c.wait()
    if comm:
        for k in swaps: k.wait_send()
        for g in gs: g.sends()

def forward_all(square,kvw,head,lat,pixels,masks,valid,labels,aux,cid=0,comm=True,gap=2):
    nt=len(TENS)
    A=pl.BlockSpec(memory_space=pl.ANY); V=pl.BlockSpec(memory_space=pltpu.VMEM); S=pl.BlockSpec(memory_space=pltpu.SMEM)
    whole=[(4,2,2,2)+tshape(n) for n in TENS]
    outs=[jax.ShapeDtypeStruct(w,BF) for w in whole]
    outs+=[jax.ShapeDtypeStruct(*SAVED[m]) for m in NAMES]+[jax.ShapeDtypeStruct((8,256),F32),jax.ShapeDtypeStruct((8,D),F32)]
    DS=pltpu.SemaphoreType.DMA
    scr=[pltpu.VMEM(w,BF) for w in whole]+[pltpu.VMEM(*SAVED[m]) for m in NAMES]
    scr+=[pltpu.VMEM((512,D),BF),pltpu.VMEM((512,D),F32),pltpu.VMEM((512,CIN),BF),
          DS((nt,25)),DS((nt,25)),DS((nt,)),DS((len(NAMES),)),DS((4,)),DS((3,))]
    cp=dict(has_side_effects=True,vmem_limit_bytes=63*MB)
    if comm: cp.update(collective_id=cid)
    r=pl.pallas_call(functools.partial(forward_kernel,comm,gap),out_shape=outs,
        in_specs=[V]*4+[A,V,S,S,V],out_specs=[A]*(nt+len(NAMES))+[V,V],scratch_shapes=scr,
        compiler_params=pltpu.CompilerParams(**cp))(square,kvw,head,lat,pixels,masks,valid,labels,aux)
    return dict(zip(TENS,r[:nt])),dict(zip(NAMES,r[nt:-2])),r[-2],r[-1]


GRADS=[N.w9,N.w8,N.w7,N.w4,N.w5,N.w6,N.w3,N.w2,N.w1,N.w0,N.kvw,N.lat]
WORDER=[N.w9,N.w8,N.w7,N.w4,N.w5,N.w6,N.w3,N.w2,N.w1,N.w0,N.kvw]
NEEDED=[N.a2,N.dg2,N.n3,N.xh3,N.rs3,N.so,N.ph,N.qkv,N.n2,N.xh2,N.rs2,N.a1,N.dg1,N.n1,N.xh1,N.rs1,N.o,N.p,N.kv,N.q,N.xb,N.xhp,N.qn,N.xh0,N.rs0,N.xh4,N.rs4]
def gshape(n): return {N.lat:(32,512),N.kvw:(64,PADC)}.get(n,(32,D))
RING=4; SRING=2; GAP=2


def backward_kernel(comm,classes,*refs):
    refs=list(refs)
    wt={n:refs.pop(0) for n in WORDER}
    sv={n:refs.pop(0) for n in NEEDED}
    vec,tail,aux=[refs.pop(0) for _ in range(3)]
    sq_out=refs.pop(0)
    kv_out,lat_out,vec_out,small_out=[refs.pop(0) for _ in range(4)]
    nt=len(GRADS)
    part=[refs.pop(0) for _ in range(nt)]
    send_ring=[refs.pop(0) for _ in range(SRING)]; send_kv,send_lat=refs.pop(0),refs.pop(0)
    core_ring=[refs.pop(0) for _ in range(RING)]; core_kv,core_lat=refs.pop(0),refs.pop(0)
    rbuf=[{k:refs.pop(0) for k in RNAMES[1:]} for _ in range(nt)]
    wslot=[refs.pop(0) for _ in range(2)]; kslot=refs.pop(0)
    aslot=[refs.pop(0) for _ in range(2)]; xslot,rslot=refs.pop(0),refs.pop(0)
    gslot,hslot,qkvslot,xbslot,xhpslot=[refs.pop(0) for _ in range(5)]
    dh,dn,g,dp,dqkv=[refs.pop(0) for _ in range(5)]
    vbuf,srecv,ssend=[refs.pop(0) for _ in range(3)]
    wsem,asem,hsem,ssem,rsem,vs,vr,sms,smr,usem=refs
    me=where_am_i(); nb=neighbours(me)
    z,y,x,c=(me[i] for i in N.zyxc)
    first=c==0
    A=[N.a2,N.n3,N.so,N.n2,N.a1,N.n1,N.o,N.qn]
    X=[N.xh4,N.xh3,N.xh2,N.xh1,N.xh0]; R=[N.rs4,N.rs3,N.rs2,N.rs1,N.rs0]
    place={n:aslot[i%2] for i,n in enumerate(A)}
    place.update({n:xslot for n in X}); place.update({n:rslot for n in R})
    place.update(dg2=gslot,dg1=gslot,p=hslot.at[1],qkv=qkvslot,xb=xbslot,xhp=xhpslot)
    wi=[n for n in WORDER if n!=N.kvw]
    place.update({n:wslot[i%2] for i,n in enumerate(wi)}); place[N.kvw]=kslot
    live={}
    def load(*names):
        for n in names:
            if n in WORDER: cs=[pltpu.make_async_copy(wt[n],place[n],wsem.at[WORDER.index(n)])]
            elif n==N.kv:
                cs=[pltpu.make_async_copy(sv[n].at[:,pl.ds(0,D)],qkvslot.at[1],asem.at[NEEDED.index(n)]),
                    pltpu.make_async_copy(sv[n].at[:,pl.ds(D,D)],qkvslot.at[2],asem.at[len(NEEDED)])]
            elif n==N.q: cs=[pltpu.make_async_copy(sv[n],qkvslot.at[0],asem.at[NEEDED.index(n)])]
            else: cs=[pltpu.make_async_copy(sv[n],place[n],asem.at[NEEDED.index(n)])]
            for k in cs: k.start()
            live[n]=cs
    def use(n):
        for k in live.pop(n): k.wait()
        return place.get(n)
    def load_head(i):
        k=pltpu.make_async_copy(sv[N.ph].at[i],hslot.at[i%2],hsem.at[i]); k.start(); live[(N.ph+str(i))]=[k]
    load(N.xh4,N.rs4,N.w9,N.a2,N.dg2,N.w8,N.n3,N.qkv)
    for i in range(2): load_head(i)
    vbuf[z,y,x,c]=vec[...]
    if comm: entry_barrier(me,nb,small_steps(me)[4:])
    gs=[]
    rings={}
    for t,n in enumerate(GRADS):
        if n==N.kvw: sb,cb=send_kv,core_kv
        elif n==N.lat: sb,cb=send_lat,core_lat
        else:
            k=wi.index(n); sb,cb=send_ring[k%SRING],core_ring[k%RING]
        out={N.kvw:kv_out,N.lat:lat_out}.get(n)
        gs.append(Scatter(me,nb,part[t],sb,dict(rbuf[t],core=cb),out,SPLIT[gshape(n)[1]],ssem.at[t],rsem.at[t]))
    gv=Gather(me,nb,vbuf,[(0,0),(0,0),(0,vbuf.shape[-1])],vs,vr)
    queue={}
    for tick in range(nt+6*GAP+1):
        q=[]
        if tick%2==0 and tick//2<=6: q.append(functools.partial(gv.phase,tick//2))
        for t in range(nt):
            p=tick-t
            if p>0 and p%GAP==0 and p//GAP<=6: q.append(functools.partial(gs[t].phase,p//GAP))
        queue[tick]=q
    now=[0]
    def pump(k):
        if not comm: return
        for _ in range(k):
            if queue[now[0]]: queue[now[0]].pop(0)()
    waited=set()
    def before_store(n):
        if n in wi and wi.index(n)>=SRING and comm:
            o=GRADS.index(wi[wi.index(n)-SRING]); gs[o].core(N.send); waited.add(o)
    def push(n):
        if not comm: return
        pump(len(queue[now[0]]))
        assert GRADS[now[0]]==n
        gs[now[0]].phase(0)
        now[0]+=1
    def store(n,v,r0,cols):
        t=GRADS.index(n); r=gshape(n)[0]; k=v.shape[0]//(2*r)
        v=v.astype(BF).reshape(k,2,r,v.shape[1])
        own=jnp.where(first,v[:,0],v[:,1]); other=jnp.where(first,v[:,1],v[:,0])
        b0=r0//(2*r)
        for ref,val in ((part[t],own),(gs[t].half,other)):
            if k==16: ref[:,:,:,:,cols]=val.reshape(4,2,2,r,v.shape[-1])
            elif k>=4: ref[b0//4:(b0+k)//4,:,:,:,cols]=val.reshape(k//4,2,2,r,v.shape[-1])
            else: ref[b0//4,(b0%4)//2,:,:,cols]=val.reshape(2,r,v.shape[-1])
    def weight_grad(n,a,dy):
        before_store(n)
        for j in range(2):
            cols=pl.ds(j*512,512)
            store(n,dot(a[...],dy[:,cols],TN),0,cols)
            pump(1)
        push(n)
    def back(dy,w,epi):
        for j in range(2):
            rows=w[2*j:2*j+2].reshape(512,D)
            epi(pl.ds(j*512,512),dot(dy[...],rows,NT))
            pump(1)
    gain=lambda i: aux[i:i+1,:]
    def norm_back(load_dn,gn,xh,rs,base,store_to):
        def body(i,tot):
            rows=pl.ds(i*RB,RB)
            d=load_dn(rows); xv=xh[rows].astype(F32)
            dx=d*gn
            m1=jnp.sum(dx,-1,keepdims=True)/D; m2=jnp.sum(dx*xv,-1,keepdims=True)/D
            r=rs[rows][:,0:1]*(dx-m1-xv*m2)
            if base is not None: r=r+base[rows]
            store_to(rows,r)
            return tot+jnp.sum(d*xv,0,keepdims=True)
        tot=jnp.zeros((1,D),F32)
        for i in range(ROWS//RB): tot=body(i,tot)
        return tot
    def to_dh(rows,r):
        dh[rows]=r; g[rows]=r.astype(BF)
    def to_dn(cols,acc): dn[:,cols]=acc
    def to_dp(cols,acc): dp[:,cols]=acc.astype(BF)
    small=ssend.at[0]
    const=tail[0:1]*(1/ROWS)
    use(N.rs4)
    dg=norm_back(lambda r: jnp.broadcast_to(const,(RB,D)),gain(4),use(N.xh4),place[N.rs4],None,to_dh)
    small[4:5]=dg
    small[5:8]=jnp.zeros((3,D),F32)
    lane=lax.broadcasted_iota(jnp.int32,(1,D),1)
    turned=pltpu.roll(tail[...],CIN,1)[1:2]
    small[6:7]=jnp.where(lane<classes-(D-CIN),turned,0.0)
    small[7:8]=tail[2:3]
    load(N.xh3,N.rs3)
    def mlp_back(wo,wi_,act,normed,dgn,xh,rs,row,nxt):
        a=use(act)
        weight_grad(wo,a,g)
        load(*nxt[0])
        w=use(wo); d=use(dgn)
        def epi(cols,acc): dp[:,cols]=(acc*d[:,cols].astype(F32)).astype(BF)
        back(g,w,epi)
        load(*nxt[1])
        weight_grad(wi_,use(normed),dp)
        load(*nxt[2])
        back(dp,use(wi_),to_dn)
        load(*nxt[3])
        use(rs)
        small[row:row+1]=norm_back(lambda r: dn[r],gain(row),use(xh),place[rs],dh,to_dh)
    mlp_back(N.w9,N.w8,N.a2,N.n3,N.dg2,N.xh3,N.rs3,3,([ N.so],[N.w7,N.dg1],[N.n2],[N.w4]))
    load(N.xh2,N.rs2)
    weight_grad(N.w7,use(N.so),g)
    load(N.a1)
    back(g,use(N.w7),to_dp)
    load(N.w5)
    use(N.qkv)
    sc=128**-0.5
    for i in range(8):
        cols=pl.ds(i*128,128)
        use((N.ph+str(i))); ph=hslot.at[i%2]
        qh,kh,vh=(qkvslot[k,:,cols] for k in range(3)); do=dp[:,cols]
        pf=ph[...].astype(F32)
        dpr=dot(do,vh,NT)
        ds=(pf*(dpr-jnp.sum(pf*dpr,-1,keepdims=True)/jnp.sum(pf,-1,keepdims=True))).astype(BF)
        dqkv[0,:,cols]=(dot(ds,kh)*sc).astype(BF)
        dqkv[1,:,cols]=(dot(ds,qh,TN)*sc).astype(BF)
        dqkv[2,:,cols]=dot(ph[...],do,TN).astype(BF)
        if i+2<8: load_head(i+2)
        pump(1)
    load(N.q,N.kv,N.p,N.xb,N.xhp)
    n2=use(N.n2)
    for i in range(3):
        weight_grad((N.w+str(4+i)),n2,dqkv.at[i])
        if i==2: load(N.n1)
        if i==0: back(dqkv.at[0],use(N.w4),to_dn)
        else:
            def add_dn(cols,acc): dn[:,cols]=dn[:,cols]+acc
            back(dqkv.at[i],use((N.w+str(4+i))),add_dn)
        load((N.w6,N.w3,N.w2)[i])
    use(N.rs2)
    small[2:3]=norm_back(lambda r: dn[r],gain(2),use(N.xh2),place[N.rs2],dh,to_dh)
    load(N.xh1,N.rs1)
    mlp_back(N.w3,N.w2,N.a1,N.n1,N.dg1,N.xh1,N.rs1,1,([N.o],[N.w1,N.kvw],[N.qn],[N.w0]))
    load(N.xh0,N.rs0)
    weight_grad(N.w1,use(N.o),g)
    back(g,use(N.w1),to_dp)
    use(N.q); use(N.kv); p=use(N.p)
    q,k,v=(qkvslot.at[i] for i in range(3))
    dpr=dot(dp[...],v[...],NT)
    pf=p[...].astype(F32)
    ds=(pf*(dpr-jnp.sum(pf*dpr,-1,keepdims=True)/jnp.sum(pf,-1,keepdims=True))).astype(BF)
    for j in range(2):
        cols=pl.ds(j*512,512)
        dqkv[0,:,cols]=(dot(ds,k[:,cols])*(1/32)).astype(BF)
        pump(1)
    weight_grad(N.w0,use(N.qn),dqkv.at[0])
    for j in range(2):
        cols=pl.ds(j*512,512)
        dqkv[1,:,cols]=(dot(ds,q[:,cols],TN)*(1/32)).astype(BF)
        dqkv[2,:,cols]=dot(p[...],dp[:,cols],TN).astype(BF)
        pump(1)
    xb=use(N.xb)
    for i in (0,1):
        store(N.kvw,dot(dqkv[1+i],xb[...],TN),i*D,pl.ds(0,PADC))
        pump(1)
    push(N.kvw)
    back(dqkv.at[0],use(N.w0),to_dn)
    use(N.rs0)
    def to_h(rows,r): dh[rows]=r
    small[0:1]=norm_back(lambda r: dn[r],gain(0),use(N.xh0),place[N.rs0],dh,to_h)
    for i in range(8):
        store(N.lat,dh[:,i*128:(i+1)*128].T,i*128,pl.ds(0,512))
    push(N.lat)
    kw=use(N.kvw); xp=use(N.xhp)
    dx=dot(dqkv[1],kw[0:2].reshape(D,PADC))+dot(dqkv[2],kw[2:4].reshape(D,PADC))
    dpg=jnp.concatenate([jnp.sum(dx*xp[...].astype(F32),0,keepdims=True),jnp.zeros((1,D-PADC),F32)],1)
    small[5:6]=jnp.where(lane<CIN,dpg,turned)
    if comm:
        sm=[pltpu.make_async_remote_copy(src_ref=ssend.at[i],dst_ref=srecv.at[i],send_sem=sms.at[i],recv_sem=smr.at[i],device_id=q_,device_id_type=MESH) for i,q_ in enumerate(small_steps(me))]
        def small_step(i):
            if i>0:
                sm[i-1].wait_recv()
                r=ssend[i-1]+srecv[i-1]
                if i<5: ssend[i]=r
                else: small_out[...]=r
            if i<5: sm[i].start()
        writes=[]
        step=0
        for tick in range(now[0],nt+6*GAP+1):
            if step<=5: small_step(step); step+=1
            for e in queue[tick]: e()
            t=tick-6*GAP
            if 0<=t<nt and GRADS[t][0]==N.w:
                k=pltpu.make_async_copy(part[t].at[z,y,x],sq_out.at[int(GRADS[t][1])],usem.at[t]); k.start(); writes.append(k)
        while step<=5: small_step(step); step+=1
        for k in writes: k.wait()
        for s_ in sm: s_.wait_send()
        gv.sends()
        for t,s_ in enumerate(gs):
            if t not in waited: s_.core(N.send)
            for r in range(3):
                for ph_ in range(5): s_.do(r,ph_,N.send)
    else:
        small_out[...]=ssend[0]
        kv_out[...]=jnp.zeros_like(kv_out); lat_out[...]=jnp.zeros_like(lat_out)
    vec_out[...]=vbuf[...]

def backward_all(w,sv,vec,tail,aux,classes,cid=1,comm=True):
    A=pl.BlockSpec(memory_space=pl.ANY); V=pl.BlockSpec(memory_space=pltpu.VMEM)
    DS=pltpu.SemaphoreType.DMA
    M=pltpu.VMEM
    nt=len(GRADS)
    outs=[jax.ShapeDtypeStruct((10,32,D),BF)]+[jax.ShapeDtypeStruct((64,PADC),F32),jax.ShapeDtypeStruct((32,512),F32),
          jax.ShapeDtypeStruct((4,2,2,2,8,256),F32),jax.ShapeDtypeStruct((8,D),F32)]
    scr=[M((4,2,2)+gshape(n),BF) for n in GRADS]
    half=lambda n: M((4,2,2)+gshape(n),BF)
    scr+=[half(N.w0)]*SRING+[half(N.kvw),half(N.lat)]+[half(N.w0)]*RING+[half(N.kvw),half(N.lat)]
    for n in GRADS:
        sh=recv_shapes(*gshape(n)); scr+=[M(sh[k],BF) for k in RNAMES[1:]]
    scr+=[M((4,2,2,2,32,D),BF)]*2+[M((4,2,2,2,64,PADC),BF)]
    scr+=[M((512,D),BF)]*3+[M((512,128),F32)]
    scr+=[M((512,D),BF),M((2,512,512),BF),M((3,512,D),BF),M((512,PADC),BF),M((512,PADC),BF)]
    scr+=[M((512,D),F32),M((512,D),F32),M((512,D),BF),M((512,D),BF),M((3,512,D),BF)]
    scr+=[M((4,2,2,2,8,256),F32),M((5,8,D),F32),M((5,8,D),F32)]
    scr+=[DS((len(WORDER),)),DS((len(NEEDED)+1,)),DS((8,)),DS((nt,25)),DS((nt,25)),DS((25,)),DS((25,)),DS((5,)),DS((5,)),DS((nt,))]
    cp=dict(has_side_effects=True,vmem_limit_bytes=63*MB+MB//2)
    if comm: cp[N.collective_id]=cid
    return pl.pallas_call(functools.partial(backward_kernel,comm,classes),out_shape=outs,
        in_specs=[A]*(len(WORDER)+len(NEEDED))+[V]*3,out_specs=[A]+[V]*4,scratch_shapes=scr,
        compiler_params=pltpu.CompilerParams(**cp))(*[w[n] for n in WORDER],*[sv[n] for n in NEEDED],vec,tail,aux)


STEP=2

def update_kernel(latent_rate,*refs):
    refs=list(refs)
    grads,kv_g,lat_g,vec,packed=[refs.pop(0) for _ in range(5)]
    old=[[refs.pop(0) for _ in range(3)] for _ in range(4)]
    new=[[refs.pop(0) for _ in range(4)] for _ in range(4)]
    count=jnp.maximum(packed[7:8,1:2],1.0)
    first=(lax.axis_index(N.dp)*lax.axis_size(N.head)+lax.axis_index(N.head))*old[2][0].shape[0]
    def step(total,weight,outs,at,rate):
        w,m,a=(r[at] for r in weight)
        g=total/count
        mom=MOMENTUM*m+g
        wn=w-rate*(g+MOMENTUM*mom)
        for r,v in zip(outs,(g,mom,wn,AVERAGE_DECAY*a+(1.0-AVERAGE_DECAY)*wn)): r[at]=v
    for i in range(STEP): step(grads[i].astype(F32),old[0],new[0],(i,),LEARN_RATE)
    @pl.when(pl.program_id(0)==0)
    def _():
        step(kv_g[:,0:CIN],old[1],new[1],(slice(None),),LEARN_RATE)
        step(lat_g[...],old[3],new[3],(slice(None),),latent_rate)
        rows=old[2][0].shape[0]; classes=old[2][0].shape[1]
        images=vec.shape[0]
        own=jnp.zeros((images,rows),F32)
        for i in range(4):
            pick=lax.broadcasted_iota(jnp.int32,(256,rows),0)+256*i==first+lax.broadcasted_iota(jnp.int32,(256,rows),1)
            own=own+dot(vec[:,i,:].astype(BF),pick.astype(BF))
        own=own.astype(BF)
        for i in range(4):
            n=min(256,classes-256*i)
            dl=vec[:,4+i,:]
            hi=dl.astype(BF); rest=dl-hi.astype(F32); mid=rest.astype(BF); lo=(rest-mid.astype(F32)).astype(BF)
            g=dot(own,hi,TN)+dot(own,mid,TN)+dot(own,lo,TN)
            step(g[:,0:n],old[2],new[2],(slice(None),slice(256*i,256*i+n)),LEARN_RATE)

def update_all(grads,kv_g,lat_g,vec,packed,square,kv,head,lat,latent_rate):
    one=lambda v: pl.BlockSpec(v.shape,lambda i,n=v.ndim: (0,)*n)
    sq=pl.BlockSpec((STEP,)+grads.shape[1:],lambda i: (i,0,0))
    outs=[jax.ShapeDtypeStruct(g[0].shape,F32) for g in (square,kv,head,lat) for _ in range(4)]
    out_specs=[sq]*4+[one(g[0]) for g in (kv,head,lat) for _ in range(4)]
    in_specs=[sq]+[one(v) for v in (kv_g,lat_g,vec,packed)]+[sq]*3+[one(v) for g in (kv,head,lat) for v in g]
    return pl.pallas_call(functools.partial(update_kernel,latent_rate),out_shape=outs,grid=(grads.shape[0]//STEP,),in_specs=in_specs,out_specs=out_specs,
        compiler_params=pltpu.CompilerParams(vmem_limit_bytes=63*MB))(grads,kv_g,lat_g,vec,packed,*square,*kv,*head,*lat)


def per_device_images(
    pixels,
    masks,
    valid,
    labels,
    square,
    kv_weight,
    head_weight,
    latents,
    small,
    square_mom,
    kv_mom,
    head_mom,
    latent_mom,
    small_mom,
    square_avg,
    kv_avg,
    head_avg,
    latent_avg,
    small_avg,
):
    classes = head_weight.shape[1]
    aux = jnp.pad(small, (0, 8 * D - small.shape[0])).reshape(8, D)
    weights, saved, vec, tail = forward_all(
        square, kv_weight.T, head_weight, latents.T, pixels, masks, valid.T, labels.T, aux
    )
    grads, d_kv, d_lat, vec_all, packed = backward_all(weights, saved, vec, tail, aux, classes)
    latent_rate = LATENTS * math.sqrt(D * MICRO * IMG_DEV * lax.axis_size(N.dp)) / 32.0
    new = update_all(
        grads,
        d_kv,
        d_lat,
        vec_all.reshape(-1, 8, 256),
        packed,
        (square, square_mom, square_avg),
        (kv_weight.T, kv_mom.T, kv_avg.T),
        (head_weight, head_mom, head_avg),
        (latents.T, latent_mom.T, latent_avg.T),
        latent_rate,
    )
    loss_sum, count = packed[7, 0], jnp.maximum(packed[7, 1], 1.0)
    small_total = packed.reshape(-1)[: small.shape[0]]
    small_new = nesterov(small, small_total / count, small_mom, small_avg, LEARN_RATE)
    turned = lambda group: [v.T for v in group]
    return (loss_sum, count, *new[:4], *turned(new[4:8]), *new[8:12], *turned(new[12:]), *small_new)


def solution(mesh):
    in_specs = (
        P(None, "dp", "head", None),
        P(None, "dp", None),
        P(None, "dp"),
        P(None, "dp"),
        P(None, ("dp", "head"), None),
        P(None, ("dp", "head")),
        P(("dp", "head"), None),
        P(None, ("dp", "head")),
        P(),
        P(None, ("dp", "head"), None),
        P(None, ("dp", "head")),
        P(("dp", "head"), None),
        P(None, ("dp", "head")),
        P(),
        P(None, ("dp", "head"), None),
        P(None, ("dp", "head")),
        P(("dp", "head"), None),
        P(None, ("dp", "head")),
        P(),
    )
    out_specs = (
        P(),
        P(),
        P(None, ("dp", "head"), None),
        P(None, ("dp", "head"), None),
        P(None, ("dp", "head"), None),
        P(None, ("dp", "head"), None),
        P(None, ("dp", "head")),
        P(None, ("dp", "head")),
        P(None, ("dp", "head")),
        P(None, ("dp", "head")),
        P(("dp", "head"), None),
        P(("dp", "head"), None),
        P(("dp", "head"), None),
        P(("dp", "head"), None),
        P(None, ("dp", "head")),
        P(None, ("dp", "head")),
        P(None, ("dp", "head")),
        P(None, ("dp", "head")),
        P(),
        P(),
        P(),
        P(),
    )
    whole_images = dict(mesh.shape) == {"dp": 8, "head": MICRO}
    per_device = per_device_images if whole_images else per_device_rows
    return jax.shard_map(
        per_device, mesh=mesh, in_specs=in_specs, out_specs=out_specs, check_vma=False
    )
```

```python
import functools
import math

import jax
import jax.numpy as jnp
from jax import lax
from jax.experimental import pallas as pl
from jax.experimental.pallas import tpu as pltpu
from jax.sharding import PartitionSpec as P

D = 1024
CIN = 261
LATENTS = 512
HEADS = 8
HEAD_DIM = 128
MICRO = 4
IMG_DEV = 1


EPS = 1e-05
NEG_BIG = -1e30
SMOOTH = 0.1
LEARN_RATE = 20.0
MOMENTUM = 0.9
AVERAGE_DECAY = 0.6


def layer_norm(v, gain):
    mean = jnp.mean(v, axis=-1, keepdims=True)
    cent = v - mean
    var = jnp.mean(cent * cent, axis=-1, keepdims=True)
    return cent * lax.rsqrt(var + EPS) * gain


def dot_nn(left, right):
    return jnp.dot(left, right, preferred_element_type=jnp.float32)


def dot_tn(left, right):
    return lax.dot_general(
        left, right, (((0,), (0,)), ((), ())), preferred_element_type=jnp.float32
    )


def dot_nt(left, right):
    return lax.dot_general(
        left, right, (((1,), (1,)), ((), ())), preferred_element_type=jnp.float32
    )


def scores_of(query, keys, valid_keys):
    scores = jnp.einsum("qhd,khd->hqk", query, keys, preferred_element_type=jnp.float32)
    scores = scores * query.shape[-1] ** (-0.5)
    if valid_keys is not None:
        scores = jnp.where(valid_keys[None, None, :], scores, NEG_BIG)
    return scores


def attend(query, keys, values, valid_keys):
    scores = scores_of(query, keys, valid_keys)
    log_total = jax.nn.logsumexp(scores, axis=-1, keepdims=True)
    probs = jnp.exp(scores - log_total).astype(jnp.bfloat16)
    out = jnp.einsum("hqk,khd->qhd", probs, values, preferred_element_type=jnp.float32)
    return (out.astype(jnp.bfloat16), log_total)


def attend_back(query, keys, values, log_total, d_out, valid_keys):
    scale = query.shape[-1] ** (-0.5)
    probs = jnp.exp(scores_of(query, keys, valid_keys) - log_total)
    probs_b = probs.astype(jnp.bfloat16)
    d_probs = jnp.einsum("qhd,khd->hqk", d_out, values, preferred_element_type=jnp.float32)
    d_scores = probs * (d_probs - jnp.sum(probs * d_probs, axis=-1, keepdims=True))
    d_scores = d_scores.astype(jnp.bfloat16)
    d_query = jnp.einsum("hqk,khd->qhd", d_scores, keys, preferred_element_type=jnp.float32) * scale
    d_keys = jnp.einsum("hqk,qhd->khd", d_scores, query, preferred_element_type=jnp.float32) * scale
    d_values = jnp.einsum("hqk,qhd->khd", probs_b, d_out, preferred_element_type=jnp.float32)
    return (d_query, d_keys, d_values)


def mlp_forward(hidden, gain, w_in, w_out):
    normed = layer_norm(hidden, gain).astype(jnp.bfloat16)
    pre = dot_nn(normed, w_in)
    active = jax.nn.gelu(pre).astype(jnp.bfloat16)
    return (hidden + dot_nn(active, w_out), (normed, pre, active))


def mlp_backward(hidden, gain, w_in, w_out, saved, d_next):
    normed, pre, active = saved
    d_next_b = d_next.astype(jnp.bfloat16)
    d_w_out = dot_tn(active, d_next_b)
    d_active = dot_nt(d_next_b, w_out)
    d_pre = jax.vjp(jax.nn.gelu, pre)[1](d_active)[0].astype(jnp.bfloat16)
    d_w_in = dot_tn(normed, d_pre)
    d_normed = dot_nt(d_pre, w_in)
    d_hidden, d_gain = jax.vjp(layer_norm, hidden, gain)[1](d_normed)
    return (d_next + d_hidden, d_gain, d_w_in, d_w_out)


def image_grads(weights, small, pixel_own, mask_row, valid_one, label, loss_scale, head_first):
    square, kv_weight, head_weight, latent_all, w_qkv = weights
    gains = small[: 5 * D].reshape(5, D)
    pix_gain = small[5 * D : 5 * D + CIN]
    bias = small[5 * D + CIN :]
    rows = latent_all.shape[0] // lax.axis_size("head")
    start = lax.axis_index("head") * rows
    latent_own = lax.dynamic_slice_in_dim(latent_all, start, rows, 0).astype(jnp.float32)
    valid_keys = mask_row > 0
    pix_float = pixel_own.astype(jnp.float32)
    normed_pix = layer_norm(pix_float, pix_gain).astype(jnp.bfloat16)
    kv_own = dot_nn(normed_pix, kv_weight).astype(jnp.bfloat16)
    kv_all = lax.all_gather(kv_own, "head", axis=0, tiled=True)
    keys_px = kv_all[:, :D].reshape(-1, 1, D)
    values_px = kv_all[:, D:].reshape(-1, 1, D)
    query_norm = layer_norm(latent_own, gains[0]).astype(jnp.bfloat16)
    query = dot_nn(query_norm, square[0]).astype(jnp.bfloat16).reshape(rows, 1, D)
    cross_out, cross_total = attend(query, keys_px, values_px, valid_keys)
    cross_out = cross_out.reshape(rows, D)
    hidden1 = latent_own + dot_nn(cross_out, square[1])
    hidden2, mlp_first = mlp_forward(hidden1, gains[1], square[2], square[3])
    self_norm = layer_norm(hidden2, gains[2]).astype(jnp.bfloat16)
    qkv = dot_nn(self_norm, w_qkv).astype(jnp.bfloat16)
    kv_latent = lax.all_gather(qkv[:, D:], "head", axis=0, tiled=True)
    self_query = qkv[:, :D].reshape(rows, HEADS, HEAD_DIM)
    self_keys = kv_latent[:, :D].reshape(-1, HEADS, HEAD_DIM)
    self_values = kv_latent[:, D:].reshape(-1, HEADS, HEAD_DIM)
    self_out, self_total = attend(self_query, self_keys, self_values, None)
    self_out = self_out.reshape(rows, D)
    hidden3 = hidden2 + dot_nn(self_out, square[7])
    hidden4, mlp_second = mlp_forward(hidden3, gains[3], square[8], square[9])
    final = layer_norm(hidden4, gains[4])
    pooled = lax.psum(jnp.sum(final, axis=0), "head") / latent_all.shape[0]
    pooled_b = pooled.astype(jnp.bfloat16)
    logits = dot_nn(pooled_b[None, :], head_weight)[0] + bias
    logp = jax.nn.log_softmax(logits)
    picked = jnp.arange(logits.shape[0]) == label
    loss = -valid_one * (
        (1.0 - SMOOTH) * jnp.sum(jnp.where(picked, logp, 0.0)) + SMOOTH * jnp.mean(logp)
    )
    target = (1.0 - SMOOTH) * picked.astype(jnp.float32) + SMOOTH / logits.shape[0]
    d_logits = valid_one * loss_scale * (jnp.exp(logp) - target)
    d_bias = d_logits * head_first
    d_head = pooled_b.astype(jnp.float32)[:, None] * d_logits[None, :] * head_first
    d_pooled = jnp.dot(head_weight.astype(jnp.float32), d_logits)
    d_final = jnp.broadcast_to(d_pooled / latent_all.shape[0], final.shape)
    d_hidden4, d_gain4 = jax.vjp(layer_norm, hidden4, gains[4])[1](d_final)
    d_hidden3, d_gain3, d_w8, d_w9 = mlp_backward(
        hidden3, gains[3], square[8], square[9], mlp_second, d_hidden4
    )
    d_hidden3_b = d_hidden3.astype(jnp.bfloat16)
    d_w7 = dot_tn(self_out, d_hidden3_b)
    d_self_out = dot_nt(d_hidden3_b, square[7]).astype(jnp.bfloat16).reshape(rows, HEADS, HEAD_DIM)
    d_query, d_keys, d_values = attend_back(
        self_query, self_keys, self_values, self_total, d_self_out, None
    )
    d_kv_terms = jnp.concatenate([d_keys.reshape(-1, D), d_values.reshape(-1, D)], axis=1)
    d_kv_own = lax.psum_scatter(
        d_kv_terms.astype(jnp.bfloat16), "head", scatter_dimension=0, tiled=True
    ).astype(jnp.float32)
    d_qkv = jnp.concatenate([d_query.reshape(rows, D), d_kv_own], axis=1).astype(jnp.bfloat16)
    d_w_qkv = dot_tn(self_norm, d_qkv)
    d_self_norm = dot_nt(d_qkv, w_qkv)
    d_hidden2_norm, d_gain2 = jax.vjp(layer_norm, hidden2, gains[2])[1](d_self_norm)
    d_hidden2 = d_hidden3 + d_hidden2_norm
    d_hidden1, d_gain1, d_w2, d_w3 = mlp_backward(
        hidden1, gains[1], square[2], square[3], mlp_first, d_hidden2
    )
    d_hidden1_b = d_hidden1.astype(jnp.bfloat16)
    d_w1 = dot_tn(cross_out, d_hidden1_b)
    d_cross = dot_nt(d_hidden1_b, square[1]).astype(jnp.bfloat16).reshape(rows, 1, D)
    d_query, d_keys, d_values = attend_back(
        query, keys_px, values_px, cross_total, d_cross, valid_keys
    )
    d_px_terms = jnp.concatenate([d_keys.reshape(-1, D), d_values.reshape(-1, D)], axis=1)
    d_kv_px = lax.psum_scatter(
        d_px_terms.astype(jnp.bfloat16), "head", scatter_dimension=0, tiled=True
    )
    d_kv_turned = dot_tn(d_kv_px, normed_pix)
    d_normed_pix = dot_nt(d_kv_px, kv_weight)
    d_pix_gain = jax.vjp(layer_norm, pix_float, pix_gain)[1](d_normed_pix)[1]
    d_query_b = d_query.reshape(rows, D).astype(jnp.bfloat16)
    d_w0 = dot_tn(query_norm, d_query_b)
    d_query_norm = dot_nt(d_query_b, square[0])
    d_latent_norm, d_gain0 = jax.vjp(layer_norm, latent_own, gains[0])[1](d_query_norm)
    d_latent_own = d_hidden1 + d_latent_norm
    d_square = jnp.stack(
        [
            d_w0,
            d_w1,
            d_w2,
            d_w3,
            d_w_qkv[:, :D],
            d_w_qkv[:, D : 2 * D],
            d_w_qkv[:, 2 * D :],
            d_w7,
            d_w8,
            d_w9,
        ]
    )
    latent_turned = lax.dynamic_update_slice_in_dim(
        jnp.zeros((D, latent_all.shape[0]), jnp.float32), d_latent_own.T, start, 1
    )
    d_small = jnp.concatenate(
        [jnp.stack([d_gain0, d_gain1, d_gain2, d_gain3, d_gain4]).reshape(-1), d_pix_gain, d_bias]
    )
    return ((d_square, d_kv_turned[None], d_head[None], latent_turned[None], d_small), loss)


def owner_layout(reduced):
    return (reduced[0], reduced[1][0].T, reduced[2][0], reduced[3][0].T)


def nesterov(weight, grad, mom, avg, rate):
    mom_new = MOMENTUM * mom + grad
    weight_new = weight - rate * (grad + MOMENTUM * mom_new)
    avg_new = AVERAGE_DECAY * avg + (1.0 - AVERAGE_DECAY) * weight_new
    return (grad, mom_new, weight_new, avg_new)


def per_device_rows(
    pixels,
    masks,
    valid,
    labels,
    square,
    kv_weight,
    head_weight,
    latents,
    small,
    square_mom,
    kv_mom,
    head_mom,
    latent_mom,
    small_mom,
    square_avg,
    kv_avg,
    head_avg,
    latent_avg,
    small_avg,
):
    gathered = (
        lax.all_gather(square.astype(jnp.bfloat16), ("dp", "head"), axis=1, tiled=True),
        lax.all_gather(kv_weight.astype(jnp.bfloat16), ("dp", "head"), axis=1, tiled=True),
        lax.all_gather(head_weight.astype(jnp.bfloat16), ("dp", "head"), axis=0, tiled=True),
        lax.all_gather(latents.astype(jnp.bfloat16), ("dp", "head"), axis=1, tiled=True),
    )
    full_square = gathered[0]
    w_qkv = jnp.concatenate([full_square[4], full_square[5], full_square[6]], axis=1)
    weights = (full_square, gathered[1], gathered[2], gathered[3], w_qkv)
    head_first = (lax.axis_index("head") == 0).astype(jnp.float32)
    valid_float = valid.astype(jnp.float32)
    early_count = lax.psum(jnp.sum(valid_float), "dp")
    loss_scale = 1.0 / jnp.maximum(early_count, 1.0)
    kv_shape = gathered[1].shape
    lat_shape = gathered[3].shape
    big_zero = (
        jnp.zeros(full_square.shape, jnp.float32),
        jnp.zeros((1, kv_shape[1], kv_shape[0]), jnp.float32),
        jnp.zeros((1,) + gathered[2].shape, jnp.float32),
        jnp.zeros((1, lat_shape[1], lat_shape[0]), jnp.float32),
    )

    def micro_step(carry, batch):
        big, small_acc, loss_acc = carry
        pix_micro, mask_micro, valid_micro, label_micro = batch
        grads, loss_part = image_grads(
            weights,
            small,
            pix_micro[0],
            mask_micro[0],
            valid_micro[0],
            label_micro[0],
            loss_scale,
            head_first,
        )
        reduced = (grads[0], grads[1], grads[2], grads[3])
        big = tuple((a + b for a, b in zip(big, reduced)))
        return ((big, small_acc + grads[4], loss_acc + loss_part), None)

    start_carry = (big_zero, jnp.zeros(small.shape, jnp.float32), jnp.float32(0.0))
    (big, small_acc, loss_acc), _ = lax.scan(
        micro_step, start_carry, (pixels, masks, valid_float, labels)
    )
    big = owner_layout(
        (
            lax.psum_scatter(big[0], ("dp", "head"), scatter_dimension=1, tiled=True),
            lax.psum_scatter(big[1], ("dp", "head"), scatter_dimension=1, tiled=True),
            lax.psum_scatter(big[2], ("dp", "head"), scatter_dimension=1, tiled=True),
            lax.psum_scatter(big[3], ("dp", "head"), scatter_dimension=1, tiled=True),
        )
    )
    small_total, loss_sum, count = lax.psum(
        (small_acc, loss_acc * head_first, jnp.sum(valid_float) * head_first), ("dp", "head")
    )
    count = jnp.maximum(count, 1.0)
    latent_rate = LATENTS * math.sqrt(D * MICRO * IMG_DEV * lax.axis_size("dp")) / 32.0
    rates = (LEARN_RATE, LEARN_RATE, LEARN_RATE, latent_rate, LEARN_RATE)
    results = [loss_sum, count]
    params = (square, kv_weight, head_weight, latents, small)
    moms = (square_mom, kv_mom, head_mom, latent_mom, small_mom)
    avgs = (square_avg, kv_avg, head_avg, latent_avg, small_avg)
    for weight, grad, mom, avg, rate in zip(params, tuple(big) + (small_total,), moms, avgs, rates):
        results.extend(nesterov(weight, grad, mom, avg, rate))
    return tuple(results)


class Names:
    def __getattr__(self, name):
        return name


N = Names()


MESH=pl.DeviceIdType.MESH
MB=1<<20

def where_am_i():
    dp=lax.axis_index(N.dp); h=lax.axis_index(N.head)
    return dict(dp=dp,h=h,z=dp//2,y=dp%2,x=h//2,c=h%2)

def neighbours(me):
    return dict(zu=(me[N.dp]+2,me[N.h]),zd=(me[N.dp]-2,me[N.h]),y=(me[N.dp]+1-2*me[N.y],me[N.h]),
                x=(me[N.dp],me[N.h]+2-4*me[N.x]),c=(me[N.dp],me[N.h]+1-2*me[N.c]))

def entry_barrier(me,nb,others=()):
    z=me[N.z]
    bar=pltpu.get_barrier_semaphore()
    for k in (N.x,N.y,N.c):
        pl.semaphore_signal(bar,inc=1,device_id=nb[k],device_id_type=MESH)
    @pl.when(z<3)
    def _(): pl.semaphore_signal(bar,inc=1,device_id=nb[N.zu],device_id_type=MESH)
    @pl.when(z>0)
    def _(): pl.semaphore_signal(bar,inc=1,device_id=nb[N.zd],device_id_type=MESH)
    for other in others:
        pl.semaphore_signal(bar,inc=1,device_id=other,device_id_type=MESH)
    pl.semaphore_wait(bar,4+(z+1)//2%2+len(others))

class Gather:
    def __init__(self,me,nb,buf,groups,ssem,rsem):
        self.me,self.nb,self.buf,self.groups,self.ssem,self.rsem=me,nb,buf,groups,ssem,rsem
        self.pending=[]
    def copy(self,src,dst,slot,dev):
        return pltpu.make_async_remote_copy(src_ref=src,dst_ref=dst,send_sem=self.ssem.at[slot],recv_sem=self.rsem.at[slot],device_id=dev,device_id_type=MESH)
    def view(self,r,*ix):
        return self.buf.at[(*ix,slice(None),pl.ds(*self.groups[r]))]
    def hopview(self,r,*ix):
        c0,w=self.groups[r]
        if r==0: w+=self.groups[1][1]
        return self.buf.at[(*ix,slice(None),pl.ds(c0,w))]
    def hop(self,r,k,op):
        if r==1: return
        z,y,x,c=(self.me[i] for i in N.zyxc)
        rest=(y,x,c) if r<2 else (slice(None),slice(None),c)
        su,sd=8*r+k-1,8*r+3+k-1
        if op==N.start:
            @pl.when((z<3)&(z>=k-1))
            def _():
                v=self.hopview(r,z-(k-1),*rest); self.copy(v,v,su,self.nb[N.zu]).start()
            @pl.when((z>0)&(z+k-1<=3))
            def _():
                v=self.hopview(r,z+(k-1),*rest); self.copy(v,v,sd,self.nb[N.zd]).start()
        elif op==N.recv:
            @pl.when(z>=k)
            def _():
                v=self.hopview(r,z-k,*rest); self.copy(v,v,su,self.nb[N.zd]).wait_recv()
            @pl.when(z+k<=3)
            def _():
                v=self.hopview(r,z+k,*rest); self.copy(v,v,sd,self.nb[N.zu]).wait_recv()
        else:
            @pl.when((z<3)&(z>=k-1))
            def _():
                v=self.hopview(r,z-(k-1),*rest); self.copy(v,v,su,self.nb[N.zu]).wait_send()
            @pl.when((z>0)&(z+k-1<=3))
            def _():
                v=self.hopview(r,z+(k-1),*rest); self.copy(v,v,sd,self.nb[N.zd]).wait_send()
    def flat(self,r,axis,op):
        z,y,x,c=(self.me[i] for i in N.zyxc)
        A=slice(None)
        if axis==N.y:
            mine={0:(A,y,x,c),1:(A,y,A,c),2:(z,y,A,c)}[r]; other={0:(A,1-y,x,c),1:(A,1-y,A,c),2:(z,1-y,A,c)}[r]; slot=8*r+6
        elif axis==N.x:
            mine={0:(A,A,x,c),1:(A,y,x,c),2:(z,y,x,c)}[r]; other={0:(A,A,1-x,c),1:(A,y,1-x,c),2:(z,y,1-x,c)}[r]; slot=8*r+7
        if op==N.start:
            v=self.view(r,*mine); self.copy(v,v,slot,self.nb[axis]).start()
        elif op==N.recv:
            v=self.view(r,*other); self.copy(v,v,slot,self.nb[axis]).wait_recv()
        else:
            v=self.view(r,*mine); self.copy(v,v,slot,self.nb[axis]).wait_send()
    def core(self,op):
        c=self.me[N.c]; A=slice(None)
        if op==N.recv:
            v=self.buf.at[A,A,A,1-c]; self.copy(v,v,24,self.nb[N.c]).wait_recv()
        else:
            v=self.buf.at[A,A,A,c]; d=self.copy(v,v,24,self.nb[N.c])
            d.start() if op==N.start else d.wait_send()
    ORDER=[[N.h1,N.h2,N.h3,N.y,N.x],[N.h1,N.h2,N.h3,N.x,N.y],[N.x,N.y,N.h1,N.h2,N.h3]]
    def do(self,r,p,op):
        n=self.ORDER[r][p]
        if n[0]==N.h: self.hop(r,int(n[1]),op)
        else: self.flat(r,n,op)
    NPH=6
    def phase(self,p):
        if p>0 and p<=5:
            for r in range(3):
                if self.groups[r][1]: self.do(r,p-1,N.recv)
                if p<5 and self.groups[r][1]: self.do(r,p,N.start)
        if p==0:
            for r in range(3):
                if self.groups[r][1]: self.do(r,0,N.start)
        if p==5: self.core(N.start)
        if p==6: self.core(N.recv)
    def sends(self):
        for r in range(3):
            if self.groups[r][1]:
                for p in range(5): self.do(r,p,N.send)
        self.core(N.send)

SPLIT={1024:((0,384),(384,384),(768,256)),512:((0,256),(256,256),(512,0)),384:((0,128),(128,256),(384,0))}


ALLS=slice(None)

def recv_shapes(r,n):
    (_,a),(_,b),(_,c)=SPLIT[n]
    d=dict(core=(4,2,2,r,n),A0=(4,2,r,a),A1=(4,r,a),Ah=(6,r,a+b),B0=(4,2,r,b),B1=(4,r,b))
    if c: d.update(Ch=(6,2,2,r,c),C0=(2,r,c),C1=(r,c))
    return d

def add_into(dst,src,cols,lead):
    for di,si in lead:
        dst[(*di,ALLS,cols)]=dst[(*di,ALLS,cols)]+src[si]

class Scatter:
    def __init__(self,me,nb,part,send_half,bufs,out,groups,ssem,rsem):
        self.me,self.nb,self.part,self.half,self.b,self.out,self.groups,self.ssem,self.rsem=me,nb,part,send_half,bufs,out,groups,ssem,rsem
    def copy(self,src,dst,slot,dev):
        return pltpu.make_async_remote_copy(src_ref=src,dst_ref=dst,send_sem=self.ssem.at[slot],recv_sem=self.rsem.at[slot],device_id=dev,device_id_type=MESH)
    def cols(self,r): return pl.ds(*self.groups[r])
    def hop(self,r,k,op):
        if r==1: return
        z,y,x=(self.me[i] for i in N.zyx)
        rest=(y,x) if r<2 else (ALLS,ALLS)
        buf=self.b[N.ABC[r]+N.h]; cols=pl.ds(self.groups[0][0],self.groups[0][1]+self.groups[1][1]) if r==0 else self.cols(r)
        su,sd=8*r+k-1,8*r+3+k-1
        up=lambda: self.copy(self.part.at[(z+k,*rest,ALLS,cols)],buf.at[k-1],su,self.nb[N.zu])
        dn=lambda: self.copy(self.part.at[(z-k,*rest,ALLS,cols)],buf.at[3+k-1],sd,self.nb[N.zd])
        if op in(N.start,N.send):
            @pl.when(z+k<=3)
            def _():
                d=up(); d.start() if op==N.start else d.wait_send()
            @pl.when(z-k>=0)
            def _():
                d=dn(); d.start() if op==N.start else d.wait_send()
        else:
            last=(k==1 and r<2)
            @pl.when((z>=1)&(z-1+k<=3))
            def _():
                self.copy(buf.at[k-1],buf.at[k-1],su,self.nb[N.zd]).wait_recv()
                self.hopadd(r,z-1+k,buf.at[k-1],cols)
            @pl.when((z<=2)&(z+1-k>=0))
            def _():
                self.copy(buf.at[3+k-1],buf.at[3+k-1],sd,self.nb[N.zu]).wait_recv()
                self.hopadd(r,z+1-k,buf.at[3+k-1],cols)
    def hopadd(self,r,d,src,cols):
        y,x=self.me[N.y],self.me[N.x]
        if r<2: add_into(self.part,src,cols,[((d,y,x),(ALLS,ALLS))])
        else: add_into(self.part,src,cols,[((d,i,j),(i,j)) for i in range(2) for j in range(2)])
    def flat(self,r,axis,op):
        z,y,x=(self.me[i] for i in N.zyx); cols=self.cols(r)
        name=N.ABC[r]
        if axis==N.x:
            mine={0:(ALLS,ALLS,1-x),1:(ALLS,y,1-x),2:(z,y,1-x)}[r]; slot=8*r+7; buf=self.b[{0:N.A0,1:N.B1,2:N.C1}[r]]
        else:
            mine={0:(ALLS,1-y,x),1:(ALLS,1-y),2:(z,1-y)}[r]; slot=8*r+6; buf=self.b[{0:N.A1,1:N.B0,2:N.C0}[r]]
        if op==N.recv:
            self.copy(buf,buf,slot,self.nb[axis]).wait_recv()
            if axis==N.x:
                lead={0:[((i,j,x),(i,j)) for i in range(4) for j in range(2)],1:[((i,y,x),(i,)) for i in range(4)],2:[((z,y,x),(ALLS,ALLS))]}[r]
            else:
                lead={0:[((i,y,x),(i,)) for i in range(4)],1:[((i,y,j),(i,j)) for i in range(4) for j in range(2)],2:[((z,y,j),(j,)) for j in range(2)]}[r]
            add_into(self.part,buf,cols,lead)
        else:
            d=self.copy(self.part.at[(*mine,)+(ALLS,)*(4-len(mine))+(cols,)],buf,slot,self.nb[axis])
            d.start() if op==N.start else d.wait_send()
    def core(self,op):
        buf=self.b[N.core]
        if op==N.recv:
            self.copy(buf,buf,24,self.nb[N.c]).wait_recv()
            @pl.loop(0,4)
            def _(i):
                for j in range(2):
                    for k in range(2):
                        self.part[i,j,k]=self.part[i,j,k]+buf[i,j,k]
        else:
            d=self.copy(self.half,buf,24,self.nb[N.c]); d.start() if op==N.start else d.wait_send()
    ORDER=[[N.x,N.y,N.h3,N.h2,N.h1],[N.y,N.x,N.h3,N.h2,N.h1],[N.h3,N.h2,N.h1,N.y,N.x]]
    def do(self,r,p,op):
        n=self.ORDER[r][p]
        if not self.groups[r][1]: return
        if n[0]==N.h: self.hop(r,int(n[1]),op)
        else: self.flat(r,n,op)
    def phase(self,p):
        if p==0: self.core(N.start); return
        if p==1: self.core(N.recv)
        for r in range(3):
            if p>=2: self.do(r,p-2,N.recv)
        for r in range(3):
            if p<=5: self.do(r,p-1,N.start)
        if p==6:
            z,y,x=(self.me[i] for i in N.zyx)
            if self.out is not None: self.out[...]=self.part[z,y,x].astype(jnp.float32)
    def sends(self):
        self.core(N.send)
        for r in range(3):
            for p in range(5): self.do(r,p,N.send)

def small_steps(me):
    dp,h=me[N.dp],me[N.h]
    z=me[N.z]
    return [(dp,h+1-2*me[N.c]),(dp,h+2-4*me[N.x]),(dp+1-2*me[N.y],h),(dp+2-4*(z%2),h),(dp+4-8*(z//2),h)]


BF=jnp.bfloat16; F32=jnp.float32
PADC=384
NN=(((1,),(0,)),((),())); NT=(((1,),(1,)),((),())); TN=(((0,),(0,)),((),()))
def dot(a,b,dims=NN): return lax.dot_general(a,b,dims,preferred_element_type=F32)
ROWS=512; TILE=512; RB=128

def norm_rows(load,gain,xhat,rstd,normed,width=D,store_sum=None):
    def body(i,tot):
        rows=pl.ds(i*RB,RB)
        v=load(rows)
        mean=jnp.sum(v,-1,keepdims=True)/width
        cent=v-mean
        var=jnp.sum(cent*cent,-1,keepdims=True)/width
        r=lax.rsqrt(var+1e-5)
        xh=cent*r
        lanes=pl.ds(0,width)
        xhat[rows,lanes]=xh.astype(BF)
        if rstd is not None: rstd[rows]=jnp.broadcast_to(r,(RB,128))
        if normed is not None: normed[rows,lanes]=(xh*gain).astype(BF)
        if tot is None: return None
        return tot+jnp.sum(xh,0,keepdims=True)
    tot=jnp.zeros((1,D),F32) if store_sum else None
    for i in range(ROWS//RB): tot=body(i,tot)
    return tot

def mm(lhs,w,epi):
    for j in range(D//TILE):
        cols=pl.ds(j*TILE,TILE)
        epi(cols,dot(lhs[...],w[:,:,:,:,:,cols].reshape(D,TILE)))

def gelu_pair(v):
    k=math.sqrt(2/math.pi)
    v2=v*v
    t=jnp.tanh(k*v*(1+0.044715*v2))
    h=0.5*(1+t)
    return v*h, h+0.5*v*(1-t*t)*(k*(1+3*0.044715*v2))

SAVED=dict(xb=((512,PADC),BF),xhp=((512,PADC),BF),kv=((512,2048),BF),q=((512,D),BF),qn=((512,D),BF),
  xh0=((512,D),BF),p=((512,512),BF),o=((512,D),BF),
  xh1=((512,D),BF),n1=((512,D),BF),a1=((512,D),BF),dg1=((512,D),BF),
  xh2=((512,D),BF),n2=((512,D),BF),qkv=((3,512,D),BF),ph=((8,512,512),BF),so=((512,D),BF),
  xh3=((512,D),BF),n3=((512,D),BF),a2=((512,D),BF),dg2=((512,D),BF),xh4=((512,D),BF),
  rs0=((512,128),F32),rs1=((512,128),F32),rs2=((512,128),F32),rs3=((512,128),F32),rs4=((512,128),F32))
NAMES=list(SAVED)
TENS=[N.lat,N.kvw]+[(N.w+str(i)) for i in range(8)]+[N.head,N.w8,N.w9]
ENTRY,FGAP=3,4
def tshape(n): return {N.lat:(32,512),N.kvw:(64,PADC)}.get(n,(32,1024))

def forward_kernel(comm,*refs):
    refs=list(refs)
    nt=len(TENS)
    square,kvw,hw_own,lat_own,pixels,masks,valids,labels,aux=[refs.pop(0) for _ in range(9)]
    whole=[refs.pop(0) for _ in range(nt)]
    out={n:refs.pop(0) for n in NAMES}
    vec,tail=refs.pop(0),refs.pop(0)
    bufs=[refs.pop(0) for _ in range(nt)]
    s={n:refs.pop(0) for n in NAMES}
    z,h,pix,ssem,rsem,wsem,osem,psend,precv=refs
    me=where_am_i(); nb=neighbours(me)
    zz,yy,xx,cc=(me[i] for i in N.zyxc)
    micro=me[N.h]
    classes=hw_own.shape[1]
    own={n:bufs[TENS.index(n)].at[zz,yy,xx,cc] for n in TENS}
    own[N.lat][...]=lat_own[...].astype(BF)
    own[N.kvw][...]=jnp.zeros((64,PADC),BF)
    own[N.kvw][:,0:CIN]=kvw[...].astype(BF)
    own[N.head][...]=jnp.zeros((32,D),BF)
    own[N.head][:,0:classes]=hw_own[...].astype(BF)
    for i in range(10): own[(N.w+str(i))][...]=square[i].astype(BF)
    for m in (N.xb,N.xhp): s[m][...]=jnp.zeros_like(s[m])
    ev=[]
    ready={}
    if comm:
        dp_,h_=me[N.dp],me[N.h]
        diag=(dp_,(h_+1-2*cc)+2-4*xx)
        entry_barrier(me,nb,[diag])
        peers=[nb[N.c],nb[N.x],diag]
        swaps=[pltpu.make_async_remote_copy(src_ref=pixels.at[p[1],0],dst_ref=pix.at[pl.ds(pl.multiple_of(micro*128,128),128)],send_sem=psend.at[i],recv_sem=precv.at[i],device_id=p,device_id_type=MESH) for i,p in enumerate(peers)]
        for k in swaps: k.start()
        keep_own=pltpu.make_async_copy(pixels.at[micro,0],pix.at[pl.ds(pl.multiple_of(micro*128,128),128)],psend.at[3])
        keep_own.start()
        gs=[Gather(me,nb,b,SPLIT[b.shape[-1]],ssem.at[i],rsem.at[i]) for i,b in enumerate(bufs)]
        for tick in range(ENTRY*(nt-1)+6*FGAP+1):
            for t in range(nt):
                p=tick-ENTRY*t
                if p>=0 and p%FGAP==0 and p//FGAP<=6:
                    ev.append(functools.partial(gs[t].phase,p//FGAP))
                    if p//FGAP==6: ready[t]=len(ev)
    else:
        for t in range(nt): ready[t]=0
    pos=[0]
    def pump(k):
        for e in ev[pos[0]:pos[0]+k]: e()
        pos[0]=min(pos[0]+k,len(ev))
    outs=[]
    def weight(name):
        t=TENS.index(name)
        if pos[0]<ready[t]: pump(ready[t]-pos[0])
        if name not in(N.lat,N.head):
            c=pltpu.make_async_copy(bufs[t],whole[t],wsem.at[t]); c.start(); outs.append(c)
        return bufs[t]
    def keep(*names):
        for m in names:
            c=pltpu.make_async_copy(s[m],out[m],osem.at[NAMES.index(m)]); c.start(); outs.append(c)
    gain=lambda i: aux[i:i+1,:]
    pump(14)
    if comm:
        keep_own.wait()
        for i,p in enumerate(peers):
            got=pix.at[pl.ds(pl.multiple_of(p[1]*128,128),128)]
            pltpu.make_async_remote_copy(src_ref=got,dst_ref=got,send_sem=psend.at[0],recv_sem=precv.at[i],device_id=p,device_id_type=MESH).wait_recv()
    norm_rows(lambda r: pix[r].astype(F32),aux[5:6,0:CIN],s[N.xhp],None,s[N.xb],width=CIN)
    keep(N.xb,N.xhp)
    lt=weight(N.lat)
    @pl.loop(0,8)
    def _(i):
        z[:,pl.ds(pl.multiple_of(i*128,128),128)]=lt[i//2,i%2].reshape(128,ROWS).T
    pump(3)
    norm_rows(lambda r: z[r].astype(F32),gain(0),s[N.xh0],s[N.rs0],s[N.qn])
    keep(N.qn,N.xh0,N.rs0)
    kt=weight(N.kvw)
    for j in range(4):
        rows=kt[j].reshape(512,PADC)
        s[N.kv][:,j*512:(j+1)*512]=dot(s[N.xb][...],rows,NT).astype(BF)
    keep(N.kv)
    pump(3)
    w=weight(N.w0)
    def epi(cols,acc): s[N.q][:,cols]=acc.astype(BF)
    mm(s[N.qn],w,epi)
    keep(N.q)
    pump(3)
    for i in range(2):
        rows=pl.ds(i*256,256)
        sc=dot(s[N.q][rows],s[N.kv][:,:D],NT)*(1/32)
        sc=jnp.where(masks[micro]>0,sc,-1e30)
        e=jnp.exp(sc-jnp.max(sc,-1,keepdims=True))
        p=(e*(1/jnp.sum(e,-1,keepdims=True))).astype(BF)
        s[N.p][rows]=p
        s[N.o][rows]=dot(p,s[N.kv][:,D:]).astype(BF)
    pump(2)
    keep(N.p,N.o)
    w=weight(N.w1)
    def epi(cols,acc): h[:,cols]=z[:,cols].astype(F32)+acc
    mm(s[N.o],w,epi)
    pump(3)
    norm_rows(lambda r: h[r],gain(1),s[N.xh1],s[N.rs1],s[N.n1])
    keep(N.xh1,N.rs1,N.n1)
    def addh(cols,acc): h[:,cols]=h[:,cols]+acc
    def mlp(wi,wo,nn,dg,act):
        w=weight(wi)
        def epi(cols,acc):
            a,d=gelu_pair(acc)
            s[act][:,cols]=a.astype(BF); s[dg][:,cols]=d.astype(BF)
        mm(s[nn],w,epi)
        keep(dg,act)
        pump(3)
        w=weight(wo)
        mm(s[act],w,addh)
    mlp(N.w2,N.w3,N.n1,N.dg1,N.a1)
    pump(3)
    norm_rows(lambda r: h[r],gain(2),s[N.xh2],s[N.rs2],s[N.n2])
    keep(N.xh2,N.rs2,N.n2)
    for i in range(3):
        w=weight((N.w+str(4+i)))
        def epi(cols,acc,i=i): s[N.qkv][i,:,cols]=acc.astype(BF)
        mm(s[N.n2],w,epi)
        pump(2)
    keep(N.qkv)
    for i in range(8):
        cols=pl.ds(i*128,128)
        sc=dot(s[N.qkv][0,:,cols],s[N.qkv][1,:,cols],NT)*(128**-0.5)
        e=jnp.exp(sc-jnp.max(sc,-1,keepdims=True))
        p=(e*(1/jnp.sum(e,-1,keepdims=True))).astype(BF)
        s[N.ph][i]=p
        s[N.so][:,cols]=dot(p,s[N.qkv][2,:,cols]).astype(BF)
        if i%4==3: pump(2)
    keep(N.ph,N.so)
    w=weight(N.w7)
    mm(s[N.so],w,addh)
    pump(3)
    norm_rows(lambda r: h[r],gain(3),s[N.xh3],s[N.rs3],s[N.n3])
    keep(N.xh3,N.rs3,N.n3)
    mlp(N.w8,N.w9,N.n3,N.dg2,N.a2)
    tot=norm_rows(lambda r: h[r],gain(4),s[N.xh4],s[N.rs4],None,store_sum=True)
    keep(N.xh4,N.rs4)
    pooled=(tot*gain(4)/ROWS).astype(BF)
    hw=weight(N.head)
    lane=lax.broadcasted_iota(jnp.int32,(1,D),1)
    turned=pltpu.roll(aux[...],D-CIN,1)
    bias=jnp.where(lane<D-CIN,turned[5:6],turned[6:7])
    logits=dot(jnp.broadcast_to(pooled,(16,D)),hw[...].reshape(D,D))[0:1]+bias
    logits=jnp.where(lane<classes,logits,-1e30)
    mx=jnp.max(logits,-1,keepdims=True)
    logp=logits-mx-jnp.log(jnp.sum(jnp.exp(logits-mx),-1,keepdims=True))
    target=jnp.where(lane<classes,jnp.where(lane==labels[0,micro],1.0-SMOOTH,0.0)+SMOOTH/classes,0.0)
    valid=jnp.full((1,D),valids[0,micro].astype(F32))
    loss=-valid*jnp.sum(target*logp,-1,keepdims=True)
    dl=valid*(jnp.exp(logp)-target)
    hi=dl.astype(BF); lo=(dl-hi.astype(F32)).astype(BF)
    dp=dot(jnp.concatenate([jnp.broadcast_to(hi,(16,D)),jnp.broadcast_to(lo,(16,D))],0),hw[...].reshape(D,D),NT)
    pf=pooled.astype(F32)
    shown=jnp.where(lane==classes,valid,dl)
    for i in range(4):
        vec[i:i+1]=pf[:,i*256:(i+1)*256]; vec[4+i:5+i]=shown[:,i*256:(i+1)*256]
    tail[0:1]=dp[0:1]+dp[16:17]; tail[1:2]=dl
    tail[2:3]=jnp.where(lane==0,loss,jnp.where(lane==1,valid,0.0))
    tail[3:4]=tot; tail[4:8]=jnp.zeros((4,D),F32)
    pump(len(ev))
    for c in outs: c.wait()
    if comm:
        for k in swaps: k.wait_send()
        for g in gs: g.sends()

def forward_all(square,kvw,head,lat,pixels,masks,valid,labels,aux,cid=0,comm=True):
    nt=len(TENS)
    A=pl.BlockSpec(memory_space=pl.ANY); V=pl.BlockSpec(memory_space=pltpu.VMEM); S=pl.BlockSpec(memory_space=pltpu.SMEM)
    whole=[(4,2,2,2)+tshape(n) for n in TENS]
    outs=[jax.ShapeDtypeStruct(w,BF) for w in whole]
    outs+=[jax.ShapeDtypeStruct(*SAVED[m]) for m in NAMES]+[jax.ShapeDtypeStruct((8,256),F32),jax.ShapeDtypeStruct((8,D),F32)]
    DS=pltpu.SemaphoreType.DMA
    scr=[pltpu.VMEM(w,BF) for w in whole]+[pltpu.VMEM(*SAVED[m]) for m in NAMES]
    scr+=[pltpu.VMEM((512,D),BF),pltpu.VMEM((512,D),F32),pltpu.VMEM((512,CIN),BF),
          DS((nt,25)),DS((nt,25)),DS((nt,)),DS((len(NAMES),)),DS((4,)),DS((3,))]
    cp=dict(has_side_effects=True,vmem_limit_bytes=63*MB)
    if comm: cp.update(collective_id=cid)
    r=pl.pallas_call(functools.partial(forward_kernel,comm),out_shape=outs,
        in_specs=[V]*4+[A,V,S,S,V],out_specs=[A]*(nt+len(NAMES))+[V,V],scratch_shapes=scr,
        compiler_params=pltpu.CompilerParams(**cp))(square,kvw,head,lat,pixels,masks,valid,labels,aux)
    return dict(zip(TENS,r[:nt])),dict(zip(NAMES,r[nt:-2])),r[-2],r[-1]


GRADS=[N.w9,N.w8,N.w7,N.w4,N.w5,N.w6,N.w3,N.w2,N.w1,N.w0,N.kvw,N.lat]
WORDER=[N.w9,N.w8,N.w7,N.w4,N.w5,N.w6,N.w3,N.w2,N.w1,N.w0,N.kvw]
NEEDED=[N.a2,N.dg2,N.n3,N.xh3,N.rs3,N.so,N.ph,N.qkv,N.n2,N.xh2,N.rs2,N.a1,N.dg1,N.n1,N.xh1,N.rs1,N.o,N.p,N.kv,N.q,N.xb,N.xhp,N.qn,N.xh0,N.rs0,N.xh4,N.rs4]
def gshape(n): return {N.lat:(32,512),N.kvw:(64,PADC)}.get(n,(32,D))
RING=4; SRING=2
GAP=3
TICKS=2*11+6*GAP+1


def backward_kernel(comm,classes,*refs):
    refs=list(refs)
    wt={n:refs.pop(0) for n in WORDER}
    sv={n:refs.pop(0) for n in NEEDED}
    vec,tail,aux=[refs.pop(0) for _ in range(3)]
    sq_out=refs.pop(0)
    kv_out,lat_out,vec_out,small_out=[refs.pop(0) for _ in range(4)]
    nt=len(GRADS)
    part=[refs.pop(0) for _ in range(nt)]
    send_ring=[refs.pop(0) for _ in range(SRING)]; send_kv,send_lat=refs.pop(0),refs.pop(0)
    core_ring=[refs.pop(0) for _ in range(RING)]; core_kv,core_lat=refs.pop(0),refs.pop(0)
    rbuf=[{k:refs.pop(0) for k in recv_shapes(*gshape(n)) if k!=N.core} for n in GRADS]
    wslot=[refs.pop(0) for _ in range(2)]; kslot=refs.pop(0)
    aslot=[refs.pop(0) for _ in range(2)]; xslot,rslot=refs.pop(0),refs.pop(0)
    gslot,hslot,qkvslot,xbslot,xhpslot=[refs.pop(0) for _ in range(5)]
    dh,dn,g,dp,dqkv=[refs.pop(0) for _ in range(5)]
    vbuf,srecv,ssend=[refs.pop(0) for _ in range(3)]
    wsem,asem,hsem,ssem,rsem,vs,vr,sms,smr,usem=refs
    me=where_am_i(); nb=neighbours(me)
    z,y,x,c=(me[i] for i in N.zyxc)
    first=c==0
    A=[N.a2,N.n3,N.so,N.n2,N.a1,N.n1,N.o,N.qn]
    X=[N.xh4,N.xh3,N.xh2,N.xh1,N.xh0]; R=[N.rs4,N.rs3,N.rs2,N.rs1,N.rs0]
    place={n:aslot[i%2] for i,n in enumerate(A)}
    place.update({n:xslot for n in X}); place.update({n:rslot for n in R})
    place.update(dg2=gslot,dg1=gslot,p=hslot.at[1],qkv=qkvslot,xb=xbslot,xhp=xhpslot)
    wi=[n for n in WORDER if n!=N.kvw]
    place.update({n:wslot[i%2] for i,n in enumerate(wi)}); place[N.kvw]=kslot
    live={}
    def load(*names):
        for n in names:
            if n in WORDER: cs=[pltpu.make_async_copy(wt[n],place[n],wsem.at[WORDER.index(n)])]
            elif n==N.kv:
                cs=[pltpu.make_async_copy(sv[n].at[:,pl.ds(0,D)],qkvslot.at[1],asem.at[NEEDED.index(n)]),
                    pltpu.make_async_copy(sv[n].at[:,pl.ds(D,D)],qkvslot.at[2],asem.at[len(NEEDED)])]
            elif n==N.q: cs=[pltpu.make_async_copy(sv[n],qkvslot.at[0],asem.at[NEEDED.index(n)])]
            else: cs=[pltpu.make_async_copy(sv[n],place[n],asem.at[NEEDED.index(n)])]
            for k in cs: k.start()
            live[n]=cs
    def use(n):
        for k in live.pop(n): k.wait()
        return place.get(n)
    def load_head(i):
        k=pltpu.make_async_copy(sv[N.ph].at[i],hslot.at[i%2],hsem.at[i]); k.start(); live[(N.ph+str(i))]=[k]
    load(N.xh4,N.rs4,N.w9,N.a2,N.dg2,N.w8,N.n3,N.qkv)
    for i in range(2): load_head(i)
    vbuf[z,y,x,c]=vec[...]
    if comm: entry_barrier(me,nb,small_steps(me)[4:])
    gs=[]
    rings={}
    for t,n in enumerate(GRADS):
        if n==N.kvw: sb,cb=send_kv,core_kv
        elif n==N.lat: sb,cb=send_lat,core_lat
        else:
            k=wi.index(n); sb,cb=send_ring[k%SRING],core_ring[k%RING]
        out={N.kvw:kv_out,N.lat:lat_out}.get(n)
        gs.append(Scatter(me,nb,part[t],sb,dict(rbuf[t],core=cb),out,SPLIT[gshape(n)[1]],ssem.at[t],rsem.at[t]))
    gv=Gather(me,nb,vbuf,[(0,0),(0,0),(0,vbuf.shape[-1])],vs,vr)
    queue={}
    for tick in range(TICKS):
        q=[]
        if tick%4==0 and tick//4<=6: q.append(functools.partial(gv.phase,tick//4))
        for t in range(nt):
            p=tick-2*t
            if p>0 and p%GAP==0 and p//GAP<=6: q.append(functools.partial(gs[t].phase,p//GAP))
        queue[tick]=q
    now=[0]
    def pump(k):
        if not comm: return
        for _ in range(k):
            if queue[now[0]]: queue[now[0]].pop(0)()
    waited=set()
    def before_store(n):
        if n in wi and wi.index(n)>=SRING and comm:
            o=GRADS.index(wi[wi.index(n)-SRING]); gs[o].core(N.send); waited.add(o)
    def half():
        if comm and now[0]%2:
            pump(len(queue[now[0]]))
            now[0]+=1
    def push(n):
        if not comm: return
        half()
        pump(len(queue[now[0]]))
        assert GRADS[now[0]//2]==n
        gs[now[0]//2].phase(0)
        now[0]+=1
    def store(n,v,r0,cols):
        t=GRADS.index(n); r=gshape(n)[0]; k=v.shape[0]//(2*r)
        v=v.astype(BF).reshape(k,2,r,v.shape[1])
        own=jnp.where(first,v[:,0],v[:,1]); other=jnp.where(first,v[:,1],v[:,0])
        b0=r0//(2*r)
        for ref,val in ((part[t],own),(gs[t].half,other)):
            if k==16: ref[:,:,:,:,cols]=val.reshape(4,2,2,r,v.shape[-1])
            elif k>=4: ref[b0//4:(b0+k)//4,:,:,:,cols]=val.reshape(k//4,2,2,r,v.shape[-1])
            else: ref[b0//4,(b0%4)//2,:,:,cols]=val.reshape(2,r,v.shape[-1])
    def weight_grad(n,a,dy):
        before_store(n)
        for j in range(2):
            cols=pl.ds(j*512,512)
            store(n,dot(a[...],dy[:,cols],TN),0,cols)
            pump(1)
        push(n)
    def back(dy,w,epi):
        for j in range(2):
            rows=w[2*j:2*j+2].reshape(512,D)
            epi(pl.ds(j*512,512),dot(dy[...],rows,NT))
            pump(1 if j==0 else 0)
        half()
    gain=lambda i: aux[i:i+1,:]
    def norm_back(load_dn,gn,xh,rs,base,store_to):
        def body(i,tot):
            rows=pl.ds(i*RB,RB)
            d=load_dn(rows); xv=xh[rows].astype(F32)
            dx=d*gn
            m1=jnp.sum(dx,-1,keepdims=True)/D; m2=jnp.sum(dx*xv,-1,keepdims=True)/D
            r=rs[rows][:,0:1]*(dx-m1-xv*m2)
            if base is not None: r=r+base[rows]
            store_to(rows,r)
            return tot+jnp.sum(d*xv,0,keepdims=True)
        tot=jnp.zeros((1,D),F32)
        for i in range(ROWS//RB): tot=body(i,tot)
        return tot
    def to_dh(rows,r):
        dh[rows]=r; g[rows]=r.astype(BF)
    def to_dn(cols,acc): dn[:,cols]=acc
    def to_dp(cols,acc): dp[:,cols]=acc.astype(BF)
    small=ssend.at[0]
    const=tail[0:1]*(1/ROWS)
    use(N.rs4)
    dg=norm_back(lambda r: jnp.broadcast_to(const,(RB,D)),gain(4),use(N.xh4),place[N.rs4],None,to_dh)
    small[4:5]=dg
    small[5:8]=jnp.zeros((3,D),F32)
    lane=lax.broadcasted_iota(jnp.int32,(1,D),1)
    turned=pltpu.roll(tail[...],CIN,1)[1:2]
    small[6:7]=jnp.where(lane<classes-(D-CIN),turned,0.0)
    small[7:8]=tail[2:3]
    load(N.xh3,N.rs3)
    def mlp_back(wo,wi_,act,normed,dgn,xh,rs,row,nxt):
        a=use(act)
        weight_grad(wo,a,g)
        load(*nxt[0])
        w=use(wo); d=use(dgn)
        def epi(cols,acc): dp[:,cols]=(acc*d[:,cols].astype(F32)).astype(BF)
        back(g,w,epi)
        load(*nxt[1])
        weight_grad(wi_,use(normed),dp)
        load(*nxt[2])
        back(dp,use(wi_),to_dn)
        load(*nxt[3])
        use(rs)
        small[row:row+1]=norm_back(lambda r: dn[r],gain(row),use(xh),place[rs],dh,to_dh)
    mlp_back(N.w9,N.w8,N.a2,N.n3,N.dg2,N.xh3,N.rs3,3,([ N.so],[N.w7,N.dg1],[N.n2],[N.w4]))
    load(N.xh2,N.rs2)
    weight_grad(N.w7,use(N.so),g)
    load(N.a1)
    back(g,use(N.w7),to_dp)
    load(N.w5)
    use(N.qkv)
    sc=128**-0.5
    for i in range(8):
        cols=pl.ds(i*128,128)
        use((N.ph+str(i))); ph=hslot.at[i%2]
        qh,kh,vh=(qkvslot[k,:,cols] for k in range(3)); do=dp[:,cols]
        pf=ph[...].astype(F32)
        dpr=dot(do,vh,NT)
        ds=(pf*(dpr-jnp.sum(pf*dpr,-1,keepdims=True)/jnp.sum(pf,-1,keepdims=True))).astype(BF)
        dqkv[0,:,cols]=(dot(ds,kh)*sc).astype(BF)
        dqkv[1,:,cols]=(dot(ds,qh,TN)*sc).astype(BF)
        dqkv[2,:,cols]=dot(ph[...],do,TN).astype(BF)
        if i+2<8: load_head(i+2)
        pump(1)
    load(N.q,N.kv,N.p,N.xb,N.xhp)
    n2=use(N.n2)
    for i in range(3):
        weight_grad((N.w+str(4+i)),n2,dqkv.at[i])
        if i==2: load(N.n1)
        if i==0: back(dqkv.at[0],use(N.w4),to_dn)
        else:
            def add_dn(cols,acc): dn[:,cols]=dn[:,cols]+acc
            back(dqkv.at[i],use((N.w+str(4+i))),add_dn)
        load((N.w6,N.w3,N.w2)[i])
    use(N.rs2)
    small[2:3]=norm_back(lambda r: dn[r],gain(2),use(N.xh2),place[N.rs2],dh,to_dh)
    load(N.xh1,N.rs1)
    mlp_back(N.w3,N.w2,N.a1,N.n1,N.dg1,N.xh1,N.rs1,1,([N.o],[N.w1,N.kvw],[N.qn],[N.w0]))
    load(N.xh0,N.rs0)
    weight_grad(N.w1,use(N.o),g)
    back(g,use(N.w1),to_dp)
    use(N.q); use(N.kv); p=use(N.p)
    q,k,v=(qkvslot.at[i] for i in range(3))
    dpr=dot(dp[...],v[...],NT)
    pf=p[...].astype(F32)
    ds=(pf*(dpr-jnp.sum(pf*dpr,-1,keepdims=True)/jnp.sum(pf,-1,keepdims=True))).astype(BF)
    for j in range(2):
        cols=pl.ds(j*512,512)
        dqkv[0,:,cols]=(dot(ds,k[:,cols])*(1/32)).astype(BF)
        pump(1)
    weight_grad(N.w0,use(N.qn),dqkv.at[0])
    for j in range(2):
        cols=pl.ds(j*512,512)
        dqkv[1,:,cols]=(dot(ds,q[:,cols],TN)*(1/32)).astype(BF)
        dqkv[2,:,cols]=dot(p[...],dp[:,cols],TN).astype(BF)
        pump(1)
    half()
    xb=use(N.xb)
    for i in (0,1):
        store(N.kvw,dot(dqkv[1+i],xb[...],TN),i*D,pl.ds(0,PADC))
        pump(1)
    push(N.kvw)
    back(dqkv.at[0],use(N.w0),to_dn)
    use(N.rs0)
    def to_h(rows,r): dh[rows]=r
    small[0:1]=norm_back(lambda r: dn[r],gain(0),use(N.xh0),place[N.rs0],dh,to_h)
    for i in range(8):
        store(N.lat,dh[:,i*128:(i+1)*128].T,i*128,pl.ds(0,512))
    push(N.lat)
    kw=use(N.kvw); xp=use(N.xhp)
    dx=dot(dqkv[1],kw[0:2].reshape(D,PADC))+dot(dqkv[2],kw[2:4].reshape(D,PADC))
    dpg=jnp.concatenate([jnp.sum(dx*xp[...].astype(F32),0,keepdims=True),jnp.zeros((1,D-PADC),F32)],1)
    small[5:6]=jnp.where(lane<CIN,dpg,turned)
    if comm:
        sm=[pltpu.make_async_remote_copy(src_ref=ssend.at[i],dst_ref=srecv.at[i],send_sem=sms.at[i],recv_sem=smr.at[i],device_id=q_,device_id_type=MESH) for i,q_ in enumerate(small_steps(me))]
        def small_step(i):
            if i>0:
                sm[i-1].wait_recv()
                r=ssend[i-1]+srecv[i-1]
                if i<5: ssend[i]=r
                else: small_out[...]=r
            if i<5: sm[i].start()
        writes=[]
        step=0
        for tick in range(now[0],TICKS):
            if step<=5: small_step(step); step+=1
            for e in queue[tick]: e()
        for t,n in enumerate(GRADS):
            if n[0]==N.w:
                k=pltpu.make_async_copy(part[t].at[z,y,x],sq_out.at[int(n[1])],usem.at[t]); k.start(); writes.append(k)
        while step<=5: small_step(step); step+=1
        for k in writes: k.wait()
        for s_ in sm: s_.wait_send()
        gv.sends()
        for t,s_ in enumerate(gs):
            if t not in waited: s_.core(N.send)
            for r in range(3):
                for ph_ in range(5): s_.do(r,ph_,N.send)
    else:
        small_out[...]=ssend[0]
        kv_out[...]=jnp.zeros_like(kv_out); lat_out[...]=jnp.zeros_like(lat_out)
    vec_out[...]=vbuf[...]

def backward_all(w,sv,vec,tail,aux,classes,cid=1,comm=True):
    A=pl.BlockSpec(memory_space=pl.ANY); V=pl.BlockSpec(memory_space=pltpu.VMEM)
    DS=pltpu.SemaphoreType.DMA
    M=pltpu.VMEM
    nt=len(GRADS)
    outs=[jax.ShapeDtypeStruct((10,32,D),BF)]+[jax.ShapeDtypeStruct((64,PADC),F32),jax.ShapeDtypeStruct((32,512),F32),
          jax.ShapeDtypeStruct((4,2,2,2,8,256),F32),jax.ShapeDtypeStruct((8,D),F32)]
    scr=[M((4,2,2)+gshape(n),BF) for n in GRADS]
    half=lambda n: M((4,2,2)+gshape(n),BF)
    scr+=[half(N.w0)]*SRING+[half(N.kvw),half(N.lat)]+[half(N.w0)]*RING+[half(N.kvw),half(N.lat)]
    for n in GRADS:
        scr+=[M(v,BF) for k,v in recv_shapes(*gshape(n)).items() if k!=N.core]
    scr+=[M((4,2,2,2,32,D),BF)]*2+[M((4,2,2,2,64,PADC),BF)]
    scr+=[M((512,D),BF)]*3+[M((512,128),F32)]
    scr+=[M((512,D),BF),M((2,512,512),BF),M((3,512,D),BF),M((512,PADC),BF),M((512,PADC),BF)]
    scr+=[M((512,D),F32),M((512,D),F32),M((512,D),BF),M((512,D),BF),M((3,512,D),BF)]
    scr+=[M((4,2,2,2,8,256),F32),M((5,8,D),F32),M((5,8,D),F32)]
    scr+=[DS((len(WORDER),)),DS((len(NEEDED)+1,)),DS((8,)),DS((nt,25)),DS((nt,25)),DS((25,)),DS((25,)),DS((5,)),DS((5,)),DS((nt,))]
    cp=dict(has_side_effects=True,vmem_limit_bytes=63*MB+MB//2)
    if comm: cp[N.collective_id]=cid
    return pl.pallas_call(functools.partial(backward_kernel,comm,classes),out_shape=outs,
        in_specs=[A]*(len(WORDER)+len(NEEDED))+[V]*3,out_specs=[A]+[V]*4,scratch_shapes=scr,
        compiler_params=pltpu.CompilerParams(**cp))(*[w[n] for n in WORDER],*[sv[n] for n in NEEDED],vec,tail,aux)


STEP=5

def update_kernel(latent_rate,*refs):
    refs=list(refs)
    grads,kv_g,lat_g,vec,packed=[refs.pop(0) for _ in range(5)]
    old=[[refs.pop(0) for _ in range(3)] for _ in range(4)]
    new=[[refs.pop(0) for _ in range(4)] for _ in range(4)]
    count=jnp.maximum(packed[7:8,1:2],1.0)
    first=(lax.axis_index(N.dp)*lax.axis_size(N.head)+lax.axis_index(N.head))*old[2][0].shape[0]
    def step(total,weight,outs,at,rate):
        w,m,a=(r[at] for r in weight)
        g=total/count
        mom=MOMENTUM*m+g
        wn=w-rate*(g+MOMENTUM*mom)
        for r,v in zip(outs,(g,mom,wn,AVERAGE_DECAY*a+(1.0-AVERAGE_DECAY)*wn)): r[at]=v
    for i in range(STEP): step(grads[i].astype(F32),old[0],new[0],(i,),LEARN_RATE)
    @pl.when(pl.program_id(0)==0)
    def _():
        step(kv_g[:,0:CIN],old[1],new[1],(slice(None),),LEARN_RATE)
        step(lat_g[...],old[3],new[3],(slice(None),),latent_rate)
        rows=old[2][0].shape[0]; classes=old[2][0].shape[1]
        images=vec.shape[0]
        own=jnp.zeros((images,rows),F32)
        for i in range(4):
            pick=lax.broadcasted_iota(jnp.int32,(256,rows),0)+256*i==first+lax.broadcasted_iota(jnp.int32,(256,rows),1)
            own=own+dot(vec[:,i,:].astype(BF),pick.astype(BF))
        own=own.astype(BF)
        for i in range(4):
            n=min(256,classes-256*i)
            dl=vec[:,4+i,:]
            hi=dl.astype(BF); rest=dl-hi.astype(F32); mid=rest.astype(BF); lo=(rest-mid.astype(F32)).astype(BF)
            g=dot(own,hi,TN)+dot(own,mid,TN)+dot(own,lo,TN)
            step(g[:,0:n],old[2],new[2],(slice(None),slice(256*i,256*i+n)),LEARN_RATE)

def update_all(grads,kv_g,lat_g,vec,packed,square,kv,head,lat,latent_rate):
    one=lambda v: pl.BlockSpec(v.shape,lambda i,n=v.ndim: (0,)*n)
    sq=pl.BlockSpec((STEP,)+grads.shape[1:],lambda i: (i,0,0))
    outs=[jax.ShapeDtypeStruct(g[0].shape,F32) for g in (square,kv,head,lat) for _ in range(4)]
    out_specs=[sq]*4+[one(g[0]) for g in (kv,head,lat) for _ in range(4)]
    in_specs=[sq]+[one(v) for v in (kv_g,lat_g,vec,packed)]+[sq]*3+[one(v) for g in (kv,head,lat) for v in g]
    return pl.pallas_call(functools.partial(update_kernel,latent_rate),out_shape=outs,grid=(grads.shape[0]//STEP,),in_specs=in_specs,out_specs=out_specs,
        compiler_params=pltpu.CompilerParams(vmem_limit_bytes=63*MB))(grads,kv_g,lat_g,vec,packed,*square,*kv,*head,*lat)


def per_device_images(
    pixels,
    masks,
    valid,
    labels,
    square,
    kv_weight,
    head_weight,
    latents,
    small,
    square_mom,
    kv_mom,
    head_mom,
    latent_mom,
    small_mom,
    square_avg,
    kv_avg,
    head_avg,
    latent_avg,
    small_avg,
):
    classes = head_weight.shape[1]
    aux = jnp.pad(small, (0, 8 * D - small.shape[0])).reshape(8, D)
    weights, saved, vec, tail = forward_all(
        square, kv_weight.T, head_weight, latents.T, pixels, masks, valid.T, labels.T, aux
    )
    grads, d_kv, d_lat, vec_all, packed = backward_all(weights, saved, vec, tail, aux, classes)
    latent_rate = LATENTS * math.sqrt(D * MICRO * IMG_DEV * lax.axis_size(N.dp)) / 32.0
    new = update_all(
        grads,
        d_kv,
        d_lat,
        vec_all.reshape(-1, 8, 256),
        packed,
        (square, square_mom, square_avg),
        (kv_weight.T, kv_mom.T, kv_avg.T),
        (head_weight, head_mom, head_avg),
        (latents.T, latent_mom.T, latent_avg.T),
        latent_rate,
    )
    loss_sum, count = packed[7, 0], jnp.maximum(packed[7, 1], 1.0)
    small_total = packed.reshape(-1)[: small.shape[0]]
    small_new = nesterov(small, small_total / count, small_mom, small_avg, LEARN_RATE)
    turned = lambda group: [v.T for v in group]
    return (loss_sum, count, *new[:4], *turned(new[4:8]), *new[8:12], *turned(new[12:]), *small_new)


def solution(mesh):
    in_specs = (
        P(None, "dp", "head", None),
        P(None, "dp", None),
        P(None, "dp"),
        P(None, "dp"),
        P(None, ("dp", "head"), None),
        P(None, ("dp", "head")),
        P(("dp", "head"), None),
        P(None, ("dp", "head")),
        P(),
        P(None, ("dp", "head"), None),
        P(None, ("dp", "head")),
        P(("dp", "head"), None),
        P(None, ("dp", "head")),
        P(),
        P(None, ("dp", "head"), None),
        P(None, ("dp", "head")),
        P(("dp", "head"), None),
        P(None, ("dp", "head")),
        P(),
    )
    out_specs = (
        P(),
        P(),
        P(None, ("dp", "head"), None),
        P(None, ("dp", "head"), None),
        P(None, ("dp", "head"), None),
        P(None, ("dp", "head"), None),
        P(None, ("dp", "head")),
        P(None, ("dp", "head")),
        P(None, ("dp", "head")),
        P(None, ("dp", "head")),
        P(("dp", "head"), None),
        P(("dp", "head"), None),
        P(("dp", "head"), None),
        P(("dp", "head"), None),
        P(None, ("dp", "head")),
        P(None, ("dp", "head")),
        P(None, ("dp", "head")),
        P(None, ("dp", "head")),
        P(),
        P(),
        P(),
        P(),
    )
    whole_images = dict(mesh.shape) == {"dp": 8, "head": MICRO}
    per_device = per_device_images if whole_images else per_device_rows
    return jax.shard_map(
        per_device, mesh=mesh, in_specs=in_specs, out_specs=out_specs, check_vma=False
    )
```

```python
import functools
import math

import jax
import jax.numpy as jnp
from jax import lax
from jax.experimental import pallas as pl
from jax.experimental.pallas import tpu as pltpu
from jax.sharding import PartitionSpec as P

D = 1024
CIN = 261
LATENTS = 512
HEADS = 8
HEAD_DIM = 128
MICRO = 4
IMG_DEV = 1


EPS = 1e-05
NEG_BIG = -1e30
SMOOTH = 0.1
LEARN_RATE = 20.0
MOMENTUM = 0.9
AVERAGE_DECAY = 0.6


def layer_norm(v, gain):
    mean = jnp.mean(v, axis=-1, keepdims=True)
    cent = v - mean
    var = jnp.mean(cent * cent, axis=-1, keepdims=True)
    return cent * lax.rsqrt(var + EPS) * gain


def dot_nn(left, right):
    return jnp.dot(left, right, preferred_element_type=jnp.float32)


def dot_tn(left, right):
    return lax.dot_general(
        left, right, (((0,), (0,)), ((), ())), preferred_element_type=jnp.float32
    )


def dot_nt(left, right):
    return lax.dot_general(
        left, right, (((1,), (1,)), ((), ())), preferred_element_type=jnp.float32
    )


def scores_of(query, keys, valid_keys):
    scores = jnp.einsum("qhd,khd->hqk", query, keys, preferred_element_type=jnp.float32)
    scores = scores * query.shape[-1] ** (-0.5)
    if valid_keys is not None:
        scores = jnp.where(valid_keys[None, None, :], scores, NEG_BIG)
    return scores


def attend(query, keys, values, valid_keys):
    scores = scores_of(query, keys, valid_keys)
    log_total = jax.nn.logsumexp(scores, axis=-1, keepdims=True)
    probs = jnp.exp(scores - log_total).astype(jnp.bfloat16)
    out = jnp.einsum("hqk,khd->qhd", probs, values, preferred_element_type=jnp.float32)
    return (out.astype(jnp.bfloat16), log_total)


def attend_back(query, keys, values, log_total, d_out, valid_keys):
    scale = query.shape[-1] ** (-0.5)
    probs = jnp.exp(scores_of(query, keys, valid_keys) - log_total)
    probs_b = probs.astype(jnp.bfloat16)
    d_probs = jnp.einsum("qhd,khd->hqk", d_out, values, preferred_element_type=jnp.float32)
    d_scores = probs * (d_probs - jnp.sum(probs * d_probs, axis=-1, keepdims=True))
    d_scores = d_scores.astype(jnp.bfloat16)
    d_query = jnp.einsum("hqk,khd->qhd", d_scores, keys, preferred_element_type=jnp.float32) * scale
    d_keys = jnp.einsum("hqk,qhd->khd", d_scores, query, preferred_element_type=jnp.float32) * scale
    d_values = jnp.einsum("hqk,qhd->khd", probs_b, d_out, preferred_element_type=jnp.float32)
    return (d_query, d_keys, d_values)


def mlp_forward(hidden, gain, w_in, w_out):
    normed = layer_norm(hidden, gain).astype(jnp.bfloat16)
    pre = dot_nn(normed, w_in)
    active = jax.nn.gelu(pre).astype(jnp.bfloat16)
    return (hidden + dot_nn(active, w_out), (normed, pre, active))


def mlp_backward(hidden, gain, w_in, w_out, saved, d_next):
    normed, pre, active = saved
    d_next_b = d_next.astype(jnp.bfloat16)
    d_w_out = dot_tn(active, d_next_b)
    d_active = dot_nt(d_next_b, w_out)
    d_pre = jax.vjp(jax.nn.gelu, pre)[1](d_active)[0].astype(jnp.bfloat16)
    d_w_in = dot_tn(normed, d_pre)
    d_normed = dot_nt(d_pre, w_in)
    d_hidden, d_gain = jax.vjp(layer_norm, hidden, gain)[1](d_normed)
    return (d_next + d_hidden, d_gain, d_w_in, d_w_out)


def image_grads(weights, small, pixel_own, mask_row, valid_one, label, loss_scale, head_first):
    square, kv_weight, head_weight, latent_all, w_qkv = weights
    gains = small[: 5 * D].reshape(5, D)
    pix_gain = small[5 * D : 5 * D + CIN]
    bias = small[5 * D + CIN :]
    rows = latent_all.shape[0] // lax.axis_size("head")
    start = lax.axis_index("head") * rows
    latent_own = lax.dynamic_slice_in_dim(latent_all, start, rows, 0).astype(jnp.float32)
    valid_keys = mask_row > 0
    pix_float = pixel_own.astype(jnp.float32)
    normed_pix = layer_norm(pix_float, pix_gain).astype(jnp.bfloat16)
    kv_own = dot_nn(normed_pix, kv_weight).astype(jnp.bfloat16)
    kv_all = lax.all_gather(kv_own, "head", axis=0, tiled=True)
    keys_px = kv_all[:, :D].reshape(-1, 1, D)
    values_px = kv_all[:, D:].reshape(-1, 1, D)
    query_norm = layer_norm(latent_own, gains[0]).astype(jnp.bfloat16)
    query = dot_nn(query_norm, square[0]).astype(jnp.bfloat16).reshape(rows, 1, D)
    cross_out, cross_total = attend(query, keys_px, values_px, valid_keys)
    cross_out = cross_out.reshape(rows, D)
    hidden1 = latent_own + dot_nn(cross_out, square[1])
    hidden2, mlp_first = mlp_forward(hidden1, gains[1], square[2], square[3])
    self_norm = layer_norm(hidden2, gains[2]).astype(jnp.bfloat16)
    qkv = dot_nn(self_norm, w_qkv).astype(jnp.bfloat16)
    kv_latent = lax.all_gather(qkv[:, D:], "head", axis=0, tiled=True)
    self_query = qkv[:, :D].reshape(rows, HEADS, HEAD_DIM)
    self_keys = kv_latent[:, :D].reshape(-1, HEADS, HEAD_DIM)
    self_values = kv_latent[:, D:].reshape(-1, HEADS, HEAD_DIM)
    self_out, self_total = attend(self_query, self_keys, self_values, None)
    self_out = self_out.reshape(rows, D)
    hidden3 = hidden2 + dot_nn(self_out, square[7])
    hidden4, mlp_second = mlp_forward(hidden3, gains[3], square[8], square[9])
    final = layer_norm(hidden4, gains[4])
    pooled = lax.psum(jnp.sum(final, axis=0), "head") / latent_all.shape[0]
    pooled_b = pooled.astype(jnp.bfloat16)
    logits = dot_nn(pooled_b[None, :], head_weight)[0] + bias
    logp = jax.nn.log_softmax(logits)
    picked = jnp.arange(logits.shape[0]) == label
    loss = -valid_one * (
        (1.0 - SMOOTH) * jnp.sum(jnp.where(picked, logp, 0.0)) + SMOOTH * jnp.mean(logp)
    )
    target = (1.0 - SMOOTH) * picked.astype(jnp.float32) + SMOOTH / logits.shape[0]
    d_logits = valid_one * loss_scale * (jnp.exp(logp) - target)
    d_bias = d_logits * head_first
    d_head = pooled_b.astype(jnp.float32)[:, None] * d_logits[None, :] * head_first
    d_pooled = jnp.dot(head_weight.astype(jnp.float32), d_logits)
    d_final = jnp.broadcast_to(d_pooled / latent_all.shape[0], final.shape)
    d_hidden4, d_gain4 = jax.vjp(layer_norm, hidden4, gains[4])[1](d_final)
    d_hidden3, d_gain3, d_w8, d_w9 = mlp_backward(
        hidden3, gains[3], square[8], square[9], mlp_second, d_hidden4
    )
    d_hidden3_b = d_hidden3.astype(jnp.bfloat16)
    d_w7 = dot_tn(self_out, d_hidden3_b)
    d_self_out = dot_nt(d_hidden3_b, square[7]).astype(jnp.bfloat16).reshape(rows, HEADS, HEAD_DIM)
    d_query, d_keys, d_values = attend_back(
        self_query, self_keys, self_values, self_total, d_self_out, None
    )
    d_kv_terms = jnp.concatenate([d_keys.reshape(-1, D), d_values.reshape(-1, D)], axis=1)
    d_kv_own = lax.psum_scatter(
        d_kv_terms.astype(jnp.bfloat16), "head", scatter_dimension=0, tiled=True
    ).astype(jnp.float32)
    d_qkv = jnp.concatenate([d_query.reshape(rows, D), d_kv_own], axis=1).astype(jnp.bfloat16)
    d_w_qkv = dot_tn(self_norm, d_qkv)
    d_self_norm = dot_nt(d_qkv, w_qkv)
    d_hidden2_norm, d_gain2 = jax.vjp(layer_norm, hidden2, gains[2])[1](d_self_norm)
    d_hidden2 = d_hidden3 + d_hidden2_norm
    d_hidden1, d_gain1, d_w2, d_w3 = mlp_backward(
        hidden1, gains[1], square[2], square[3], mlp_first, d_hidden2
    )
    d_hidden1_b = d_hidden1.astype(jnp.bfloat16)
    d_w1 = dot_tn(cross_out, d_hidden1_b)
    d_cross = dot_nt(d_hidden1_b, square[1]).astype(jnp.bfloat16).reshape(rows, 1, D)
    d_query, d_keys, d_values = attend_back(
        query, keys_px, values_px, cross_total, d_cross, valid_keys
    )
    d_px_terms = jnp.concatenate([d_keys.reshape(-1, D), d_values.reshape(-1, D)], axis=1)
    d_kv_px = lax.psum_scatter(
        d_px_terms.astype(jnp.bfloat16), "head", scatter_dimension=0, tiled=True
    )
    d_kv_turned = dot_tn(d_kv_px, normed_pix)
    d_normed_pix = dot_nt(d_kv_px, kv_weight)
    d_pix_gain = jax.vjp(layer_norm, pix_float, pix_gain)[1](d_normed_pix)[1]
    d_query_b = d_query.reshape(rows, D).astype(jnp.bfloat16)
    d_w0 = dot_tn(query_norm, d_query_b)
    d_query_norm = dot_nt(d_query_b, square[0])
    d_latent_norm, d_gain0 = jax.vjp(layer_norm, latent_own, gains[0])[1](d_query_norm)
    d_latent_own = d_hidden1 + d_latent_norm
    d_square = jnp.stack(
        [
            d_w0,
            d_w1,
            d_w2,
            d_w3,
            d_w_qkv[:, :D],
            d_w_qkv[:, D : 2 * D],
            d_w_qkv[:, 2 * D :],
            d_w7,
            d_w8,
            d_w9,
        ]
    )
    latent_turned = lax.dynamic_update_slice_in_dim(
        jnp.zeros((D, latent_all.shape[0]), jnp.float32), d_latent_own.T, start, 1
    )
    d_small = jnp.concatenate(
        [jnp.stack([d_gain0, d_gain1, d_gain2, d_gain3, d_gain4]).reshape(-1), d_pix_gain, d_bias]
    )
    return ((d_square, d_kv_turned[None], d_head[None], latent_turned[None], d_small), loss)


def owner_layout(reduced):
    return (reduced[0], reduced[1][0].T, reduced[2][0], reduced[3][0].T)


def nesterov(weight, grad, mom, avg, rate):
    mom_new = MOMENTUM * mom + grad
    weight_new = weight - rate * (grad + MOMENTUM * mom_new)
    avg_new = AVERAGE_DECAY * avg + (1.0 - AVERAGE_DECAY) * weight_new
    return (grad, mom_new, weight_new, avg_new)


def per_device_rows(
    pixels,
    masks,
    valid,
    labels,
    square,
    kv_weight,
    head_weight,
    latents,
    small,
    square_mom,
    kv_mom,
    head_mom,
    latent_mom,
    small_mom,
    square_avg,
    kv_avg,
    head_avg,
    latent_avg,
    small_avg,
):
    gathered = (
        lax.all_gather(square.astype(jnp.bfloat16), ("dp", "head"), axis=1, tiled=True),
        lax.all_gather(kv_weight.astype(jnp.bfloat16), ("dp", "head"), axis=1, tiled=True),
        lax.all_gather(head_weight.astype(jnp.bfloat16), ("dp", "head"), axis=0, tiled=True),
        lax.all_gather(latents.astype(jnp.bfloat16), ("dp", "head"), axis=1, tiled=True),
    )
    full_square = gathered[0]
    w_qkv = jnp.concatenate([full_square[4], full_square[5], full_square[6]], axis=1)
    weights = (full_square, gathered[1], gathered[2], gathered[3], w_qkv)
    head_first = (lax.axis_index("head") == 0).astype(jnp.float32)
    valid_float = valid.astype(jnp.float32)
    early_count = lax.psum(jnp.sum(valid_float), "dp")
    loss_scale = 1.0 / jnp.maximum(early_count, 1.0)
    kv_shape = gathered[1].shape
    lat_shape = gathered[3].shape
    big_zero = (
        jnp.zeros(full_square.shape, jnp.float32),
        jnp.zeros((1, kv_shape[1], kv_shape[0]), jnp.float32),
        jnp.zeros((1,) + gathered[2].shape, jnp.float32),
        jnp.zeros((1, lat_shape[1], lat_shape[0]), jnp.float32),
    )

    def micro_step(carry, batch):
        big, small_acc, loss_acc = carry
        pix_micro, mask_micro, valid_micro, label_micro = batch
        grads, loss_part = image_grads(
            weights,
            small,
            pix_micro[0],
            mask_micro[0],
            valid_micro[0],
            label_micro[0],
            loss_scale,
            head_first,
        )
        reduced = (grads[0], grads[1], grads[2], grads[3])
        big = tuple((a + b for a, b in zip(big, reduced)))
        return ((big, small_acc + grads[4], loss_acc + loss_part), None)

    start_carry = (big_zero, jnp.zeros(small.shape, jnp.float32), jnp.float32(0.0))
    (big, small_acc, loss_acc), _ = lax.scan(
        micro_step, start_carry, (pixels, masks, valid_float, labels)
    )
    big = owner_layout(
        (
            lax.psum_scatter(big[0], ("dp", "head"), scatter_dimension=1, tiled=True),
            lax.psum_scatter(big[1], ("dp", "head"), scatter_dimension=1, tiled=True),
            lax.psum_scatter(big[2], ("dp", "head"), scatter_dimension=1, tiled=True),
            lax.psum_scatter(big[3], ("dp", "head"), scatter_dimension=1, tiled=True),
        )
    )
    small_total, loss_sum, count = lax.psum(
        (small_acc, loss_acc * head_first, jnp.sum(valid_float) * head_first), ("dp", "head")
    )
    count = jnp.maximum(count, 1.0)
    latent_rate = LATENTS * math.sqrt(D * MICRO * IMG_DEV * lax.axis_size("dp")) / 32.0
    rates = (LEARN_RATE, LEARN_RATE, LEARN_RATE, latent_rate, LEARN_RATE)
    results = [loss_sum, count]
    params = (square, kv_weight, head_weight, latents, small)
    moms = (square_mom, kv_mom, head_mom, latent_mom, small_mom)
    avgs = (square_avg, kv_avg, head_avg, latent_avg, small_avg)
    for weight, grad, mom, avg, rate in zip(params, tuple(big) + (small_total,), moms, avgs, rates):
        results.extend(nesterov(weight, grad, mom, avg, rate))
    return tuple(results)


class Names:
    def __getattr__(self, name):
        return name


N = Names()


MESH=pl.DeviceIdType.MESH
MB=1<<20

def where_am_i():
    dp=lax.axis_index(N.dp); h=lax.axis_index(N.head)
    return dict(dp=dp,h=h,z=dp//2,y=dp%2,x=h//2,c=h%2)

def neighbours(me):
    return dict(zu=(me[N.dp]+2,me[N.h]),zd=(me[N.dp]-2,me[N.h]),y=(me[N.dp]+1-2*me[N.y],me[N.h]),
                x=(me[N.dp],me[N.h]+2-4*me[N.x]),c=(me[N.dp],me[N.h]+1-2*me[N.c]))

def entry_barrier(me,nb,others=()):
    z=me[N.z]
    bar=pltpu.get_barrier_semaphore()
    for k in (N.x,N.y,N.c):
        pl.semaphore_signal(bar,inc=1,device_id=nb[k],device_id_type=MESH)
    @pl.when(z<3)
    def _(): pl.semaphore_signal(bar,inc=1,device_id=nb[N.zu],device_id_type=MESH)
    @pl.when(z>0)
    def _(): pl.semaphore_signal(bar,inc=1,device_id=nb[N.zd],device_id_type=MESH)
    for other in others:
        pl.semaphore_signal(bar,inc=1,device_id=other,device_id_type=MESH)
    pl.semaphore_wait(bar,4+(z+1)//2%2+len(others))

class Gather:
    def __init__(self,me,nb,buf,groups,ssem,rsem):
        self.me,self.nb,self.buf,self.groups,self.ssem,self.rsem=me,nb,buf,groups,ssem,rsem
        self.pending=[]
    def copy(self,src,dst,slot,dev):
        return pltpu.make_async_remote_copy(src_ref=src,dst_ref=dst,send_sem=self.ssem.at[slot],recv_sem=self.rsem.at[slot],device_id=dev,device_id_type=MESH)
    def view(self,r,*ix):
        return self.buf.at[(*ix,slice(None),pl.ds(*self.groups[r]))]
    def hopview(self,r,*ix):
        c0,w=self.groups[r]
        if r==0: w+=self.groups[1][1]
        return self.buf.at[(*ix,slice(None),pl.ds(c0,w))]
    def hop(self,r,k,op):
        if r==1: return
        z,y,x,c=(self.me[i] for i in N.zyxc)
        rest=(y,x,c) if r<2 else (slice(None),slice(None),c)
        su,sd=8*r+k-1,8*r+3+k-1
        if op==N.start:
            @pl.when((z<3)&(z>=k-1))
            def _():
                v=self.hopview(r,z-(k-1),*rest); self.copy(v,v,su,self.nb[N.zu]).start()
            @pl.when((z>0)&(z+k-1<=3))
            def _():
                v=self.hopview(r,z+(k-1),*rest); self.copy(v,v,sd,self.nb[N.zd]).start()
        elif op==N.recv:
            @pl.when(z>=k)
            def _():
                v=self.hopview(r,z-k,*rest); self.copy(v,v,su,self.nb[N.zd]).wait_recv()
            @pl.when(z+k<=3)
            def _():
                v=self.hopview(r,z+k,*rest); self.copy(v,v,sd,self.nb[N.zu]).wait_recv()
        else:
            @pl.when((z<3)&(z>=k-1))
            def _():
                v=self.hopview(r,z-(k-1),*rest); self.copy(v,v,su,self.nb[N.zu]).wait_send()
            @pl.when((z>0)&(z+k-1<=3))
            def _():
                v=self.hopview(r,z+(k-1),*rest); self.copy(v,v,sd,self.nb[N.zd]).wait_send()
    def flat(self,r,axis,op):
        z,y,x,c=(self.me[i] for i in N.zyxc)
        A=slice(None)
        if axis==N.y:
            mine={0:(A,y,x,c),1:(A,y,A,c),2:(z,y,A,c)}[r]; other={0:(A,1-y,x,c),1:(A,1-y,A,c),2:(z,1-y,A,c)}[r]; slot=8*r+6
        elif axis==N.x:
            mine={0:(A,A,x,c),1:(A,y,x,c),2:(z,y,x,c)}[r]; other={0:(A,A,1-x,c),1:(A,y,1-x,c),2:(z,y,1-x,c)}[r]; slot=8*r+7
        if op==N.start:
            v=self.view(r,*mine); self.copy(v,v,slot,self.nb[axis]).start()
        elif op==N.recv:
            v=self.view(r,*other); self.copy(v,v,slot,self.nb[axis]).wait_recv()
        else:
            v=self.view(r,*mine); self.copy(v,v,slot,self.nb[axis]).wait_send()
    def core(self,op):
        c=self.me[N.c]; A=slice(None)
        if op==N.recv:
            v=self.buf.at[A,A,A,1-c]; self.copy(v,v,24,self.nb[N.c]).wait_recv()
        else:
            v=self.buf.at[A,A,A,c]; d=self.copy(v,v,24,self.nb[N.c])
            d.start() if op==N.start else d.wait_send()
    ORDER=[[N.h1,N.h2,N.h3,N.y,N.x],[N.h1,N.h2,N.h3,N.x,N.y],[N.x,N.y,N.h1,N.h2,N.h3]]
    def do(self,r,p,op):
        n=self.ORDER[r][p]
        if n[0]==N.h: self.hop(r,int(n[1]),op)
        else: self.flat(r,n,op)
    NPH=6
    def phase(self,p):
        if p>0 and p<=5:
            for r in range(3):
                if self.groups[r][1]: self.do(r,p-1,N.recv)
                if p<5 and self.groups[r][1]: self.do(r,p,N.start)
        if p==0:
            for r in range(3):
                if self.groups[r][1]: self.do(r,0,N.start)
        if p==5: self.core(N.start)
        if p==6: self.core(N.recv)
    def sends(self):
        for r in range(3):
            if self.groups[r][1]:
                for p in range(5): self.do(r,p,N.send)
        self.core(N.send)

SPLIT={1024:((0,384),(384,384),(768,256)),512:((0,256),(256,256),(512,0)),384:((0,128),(128,256),(384,0))}


ALLS=slice(None)

def recv_shapes(r,n):
    (_,a),(_,b),(_,c)=SPLIT[n]
    d=dict(core=(4,2,2,r,n),A0=(4,2,r,a),A1=(4,r,a),Ah=(6,r,a+b),B0=(4,2,r,b),B1=(4,r,b))
    if c: d.update(Ch=(6,2,2,r,c),C0=(2,r,c),C1=(r,c))
    return d

def add_into(dst,src,cols,lead):
    for di,si in lead:
        dst[(*di,ALLS,cols)]=dst[(*di,ALLS,cols)]+src[si]

class Scatter:
    def __init__(self,me,nb,part,send_half,bufs,out,groups,ssem,rsem):
        self.me,self.nb,self.part,self.half,self.b,self.out,self.groups,self.ssem,self.rsem=me,nb,part,send_half,bufs,out,groups,ssem,rsem
    def copy(self,src,dst,slot,dev):
        return pltpu.make_async_remote_copy(src_ref=src,dst_ref=dst,send_sem=self.ssem.at[slot],recv_sem=self.rsem.at[slot],device_id=dev,device_id_type=MESH)
    def cols(self,r): return pl.ds(*self.groups[r])
    def hop(self,r,k,op):
        if r==1: return
        z,y,x=(self.me[i] for i in N.zyx)
        rest=(y,x) if r<2 else (ALLS,ALLS)
        buf=self.b[N.ABC[r]+N.h]; cols=pl.ds(self.groups[0][0],self.groups[0][1]+self.groups[1][1]) if r==0 else self.cols(r)
        su,sd=8*r+k-1,8*r+3+k-1
        up=lambda: self.copy(self.part.at[(z+k,*rest,ALLS,cols)],buf.at[k-1],su,self.nb[N.zu])
        dn=lambda: self.copy(self.part.at[(z-k,*rest,ALLS,cols)],buf.at[3+k-1],sd,self.nb[N.zd])
        if op in(N.start,N.send):
            @pl.when(z+k<=3)
            def _():
                d=up(); d.start() if op==N.start else d.wait_send()
            @pl.when(z-k>=0)
            def _():
                d=dn(); d.start() if op==N.start else d.wait_send()
        else:
            last=(k==1 and r<2)
            @pl.when((z>=1)&(z-1+k<=3))
            def _():
                self.copy(buf.at[k-1],buf.at[k-1],su,self.nb[N.zd]).wait_recv()
                self.hopadd(r,z-1+k,buf.at[k-1],cols)
            @pl.when((z<=2)&(z+1-k>=0))
            def _():
                self.copy(buf.at[3+k-1],buf.at[3+k-1],sd,self.nb[N.zu]).wait_recv()
                self.hopadd(r,z+1-k,buf.at[3+k-1],cols)
    def hopadd(self,r,d,src,cols):
        y,x=self.me[N.y],self.me[N.x]
        if r<2: add_into(self.part,src,cols,[((d,y,x),(ALLS,ALLS))])
        else: add_into(self.part,src,cols,[((d,i,j),(i,j)) for i in range(2) for j in range(2)])
    def flat(self,r,axis,op):
        z,y,x=(self.me[i] for i in N.zyx); cols=self.cols(r)
        name=N.ABC[r]
        if axis==N.x:
            mine={0:(ALLS,ALLS,1-x),1:(ALLS,y,1-x),2:(z,y,1-x)}[r]; slot=8*r+7; buf=self.b[{0:N.A0,1:N.B1,2:N.C1}[r]]
        else:
            mine={0:(ALLS,1-y,x),1:(ALLS,1-y),2:(z,1-y)}[r]; slot=8*r+6; buf=self.b[{0:N.A1,1:N.B0,2:N.C0}[r]]
        if op==N.recv:
            self.copy(buf,buf,slot,self.nb[axis]).wait_recv()
            if axis==N.x:
                lead={0:[((i,j,x),(i,j)) for i in range(4) for j in range(2)],1:[((i,y,x),(i,)) for i in range(4)],2:[((z,y,x),(ALLS,ALLS))]}[r]
            else:
                lead={0:[((i,y,x),(i,)) for i in range(4)],1:[((i,y,j),(i,j)) for i in range(4) for j in range(2)],2:[((z,y,j),(j,)) for j in range(2)]}[r]
            add_into(self.part,buf,cols,lead)
        else:
            d=self.copy(self.part.at[(*mine,)+(ALLS,)*(4-len(mine))+(cols,)],buf,slot,self.nb[axis])
            d.start() if op==N.start else d.wait_send()
    def core(self,op):
        buf=self.b[N.core]
        if op==N.recv:
            self.copy(buf,buf,24,self.nb[N.c]).wait_recv()
            @pl.loop(0,4)
            def _(i):
                for j in range(2):
                    for k in range(2):
                        self.part[i,j,k]=self.part[i,j,k]+buf[i,j,k]
        else:
            d=self.copy(self.half,buf,24,self.nb[N.c]); d.start() if op==N.start else d.wait_send()
    ORDER=[[N.x,N.y,N.h3,N.h2,N.h1],[N.y,N.x,N.h3,N.h2,N.h1],[N.h3,N.h2,N.h1,N.y,N.x]]
    def do(self,r,p,op):
        n=self.ORDER[r][p]
        if not self.groups[r][1]: return
        if n[0]==N.h: self.hop(r,int(n[1]),op)
        else: self.flat(r,n,op)
    def phase(self,p):
        if p==0: self.core(N.start); return
        if p==1: self.core(N.recv)
        for r in range(3):
            if p>=2: self.do(r,p-2,N.recv)
        for r in range(3):
            if p<=5: self.do(r,p-1,N.start)
        if p==6:
            z,y,x=(self.me[i] for i in N.zyx)
            if self.out is not None: self.out[...]=self.part[z,y,x].astype(jnp.float32)
    def sends(self):
        self.core(N.send)
        for r in range(3):
            for p in range(5): self.do(r,p,N.send)

def small_steps(me):
    dp,h=me[N.dp],me[N.h]
    z=me[N.z]
    return [(dp,h+1-2*me[N.c]),(dp,h+2-4*me[N.x]),(dp+1-2*me[N.y],h),(dp+2-4*(z%2),h),(dp+4-8*(z//2),h)]


BF=jnp.bfloat16; F32=jnp.float32
PADC=384
NN=(((1,),(0,)),((),())); NT=(((1,),(1,)),((),())); TN=(((0,),(0,)),((),()))
def dot(a,b,dims=NN): return lax.dot_general(a,b,dims,preferred_element_type=F32)
ROWS=512; TILE=512; RB=128

def norm_rows(load,gain,xhat,rstd,normed,width=D,store_sum=None):
    def body(i,tot):
        rows=pl.ds(i*RB,RB)
        v=load(rows)
        mean=jnp.sum(v,-1,keepdims=True)/width
        cent=v-mean
        var=jnp.sum(cent*cent,-1,keepdims=True)/width
        r=lax.rsqrt(var+1e-5)
        xh=cent*r
        lanes=pl.ds(0,width)
        xhat[rows,lanes]=xh.astype(BF)
        if rstd is not None: rstd[rows]=jnp.broadcast_to(r,(RB,128))
        if normed is not None: normed[rows,lanes]=(xh*gain).astype(BF)
        if tot is None: return None
        return tot+jnp.sum(xh,0,keepdims=True)
    tot=jnp.zeros((1,D),F32) if store_sum else None
    for i in range(ROWS//RB): tot=body(i,tot)
    return tot

def mm(lhs,w,epi):
    for j in range(D//TILE):
        cols=pl.ds(j*TILE,TILE)
        epi(cols,dot(lhs[...],w[:,:,:,:,:,cols].reshape(D,TILE)))

def gelu_pair(v):
    k=math.sqrt(2/math.pi)
    v2=v*v
    t=jnp.tanh(k*v*(1+0.044715*v2))
    h=0.5*(1+t)
    return v*h, h+0.5*v*(1-t*t)*(k*(1+3*0.044715*v2))

SAVED=dict(xb=((512,PADC),BF),xhp=((512,PADC),BF),kv=((512,2048),BF),q=((512,D),BF),qn=((512,D),BF),
  xh0=((512,D),BF),p=((512,512),BF),o=((512,D),BF),
  xh1=((512,D),BF),n1=((512,D),BF),a1=((512,D),BF),dg1=((512,D),BF),
  xh2=((512,D),BF),n2=((512,D),BF),qkv=((3,512,D),BF),ph=((8,512,512),BF),so=((512,D),BF),
  xh3=((512,D),BF),n3=((512,D),BF),a2=((512,D),BF),dg2=((512,D),BF),xh4=((512,D),BF),
  rs0=((512,128),F32),rs1=((512,128),F32),rs2=((512,128),F32),rs3=((512,128),F32),rs4=((512,128),F32))
NAMES=list(SAVED)
TENS=[N.lat,N.kvw]+[(N.w+str(i)) for i in range(8)]+[N.head,N.w8,N.w9]
ENTRY,FGAP=3,4
def tshape(n): return {N.lat:(32,512),N.kvw:(64,PADC)}.get(n,(32,1024))

def forward_kernel(comm,*refs):
    refs=list(refs)
    nt=len(TENS)
    square,kvw,hw_own,lat_own,pixels,masks,valids,labels,aux=[refs.pop(0) for _ in range(9)]
    whole=[refs.pop(0) for _ in range(nt)]
    out={n:refs.pop(0) for n in NAMES}
    vec,tail=refs.pop(0),refs.pop(0)
    bufs=[refs.pop(0) for _ in range(nt)]
    s={n:refs.pop(0) for n in NAMES}
    z,h,pix,ssem,rsem,wsem,osem,psend,precv=refs
    me=where_am_i(); nb=neighbours(me)
    zz,yy,xx,cc=(me[i] for i in N.zyxc)
    micro=me[N.h]
    classes=hw_own.shape[1]
    own={n:bufs[TENS.index(n)].at[zz,yy,xx,cc] for n in TENS}
    own[N.lat][...]=lat_own[...].astype(BF)
    own[N.kvw][...]=jnp.zeros((64,PADC),BF)
    own[N.kvw][:,0:CIN]=kvw[...].astype(BF)
    ev=[]
    ready={}
    if comm:
        dp_,h_=me[N.dp],me[N.h]
        diag=(dp_,(h_+1-2*cc)+2-4*xx)
        entry_barrier(me,nb,[diag])
        peers=[nb[N.c],nb[N.x],diag]
        swaps=[pltpu.make_async_remote_copy(src_ref=pixels.at[p[1],0],dst_ref=pix.at[pl.ds(pl.multiple_of(micro*128,128),128)],send_sem=psend.at[i],recv_sem=precv.at[i],device_id=p,device_id_type=MESH) for i,p in enumerate(peers)]
        for k in swaps: k.start()
        keep_own=pltpu.make_async_copy(pixels.at[micro,0],pix.at[pl.ds(pl.multiple_of(micro*128,128),128)],psend.at[3])
        keep_own.start()
        gs=[Gather(me,nb,b,SPLIT[b.shape[-1]],ssem.at[i],rsem.at[i]) for i,b in enumerate(bufs)]
        for tick in range(ENTRY*(nt-1)+6*FGAP+1):
            for t in range(nt):
                p=tick-ENTRY*t
                if p>=0 and p%FGAP==0 and p//FGAP<=6:
                    ev.append(functools.partial(gs[t].phase,p//FGAP))
                    if p//FGAP==6: ready[t]=len(ev)
    else:
        for t in range(nt): ready[t]=0
    pos=[0]
    def pump(k):
        for e in ev[pos[0]:pos[0]+k]: e()
        pos[0]=min(pos[0]+k,len(ev))
    outs=[]
    def weight(name):
        t=TENS.index(name)
        if pos[0]<ready[t]: pump(ready[t]-pos[0])
        if name not in(N.lat,N.head):
            c=pltpu.make_async_copy(bufs[t],whole[t],wsem.at[t]); c.start(); outs.append(c)
        return bufs[t]
    def keep(*names):
        for m in names:
            c=pltpu.make_async_copy(s[m],out[m],osem.at[NAMES.index(m)]); c.start(); outs.append(c)
    gain=lambda i: aux[i:i+1,:]
    pump(2)
    own[N.head][...]=jnp.zeros((32,D),BF)
    own[N.head][:,0:classes]=hw_own[...].astype(BF)
    for i in range(10): own[(N.w+str(i))][...]=square[i].astype(BF)
    for m in (N.xb,N.xhp): s[m][...]=jnp.zeros_like(s[m])
    pump(12)
    if comm:
        keep_own.wait()
        for i,p in enumerate(peers):
            got=pix.at[pl.ds(pl.multiple_of(p[1]*128,128),128)]
            pltpu.make_async_remote_copy(src_ref=got,dst_ref=got,send_sem=psend.at[0],recv_sem=precv.at[i],device_id=p,device_id_type=MESH).wait_recv()
    norm_rows(lambda r: pix[r].astype(F32),aux[5:6,0:CIN],s[N.xhp],None,s[N.xb],width=CIN)
    keep(N.xb,N.xhp)
    lt=weight(N.lat)
    @pl.loop(0,8)
    def _(i):
        z[:,pl.ds(pl.multiple_of(i*128,128),128)]=lt[i//2,i%2].reshape(128,ROWS).T
    pump(3)
    norm_rows(lambda r: z[r].astype(F32),gain(0),s[N.xh0],s[N.rs0],s[N.qn])
    keep(N.qn,N.xh0,N.rs0)
    kt=weight(N.kvw)
    for j in range(4):
        rows=kt[j].reshape(512,PADC)
        s[N.kv][:,j*512:(j+1)*512]=dot(s[N.xb][...],rows,NT).astype(BF)
    keep(N.kv)
    pump(3)
    w=weight(N.w0)
    def epi(cols,acc): s[N.q][:,cols]=acc.astype(BF)
    mm(s[N.qn],w,epi)
    keep(N.q)
    pump(3)
    for i in range(2):
        rows=pl.ds(i*256,256)
        sc=dot(s[N.q][rows],s[N.kv][:,:D],NT)*(1/32)
        sc=jnp.where(masks[micro]>0,sc,-1e30)
        e=jnp.exp(sc-jnp.max(sc,-1,keepdims=True))
        p=(e*(1/jnp.sum(e,-1,keepdims=True))).astype(BF)
        s[N.p][rows]=p
        s[N.o][rows]=dot(p,s[N.kv][:,D:]).astype(BF)
    pump(2)
    keep(N.p,N.o)
    w=weight(N.w1)
    def epi(cols,acc): h[:,cols]=z[:,cols].astype(F32)+acc
    mm(s[N.o],w,epi)
    pump(3)
    norm_rows(lambda r: h[r],gain(1),s[N.xh1],s[N.rs1],s[N.n1])
    keep(N.xh1,N.rs1,N.n1)
    def addh(cols,acc): h[:,cols]=h[:,cols]+acc
    def mlp(wi,wo,nn,dg,act):
        w=weight(wi)
        def epi(cols,acc):
            a,d=gelu_pair(acc)
            s[act][:,cols]=a.astype(BF); s[dg][:,cols]=d.astype(BF)
        mm(s[nn],w,epi)
        keep(dg,act)
        pump(3)
        w=weight(wo)
        mm(s[act],w,addh)
    mlp(N.w2,N.w3,N.n1,N.dg1,N.a1)
    pump(3)
    norm_rows(lambda r: h[r],gain(2),s[N.xh2],s[N.rs2],s[N.n2])
    keep(N.xh2,N.rs2,N.n2)
    for i in range(3):
        w=weight((N.w+str(4+i)))
        def epi(cols,acc,i=i): s[N.qkv][i,:,cols]=acc.astype(BF)
        mm(s[N.n2],w,epi)
        pump(2)
    keep(N.qkv)
    for i in range(8):
        cols=pl.ds(i*128,128)
        sc=dot(s[N.qkv][0,:,cols],s[N.qkv][1,:,cols],NT)*(128**-0.5)
        e=jnp.exp(sc-jnp.max(sc,-1,keepdims=True))
        p=(e*(1/jnp.sum(e,-1,keepdims=True))).astype(BF)
        s[N.ph][i]=p
        s[N.so][:,cols]=dot(p,s[N.qkv][2,:,cols]).astype(BF)
        if i%4==3: pump(2)
    keep(N.ph,N.so)
    w=weight(N.w7)
    mm(s[N.so],w,addh)
    pump(3)
    norm_rows(lambda r: h[r],gain(3),s[N.xh3],s[N.rs3],s[N.n3])
    keep(N.xh3,N.rs3,N.n3)
    mlp(N.w8,N.w9,N.n3,N.dg2,N.a2)
    tot=norm_rows(lambda r: h[r],gain(4),s[N.xh4],s[N.rs4],None,store_sum=True)
    keep(N.xh4,N.rs4)
    pooled=(tot*gain(4)/ROWS).astype(BF)
    hw=weight(N.head)
    lane=lax.broadcasted_iota(jnp.int32,(1,D),1)
    turned=pltpu.roll(aux[...],D-CIN,1)
    bias=jnp.where(lane<D-CIN,turned[5:6],turned[6:7])
    logits=dot(jnp.broadcast_to(pooled,(16,D)),hw[...].reshape(D,D))[0:1]+bias
    logits=jnp.where(lane<classes,logits,-1e30)
    mx=jnp.max(logits,-1,keepdims=True)
    logp=logits-mx-jnp.log(jnp.sum(jnp.exp(logits-mx),-1,keepdims=True))
    target=jnp.where(lane<classes,jnp.where(lane==labels[0,micro],1.0-SMOOTH,0.0)+SMOOTH/classes,0.0)
    valid=jnp.full((1,D),valids[0,micro].astype(F32))
    loss=-valid*jnp.sum(target*logp,-1,keepdims=True)
    dl=valid*(jnp.exp(logp)-target)
    hi=dl.astype(BF); lo=(dl-hi.astype(F32)).astype(BF)
    dp=dot(jnp.concatenate([jnp.broadcast_to(hi,(16,D)),jnp.broadcast_to(lo,(16,D))],0),hw[...].reshape(D,D),NT)
    pf=pooled.astype(F32)
    shown=jnp.where(lane==classes,valid,dl)
    for i in range(4):
        vec[i:i+1]=pf[:,i*256:(i+1)*256]; vec[4+i:5+i]=shown[:,i*256:(i+1)*256]
    tail[0:1]=dp[0:1]+dp[16:17]; tail[1:2]=dl
    tail[2:3]=jnp.where(lane==0,loss,jnp.where(lane==1,valid,0.0))
    tail[3:4]=tot; tail[4:8]=jnp.zeros((4,D),F32)
    pump(len(ev))
    for c in outs: c.wait()
    if comm:
        for k in swaps: k.wait_send()
        for g in gs: g.sends()

def forward_all(square,kvw,head,lat,pixels,masks,valid,labels,aux,cid=0,comm=True):
    nt=len(TENS)
    A=pl.BlockSpec(memory_space=pl.ANY); V=pl.BlockSpec(memory_space=pltpu.VMEM); S=pl.BlockSpec(memory_space=pltpu.SMEM)
    whole=[(4,2,2,2)+tshape(n) for n in TENS]
    outs=[jax.ShapeDtypeStruct(w,BF) for w in whole]
    outs+=[jax.ShapeDtypeStruct(*SAVED[m]) for m in NAMES]+[jax.ShapeDtypeStruct((8,256),F32),jax.ShapeDtypeStruct((8,D),F32)]
    DS=pltpu.SemaphoreType.DMA
    scr=[pltpu.VMEM(w,BF) for w in whole]+[pltpu.VMEM(*SAVED[m]) for m in NAMES]
    scr+=[pltpu.VMEM((512,D),BF),pltpu.VMEM((512,D),F32),pltpu.VMEM((512,CIN),BF),
          DS((nt,25)),DS((nt,25)),DS((nt,)),DS((len(NAMES),)),DS((4,)),DS((3,))]
    cp=dict(has_side_effects=True,vmem_limit_bytes=63*MB)
    if comm: cp.update(collective_id=cid)
    r=pl.pallas_call(functools.partial(forward_kernel,comm),out_shape=outs,
        in_specs=[V]*4+[A,V,S,S,V],out_specs=[A]*(nt+len(NAMES))+[V,V],scratch_shapes=scr,
        compiler_params=pltpu.CompilerParams(**cp))(square,kvw,head,lat,pixels,masks,valid,labels,aux)
    return dict(zip(TENS,r[:nt])),dict(zip(NAMES,r[nt:-2])),r[-2],r[-1]


GRADS=[N.w9,N.w8,N.w7,N.w4,N.w5,N.w6,N.w3,N.w2,N.w1,N.w0,N.kvw,N.lat]
WORDER=[N.w9,N.w8,N.w7,N.w4,N.w5,N.w6,N.w3,N.w2,N.w1,N.w0,N.kvw]
NEEDED=[N.a2,N.dg2,N.n3,N.xh3,N.rs3,N.so,N.ph,N.qkv,N.n2,N.xh2,N.rs2,N.a1,N.dg1,N.n1,N.xh1,N.rs1,N.o,N.p,N.kv,N.q,N.xb,N.xhp,N.qn,N.xh0,N.rs0,N.xh4,N.rs4]
def gshape(n): return {N.lat:(32,512),N.kvw:(64,PADC)}.get(n,(32,D))
RING=4; SRING=2
GAP=3
TICKS=2*11+6*GAP+1


def backward_kernel(comm,classes,*refs):
    refs=list(refs)
    wt={n:refs.pop(0) for n in WORDER}
    sv={n:refs.pop(0) for n in NEEDED}
    vec,tail,aux=[refs.pop(0) for _ in range(3)]
    sq_out=refs.pop(0)
    kv_out,lat_out,vec_out,small_out=[refs.pop(0) for _ in range(4)]
    nt=len(GRADS)
    part=[refs.pop(0) for _ in range(nt)]
    send_ring=[refs.pop(0) for _ in range(SRING)]; send_kv,send_lat=refs.pop(0),refs.pop(0)
    core_ring=[refs.pop(0) for _ in range(RING)]; core_kv,core_lat=refs.pop(0),refs.pop(0)
    rbuf=[{k:refs.pop(0) for k in recv_shapes(*gshape(n)) if k!=N.core} for n in GRADS]
    wslot=[refs.pop(0) for _ in range(2)]; kslot=refs.pop(0)
    aslot=[refs.pop(0) for _ in range(2)]; xslot,rslot=refs.pop(0),refs.pop(0)
    gslot,hslot,qkvslot,xbslot,xhpslot=[refs.pop(0) for _ in range(5)]
    dh,dn,g,dp,dqkv=[refs.pop(0) for _ in range(5)]
    vbuf,srecv,ssend=[refs.pop(0) for _ in range(3)]
    wsem,asem,hsem,ssem,rsem,vs,vr,sms,smr,usem=refs
    me=where_am_i(); nb=neighbours(me)
    z,y,x,c=(me[i] for i in N.zyxc)
    first=c==0
    A=[N.a2,N.n3,N.so,N.n2,N.a1,N.n1,N.o,N.qn]
    X=[N.xh4,N.xh3,N.xh2,N.xh1,N.xh0]; R=[N.rs4,N.rs3,N.rs2,N.rs1,N.rs0]
    place={n:aslot[i%2] for i,n in enumerate(A)}
    place.update({n:xslot for n in X}); place.update({n:rslot for n in R})
    place.update(dg2=gslot,dg1=gslot,p=hslot.at[1],qkv=qkvslot,xb=xbslot,xhp=xhpslot)
    wi=[n for n in WORDER if n!=N.kvw]
    place.update({n:wslot[i%2] for i,n in enumerate(wi)}); place[N.kvw]=kslot
    live={}
    def load(*names):
        for n in names:
            if n in WORDER: cs=[pltpu.make_async_copy(wt[n],place[n],wsem.at[WORDER.index(n)])]
            elif n==N.kv:
                cs=[pltpu.make_async_copy(sv[n].at[:,pl.ds(0,D)],qkvslot.at[1],asem.at[NEEDED.index(n)]),
                    pltpu.make_async_copy(sv[n].at[:,pl.ds(D,D)],qkvslot.at[2],asem.at[len(NEEDED)])]
            elif n==N.q: cs=[pltpu.make_async_copy(sv[n],qkvslot.at[0],asem.at[NEEDED.index(n)])]
            else: cs=[pltpu.make_async_copy(sv[n],place[n],asem.at[NEEDED.index(n)])]
            for k in cs: k.start()
            live[n]=cs
    def use(n):
        for k in live.pop(n): k.wait()
        return place.get(n)
    def load_head(i):
        k=pltpu.make_async_copy(sv[N.ph].at[i],hslot.at[i%2],hsem.at[i]); k.start(); live[(N.ph+str(i))]=[k]
    load(N.xh4,N.rs4,N.w9,N.a2,N.dg2,N.w8,N.n3,N.qkv)
    for i in range(2): load_head(i)
    vbuf[z,y,x,c]=vec[...]
    if comm: entry_barrier(me,nb,small_steps(me)[4:])
    gs=[]
    rings={}
    for t,n in enumerate(GRADS):
        if n==N.kvw: sb,cb=send_kv,core_kv
        elif n==N.lat: sb,cb=send_lat,core_lat
        else:
            k=wi.index(n); sb,cb=send_ring[k%SRING],core_ring[k%RING]
        out={N.kvw:kv_out,N.lat:lat_out}.get(n)
        gs.append(Scatter(me,nb,part[t],sb,dict(rbuf[t],core=cb),out,SPLIT[gshape(n)[1]],ssem.at[t],rsem.at[t]))
    gv=Gather(me,nb,vbuf,[(0,0),(0,0),(0,vbuf.shape[-1])],vs,vr)
    queue={}
    for tick in range(TICKS):
        q=[]
        if tick%4==0 and tick//4<=6: q.append(functools.partial(gv.phase,tick//4))
        for t in range(nt):
            p=tick-2*t
            if p>0 and p%GAP==0 and p//GAP<=6: q.append(functools.partial(gs[t].phase,p//GAP))
        queue[tick]=q
    now=[0]
    def pump(k):
        if not comm: return
        for _ in range(k):
            if queue[now[0]]: queue[now[0]].pop(0)()
    waited=set()
    def before_store(n):
        if n in wi and wi.index(n)>=SRING and comm:
            o=GRADS.index(wi[wi.index(n)-SRING]); gs[o].core(N.send); waited.add(o)
    def half():
        if comm and now[0]%2:
            pump(len(queue[now[0]]))
            now[0]+=1
    def push(n):
        if not comm: return
        half()
        pump(len(queue[now[0]]))
        assert GRADS[now[0]//2]==n
        gs[now[0]//2].phase(0)
        now[0]+=1
    def store(n,v,r0,cols):
        t=GRADS.index(n); r=gshape(n)[0]; k=v.shape[0]//(2*r)
        v=v.astype(BF).reshape(k,2,r,v.shape[1])
        own=jnp.where(first,v[:,0],v[:,1]); other=jnp.where(first,v[:,1],v[:,0])
        b0=r0//(2*r)
        for ref,val in ((part[t],own),(gs[t].half,other)):
            if k==16: ref[:,:,:,:,cols]=val.reshape(4,2,2,r,v.shape[-1])
            elif k>=4: ref[b0//4:(b0+k)//4,:,:,:,cols]=val.reshape(k//4,2,2,r,v.shape[-1])
            else: ref[b0//4,(b0%4)//2,:,:,cols]=val.reshape(2,r,v.shape[-1])
    def weight_grad(n,a,dy):
        before_store(n)
        for j in range(2):
            cols=pl.ds(j*512,512)
            store(n,dot(a[...],dy[:,cols],TN),0,cols)
            pump(2)
        push(n)
    def back(dy,w,epi):
        for j in range(2):
            rows=w[2*j:2*j+2].reshape(512,D)
            epi(pl.ds(j*512,512),dot(dy[...],rows,NT))
            pump(2 if j==0 else 1)
        half()
    gain=lambda i: aux[i:i+1,:]
    def norm_back(load_dn,gn,xh,rs,base,store_to):
        def body(i,tot):
            rows=pl.ds(i*RB,RB)
            d=load_dn(rows); xv=xh[rows].astype(F32)
            dx=d*gn
            m1=jnp.sum(dx,-1,keepdims=True)/D; m2=jnp.sum(dx*xv,-1,keepdims=True)/D
            r=rs[rows][:,0:1]*(dx-m1-xv*m2)
            if base is not None: r=r+base[rows]
            store_to(rows,r)
            return tot+jnp.sum(d*xv,0,keepdims=True)
        tot=jnp.zeros((1,D),F32)
        for i in range(ROWS//RB): tot=body(i,tot)
        return tot
    def to_dh(rows,r):
        dh[rows]=r; g[rows]=r.astype(BF)
    def to_dn(cols,acc): dn[:,cols]=acc
    def to_dp(cols,acc): dp[:,cols]=acc.astype(BF)
    small=ssend.at[0]
    const=tail[0:1]*(1/ROWS)
    use(N.rs4)
    dg=norm_back(lambda r: jnp.broadcast_to(const,(RB,D)),gain(4),use(N.xh4),place[N.rs4],None,to_dh)
    small[4:5]=dg
    small[5:8]=jnp.zeros((3,D),F32)
    lane=lax.broadcasted_iota(jnp.int32,(1,D),1)
    turned=pltpu.roll(tail[...],CIN,1)[1:2]
    small[6:7]=jnp.where(lane<classes-(D-CIN),turned,0.0)
    small[7:8]=tail[2:3]
    load(N.xh3,N.rs3)
    def mlp_back(wo,wi_,act,normed,dgn,xh,rs,row,nxt):
        a=use(act)
        weight_grad(wo,a,g)
        load(*nxt[0])
        w=use(wo); d=use(dgn)
        def epi(cols,acc): dp[:,cols]=(acc*d[:,cols].astype(F32)).astype(BF)
        back(g,w,epi)
        load(*nxt[1])
        weight_grad(wi_,use(normed),dp)
        load(*nxt[2])
        back(dp,use(wi_),to_dn)
        load(*nxt[3])
        use(rs)
        small[row:row+1]=norm_back(lambda r: dn[r],gain(row),use(xh),place[rs],dh,to_dh)
    mlp_back(N.w9,N.w8,N.a2,N.n3,N.dg2,N.xh3,N.rs3,3,([ N.so],[N.w7,N.dg1],[N.n2],[N.w4]))
    load(N.xh2,N.rs2)
    weight_grad(N.w7,use(N.so),g)
    load(N.a1)
    back(g,use(N.w7),to_dp)
    load(N.w5)
    use(N.qkv)
    sc=128**-0.5
    for i in range(8):
        cols=pl.ds(i*128,128)
        use((N.ph+str(i))); ph=hslot.at[i%2]
        qh,kh,vh=(qkvslot[k,:,cols] for k in range(3)); do=dp[:,cols]
        pf=ph[...].astype(F32)
        dpr=dot(do,vh,NT)
        ds=(pf*(dpr-jnp.sum(pf*dpr,-1,keepdims=True)/jnp.sum(pf,-1,keepdims=True))).astype(BF)
        dqkv[0,:,cols]=(dot(ds,kh)*sc).astype(BF)
        dqkv[1,:,cols]=(dot(ds,qh,TN)*sc).astype(BF)
        dqkv[2,:,cols]=dot(ph[...],do,TN).astype(BF)
        if i+2<8: load_head(i+2)
        pump(1)
    load(N.q,N.kv,N.p,N.xb,N.xhp)
    n2=use(N.n2)
    for i in range(3):
        weight_grad((N.w+str(4+i)),n2,dqkv.at[i])
        if i==2: load(N.n1)
        if i==0: back(dqkv.at[0],use(N.w4),to_dn)
        else:
            def add_dn(cols,acc): dn[:,cols]=dn[:,cols]+acc
            back(dqkv.at[i],use((N.w+str(4+i))),add_dn)
        load((N.w6,N.w3,N.w2)[i])
    use(N.rs2)
    small[2:3]=norm_back(lambda r: dn[r],gain(2),use(N.xh2),place[N.rs2],dh,to_dh)
    load(N.xh1,N.rs1)
    mlp_back(N.w3,N.w2,N.a1,N.n1,N.dg1,N.xh1,N.rs1,1,([N.o],[N.w1,N.kvw],[N.qn],[N.w0]))
    load(N.xh0,N.rs0)
    weight_grad(N.w1,use(N.o),g)
    back(g,use(N.w1),to_dp)
    use(N.q); use(N.kv); p=use(N.p)
    q,k,v=(qkvslot.at[i] for i in range(3))
    dpr=dot(dp[...],v[...],NT)
    pf=p[...].astype(F32)
    ds=(pf*(dpr-jnp.sum(pf*dpr,-1,keepdims=True)/jnp.sum(pf,-1,keepdims=True))).astype(BF)
    for j in range(2):
        cols=pl.ds(j*512,512)
        dqkv[0,:,cols]=(dot(ds,k[:,cols])*(1/32)).astype(BF)
        pump(1)
    weight_grad(N.w0,use(N.qn),dqkv.at[0])
    for j in range(2):
        cols=pl.ds(j*512,512)
        dqkv[1,:,cols]=(dot(ds,q[:,cols],TN)*(1/32)).astype(BF)
        dqkv[2,:,cols]=dot(p[...],dp[:,cols],TN).astype(BF)
        pump(1)
    half()
    xb=use(N.xb)
    for i in (0,1):
        store(N.kvw,dot(dqkv[1+i],xb[...],TN),i*D,pl.ds(0,PADC))
        pump(1)
    push(N.kvw)
    back(dqkv.at[0],use(N.w0),to_dn)
    use(N.rs0)
    def to_h(rows,r): dh[rows]=r
    small[0:1]=norm_back(lambda r: dn[r],gain(0),use(N.xh0),place[N.rs0],dh,to_h)
    for i in range(8):
        store(N.lat,dh[:,i*128:(i+1)*128].T,i*128,pl.ds(0,512))
    push(N.lat)
    kw=use(N.kvw); xp=use(N.xhp)
    dx=dot(dqkv[1],kw[0:2].reshape(D,PADC))+dot(dqkv[2],kw[2:4].reshape(D,PADC))
    dpg=jnp.concatenate([jnp.sum(dx*xp[...].astype(F32),0,keepdims=True),jnp.zeros((1,D-PADC),F32)],1)
    small[5:6]=jnp.where(lane<CIN,dpg,turned)
    if comm:
        sm=[pltpu.make_async_remote_copy(src_ref=ssend.at[i],dst_ref=srecv.at[i],send_sem=sms.at[i],recv_sem=smr.at[i],device_id=q_,device_id_type=MESH) for i,q_ in enumerate(small_steps(me))]
        def small_step(i):
            if i>0:
                sm[i-1].wait_recv()
                r=ssend[i-1]+srecv[i-1]
                if i<5: ssend[i]=r
                else: small_out[...]=r
            if i<5: sm[i].start()
        writes=[]
        step=0
        for tick in range(now[0],TICKS):
            if step<=5: small_step(step); step+=1
            for e in queue[tick]: e()
        for t,n in enumerate(GRADS):
            if n[0]==N.w:
                k=pltpu.make_async_copy(part[t].at[z,y,x],sq_out.at[int(n[1])],usem.at[t]); k.start(); writes.append(k)
        while step<=5: small_step(step); step+=1
        for k in writes: k.wait()
        for s_ in sm: s_.wait_send()
        gv.sends()
        for t,s_ in enumerate(gs):
            if t not in waited: s_.core(N.send)
            for r in range(3):
                for ph_ in range(5): s_.do(r,ph_,N.send)
    else:
        small_out[...]=ssend[0]
        kv_out[...]=jnp.zeros_like(kv_out); lat_out[...]=jnp.zeros_like(lat_out)
    vec_out[...]=vbuf[...]

def backward_all(w,sv,vec,tail,aux,classes,cid=1,comm=True):
    A=pl.BlockSpec(memory_space=pl.ANY); V=pl.BlockSpec(memory_space=pltpu.VMEM)
    DS=pltpu.SemaphoreType.DMA
    M=pltpu.VMEM
    nt=len(GRADS)
    outs=[jax.ShapeDtypeStruct((10,32,D),BF)]+[jax.ShapeDtypeStruct((64,PADC),F32),jax.ShapeDtypeStruct((32,512),F32),
          jax.ShapeDtypeStruct((4,2,2,2,8,256),F32),jax.ShapeDtypeStruct((8,D),F32)]
    scr=[M((4,2,2)+gshape(n),BF) for n in GRADS]
    half=lambda n: M((4,2,2)+gshape(n),BF)
    scr+=[half(N.w0)]*SRING+[half(N.kvw),half(N.lat)]+[half(N.w0)]*RING+[half(N.kvw),half(N.lat)]
    for n in GRADS:
        scr+=[M(v,BF) for k,v in recv_shapes(*gshape(n)).items() if k!=N.core]
    scr+=[M((4,2,2,2,32,D),BF)]*2+[M((4,2,2,2,64,PADC),BF)]
    scr+=[M((512,D),BF)]*3+[M((512,128),F32)]
    scr+=[M((512,D),BF),M((2,512,512),BF),M((3,512,D),BF),M((512,PADC),BF),M((512,PADC),BF)]
    scr+=[M((512,D),F32),M((512,D),F32),M((512,D),BF),M((512,D),BF),M((3,512,D),BF)]
    scr+=[M((4,2,2,2,8,256),F32),M((5,8,D),F32),M((5,8,D),F32)]
    scr+=[DS((len(WORDER),)),DS((len(NEEDED)+1,)),DS((8,)),DS((nt,25)),DS((nt,25)),DS((25,)),DS((25,)),DS((5,)),DS((5,)),DS((nt,))]
    cp=dict(has_side_effects=True,vmem_limit_bytes=63*MB+MB//2)
    if comm: cp[N.collective_id]=cid
    return pl.pallas_call(functools.partial(backward_kernel,comm,classes),out_shape=outs,
        in_specs=[A]*(len(WORDER)+len(NEEDED))+[V]*3,out_specs=[A]+[V]*4,scratch_shapes=scr,
        compiler_params=pltpu.CompilerParams(**cp))(*[w[n] for n in WORDER],*[sv[n] for n in NEEDED],vec,tail,aux)


STEP=5

def update_kernel(latent_rate,*refs):
    refs=list(refs)
    grads,kv_g,lat_g,vec,packed=[refs.pop(0) for _ in range(5)]
    old=[[refs.pop(0) for _ in range(3)] for _ in range(4)]
    new=[[refs.pop(0) for _ in range(4)] for _ in range(4)]
    count=jnp.maximum(packed[7:8,1:2],1.0)
    first=(lax.axis_index(N.dp)*lax.axis_size(N.head)+lax.axis_index(N.head))*old[2][0].shape[0]
    def step(total,weight,outs,at,rate):
        w,m,a=(r[at] for r in weight)
        g=total/count
        mom=MOMENTUM*m+g
        wn=w-rate*(g+MOMENTUM*mom)
        for r,v in zip(outs,(g,mom,wn,AVERAGE_DECAY*a+(1.0-AVERAGE_DECAY)*wn)): r[at]=v
    for i in range(STEP): step(grads[i].astype(F32),old[0],new[0],(i,),LEARN_RATE)
    @pl.when(pl.program_id(0)==0)
    def _():
        step(kv_g[:,0:CIN],old[1],new[1],(slice(None),),LEARN_RATE)
        step(lat_g[...],old[3],new[3],(slice(None),),latent_rate)
        rows=old[2][0].shape[0]; classes=old[2][0].shape[1]
        images=vec.shape[0]
        own=jnp.zeros((images,rows),F32)
        for i in range(4):
            pick=lax.broadcasted_iota(jnp.int32,(256,rows),0)+256*i==first+lax.broadcasted_iota(jnp.int32,(256,rows),1)
            own=own+dot(vec[:,i,:].astype(BF),pick.astype(BF))
        own=own.astype(BF)
        for i in range(4):
            n=min(256,classes-256*i)
            dl=vec[:,4+i,:]
            hi=dl.astype(BF); rest=dl-hi.astype(F32); mid=rest.astype(BF); lo=(rest-mid.astype(F32)).astype(BF)
            g=dot(own,hi,TN)+dot(own,mid,TN)+dot(own,lo,TN)
            step(g[:,0:n],old[2],new[2],(slice(None),slice(256*i,256*i+n)),LEARN_RATE)

def update_all(grads,kv_g,lat_g,vec,packed,square,kv,head,lat,latent_rate):
    one=lambda v: pl.BlockSpec(v.shape,lambda i,n=v.ndim: (0,)*n)
    sq=pl.BlockSpec((STEP,)+grads.shape[1:],lambda i: (i,0,0))
    outs=[jax.ShapeDtypeStruct(g[0].shape,F32) for g in (square,kv,head,lat) for _ in range(4)]
    out_specs=[sq]*4+[one(g[0]) for g in (kv,head,lat) for _ in range(4)]
    in_specs=[sq]+[one(v) for v in (kv_g,lat_g,vec,packed)]+[sq]*3+[one(v) for g in (kv,head,lat) for v in g]
    return pl.pallas_call(functools.partial(update_kernel,latent_rate),out_shape=outs,grid=(grads.shape[0]//STEP,),in_specs=in_specs,out_specs=out_specs,
        compiler_params=pltpu.CompilerParams(vmem_limit_bytes=63*MB))(grads,kv_g,lat_g,vec,packed,*square,*kv,*head,*lat)


def per_device_images(
    pixels,
    masks,
    valid,
    labels,
    square,
    kv_weight,
    head_weight,
    latents,
    small,
    square_mom,
    kv_mom,
    head_mom,
    latent_mom,
    small_mom,
    square_avg,
    kv_avg,
    head_avg,
    latent_avg,
    small_avg,
):
    classes = head_weight.shape[1]
    aux = jnp.pad(small, (0, 8 * D - small.shape[0])).reshape(8, D)
    weights, saved, vec, tail = forward_all(
        square, kv_weight.T, head_weight, latents.T, pixels, masks, valid.T, labels.T, aux
    )
    grads, d_kv, d_lat, vec_all, packed = backward_all(weights, saved, vec, tail, aux, classes)
    latent_rate = LATENTS * math.sqrt(D * MICRO * IMG_DEV * lax.axis_size(N.dp)) / 32.0
    new = update_all(
        grads,
        d_kv,
        d_lat,
        vec_all.reshape(-1, 8, 256),
        packed,
        (square, square_mom, square_avg),
        (kv_weight.T, kv_mom.T, kv_avg.T),
        (head_weight, head_mom, head_avg),
        (latents.T, latent_mom.T, latent_avg.T),
        latent_rate,
    )
    loss_sum, count = packed[7, 0], jnp.maximum(packed[7, 1], 1.0)
    small_total = packed.reshape(-1)[: small.shape[0]]
    small_new = nesterov(small, small_total / count, small_mom, small_avg, LEARN_RATE)
    turned = lambda group: [v.T for v in group]
    return (loss_sum, count, *new[:4], *turned(new[4:8]), *new[8:12], *turned(new[12:]), *small_new)


def solution(mesh):
    in_specs = (
        P(None, "dp", "head", None),
        P(None, "dp", None),
        P(None, "dp"),
        P(None, "dp"),
        P(None, ("dp", "head"), None),
        P(None, ("dp", "head")),
        P(("dp", "head"), None),
        P(None, ("dp", "head")),
        P(),
        P(None, ("dp", "head"), None),
        P(None, ("dp", "head")),
        P(("dp", "head"), None),
        P(None, ("dp", "head")),
        P(),
        P(None, ("dp", "head"), None),
        P(None, ("dp", "head")),
        P(("dp", "head"), None),
        P(None, ("dp", "head")),
        P(),
    )
    out_specs = (
        P(),
        P(),
        P(None, ("dp", "head"), None),
        P(None, ("dp", "head"), None),
        P(None, ("dp", "head"), None),
        P(None, ("dp", "head"), None),
        P(None, ("dp", "head")),
        P(None, ("dp", "head")),
        P(None, ("dp", "head")),
        P(None, ("dp", "head")),
        P(("dp", "head"), None),
        P(("dp", "head"), None),
        P(("dp", "head"), None),
        P(("dp", "head"), None),
        P(None, ("dp", "head")),
        P(None, ("dp", "head")),
        P(None, ("dp", "head")),
        P(None, ("dp", "head")),
        P(),
        P(),
        P(),
        P(),
    )
    whole_images = dict(mesh.shape) == {"dp": 8, "head": MICRO}
    per_device = per_device_images if whole_images else per_device_rows
    return jax.shard_map(
        per_device, mesh=mesh, in_specs=in_specs, out_specs=out_specs, check_vma=False
    )
```
